32 devices in a mesh: src: 8 (over y, x, core), rcv: 4 (over z).
Axes of the slice: x: 2, y: 2, z: 4, core: 2. Of those that a mesh axis runs over, the one named last changes fastest.
Arguments:
- src_spec: bfloat16 [2, 16, 256, 512], P(None, None, 'rcv', 'src'), may hold values from -6 to 6
- rcv_spec: bfloat16 [2, 16, 256, 1024], P(None, None, 'src', 'rcv'), may hold values from -6 to 6
- lag_table: int32 [16, 8192], replicated, may hold values from 0 to 511
- src_pos: int32 [512], P('src'), may hold values from 0 to 8191
- rcv_pos: int32 [1024], P('rcv'), may hold values from 0 to 8191
Outputs:
- panel_src: float32 [16, 2, 512, 256], P(None, None, ('src', 'rcv'))
- panel_rcv: float32 [16, 2, 256, 1024], P(None, None, 'src', 'rcv')
The draws below stay inside these ranges and needn't reach their ends.
All inputs are finite; a program needn't handle non-finite values.
Results may differ from the reference program's by a relative error of at most 0.0035.
Values may be sent and summed in bfloat16 or wider, within the bound.
No kernel may reach another device: no remote copies, remote signals or barrier semaphores. Data moves between devices by JAX's collectives and lax.ppermute only.
A program may use at most 64 MiB of HBM per device.

```python
import math
import jax
import jax.numpy as jnp
from jax import lax

F = 256
P_SIZE = 16
WIN = 8
SEGS = 2
NPOS = 8192
NWIN = 16
S = 512
R = 1024


def set_ends(array, own_key, smallest, top_value):
    place = [jax.random.randint(jax.random.fold_in(own_key, axis), (), 0, length) for axis, length in enumerate(array.shape)]
    main_axis = array.shape.index(max(array.shape))
    next_to = place[:main_axis] + [(place[main_axis] + 1) % array.shape[main_axis]] + place[main_axis + 1:]
    return array.at[tuple(place)].set(smallest).at[tuple(next_to)].set(top_value)


def shard_levels(rng, dims, cuts, least, largest):
    loudness, own = 1.0, jax.random.fold_in(rng, 6)
    for position, blocks in cuts:
        steps = jnp.exp(jax.random.uniform(jax.random.fold_in(own, position), (blocks,), jnp.float32, least / len(cuts), largest / len(cuts)))
        loudness = loudness * jnp.repeat(steps, dims[position] // blocks).reshape([-1 if axis == position else 1 for axis in range(len(dims))])
    return loudness


def normal_values(stream_key, extent, scale, reach, cuts=(), kind=jnp.bfloat16):
    values = scale * jax.random.normal(stream_key, extent, jnp.float32)
    if cuts:
        values = values * shard_levels(stream_key, extent, cuts, -0.22, 0.18)
    return jnp.clip(values, -reach, reach).astype(kind)


def setup_inputs(seed: int = 0) -> dict:
    seeds = jax.random.split(jax.random.key(seed), 6)
    return {
        "src_spec": normal_values(seeds[0], (2, NWIN, F, S), 1.0, 6.0, ((2, 4), (3, 8))),
        "rcv_spec": normal_values(seeds[1], (2, NWIN, F, R), 1.0, 6.0, ((2, 8), (3, 4))),
        "lag_table": set_ends(jax.random.randint(seeds[2], (P_SIZE, NPOS), 0, 2 * F), jax.random.fold_in(seeds[2], 1), 0, (2 * F) - 1).astype(jnp.int32),
        "src_pos": set_ends(jax.random.randint(seeds[3], (S,), 0, NPOS), jax.random.fold_in(seeds[3], 1), 0, NPOS - 1).astype(jnp.int32),
        "rcv_pos": set_ends(jax.random.randint(seeds[4], (R,), 0, NPOS), jax.random.fold_in(seeds[4], 1), 0, NPOS - 1).astype(jnp.int32),
    }


def product(left_op, right_op):
    return jnp.dot(left_op.astype(jnp.float32), right_op.astype(jnp.float32), precision=lax.Precision.HIGHEST, preferred_element_type=jnp.float32)

def phase_table(frequency, lags):
    index_mod = frequency * lags % (2 * F)
    angles = index_mod.astype(jnp.float32) * (math.pi / F)
    return (jnp.cos(angles), jnp.sin(angles))

def reference(src_spec, rcv_spec, lag_table, src_pos, rcv_pos):
    lag_src = jnp.take(lag_table, src_pos, axis=1)
    lag_rcv = jnp.take(lag_table, rcv_pos, axis=1)
    count_src = src_spec.shape[3]
    count_rcv = rcv_spec.shape[3]
    src_factor = 1.0 / math.sqrt(count_rcv)
    rcv_factor = 1.0 / math.sqrt(count_src)

    def per_freq(frequency):
        src_block = lax.dynamic_index_in_dim(src_spec, frequency, 2, keepdims=False).astype(jnp.float32)
        rcv_block = lax.dynamic_index_in_dim(rcv_spec, frequency, 2, keepdims=False).astype(jnp.float32)
        total_re = jnp.zeros((count_src, count_rcv), jnp.float32)
        total_im = jnp.zeros((count_src, count_rcv), jnp.float32)
        for segment in range(SEGS):
            src_re = src_block[0, segment * WIN:(segment + 1) * WIN]
            src_im = src_block[1, segment * WIN:(segment + 1) * WIN]
            rcv_re = rcv_block[0, segment * WIN:(segment + 1) * WIN]
            rcv_im = rcv_block[1, segment * WIN:(segment + 1) * WIN]
            real_part = product(src_re.T, rcv_re) + product(src_im.T, rcv_im)
            imag_part = product(src_im.T, rcv_re) - product(src_re.T, rcv_im)
            floor_mod = jnp.maximum(jnp.sqrt(real_part * real_part + imag_part * imag_part), 1.0)
            total_re = total_re + real_part / floor_mod
            total_im = total_im + imag_part / floor_mod
        stacked_re = (total_re / SEGS).astype(jnp.bfloat16)
        stacked_im = (total_im / SEGS).astype(jnp.bfloat16)
        rcv_cos, rcv_sin = phase_table(frequency, lag_rcv)
        src_cos, src_sin = phase_table(frequency, lag_src)
        rcv_cos_b = rcv_cos.astype(jnp.bfloat16)
        rcv_sin_b = rcv_sin.astype(jnp.bfloat16)
        src_cos_b = src_cos.astype(jnp.bfloat16)
        src_sin_b = src_sin.astype(jnp.bfloat16)
        sum_re = product(stacked_re, rcv_cos_b.T) - product(stacked_im, rcv_sin_b.T)
        sum_im = product(stacked_re, rcv_sin_b.T) + product(stacked_im, rcv_cos_b.T)
        panel_re = (sum_re * src_cos.T + sum_im * src_sin.T) * src_factor
        panel_im = (sum_im * src_cos.T - sum_re * src_sin.T) * src_factor
        other_re = product(stacked_re.T, src_cos_b.T) + product(stacked_im.T, src_sin_b.T)
        other_im = product(stacked_im.T, src_cos_b.T) - product(stacked_re.T, src_sin_b.T)
        rcvpan_re = (other_re * rcv_cos.T - other_im * rcv_sin.T) * rcv_factor
        rcvpan_im = (other_re * rcv_sin.T + other_im * rcv_cos.T) * rcv_factor
        return (jnp.stack([panel_re.T, panel_im.T], axis=1), jnp.stack([rcvpan_re.T, rcvpan_im.T], axis=1))
    src_all, rcv_all = lax.map(per_freq, jnp.arange(F, dtype=jnp.int32))
    return (jnp.transpose(src_all, (1, 2, 3, 0)), jnp.transpose(rcv_all, (1, 2, 0, 3)))
```

```python
import math

import jax
import jax.numpy as jnp
from jax import lax
from jax.experimental import pallas as pl
from jax.experimental.pallas import tpu as pltpu
from jax.sharding import PartitionSpec as P

WIN = 8
SEGS = 2


def phase_table(freqs, lags, n_freq):
    index_mod = freqs[:, None, None] * jnp.transpose(lags)[None, :, :] % (2 * n_freq)
    angles = index_mod.astype(jnp.float32) * (math.pi / n_freq)
    return (jnp.cos(angles), jnp.sin(angles))


def cross_block(src_block, rcv_block):
    block_width = src_block.shape[2]
    src_five = src_block.reshape(2, SEGS, WIN, block_width, src_block.shape[3])
    rcv_five = rcv_block.reshape(2, SEGS, WIN, block_width, rcv_block.shape[3])
    swapped = jnp.stack([src_five[1], -src_five[0]])
    real_part = jnp.einsum(
        "cgwfs,cgwfr->gfsr", src_five, rcv_five, preferred_element_type=jnp.float32
    )
    imag_part = jnp.einsum(
        "cgwfs,cgwfr->gfsr", swapped, rcv_five, preferred_element_type=jnp.float32
    )
    floor_mod = jnp.maximum(jnp.sqrt(real_part * real_part + imag_part * imag_part), 1.0)
    stacked_re = (jnp.sum(real_part / floor_mod, axis=0) / SEGS).astype(jnp.bfloat16)
    stacked_im = (jnp.sum(imag_part / floor_mod, axis=0) / SEGS).astype(jnp.bfloat16)
    return (stacked_re, stacked_im)


def source_slant(stacked_re, stacked_im, rcv_cos, rcv_sin, src_cos, src_sin, factor):
    left_op = jnp.concatenate([stacked_re, stacked_im], axis=2)
    cos_b = rcv_cos.astype(jnp.bfloat16)
    sin_b = rcv_sin.astype(jnp.bfloat16)
    upper_half = jnp.concatenate([cos_b, sin_b], axis=2)
    bottom = jnp.concatenate([-sin_b, cos_b], axis=2)
    right_op = jnp.concatenate([upper_half, bottom], axis=1)
    sums = jnp.einsum("fsk,fkq->fsq", left_op, right_op, preferred_element_type=jnp.float32)
    n_slow = rcv_cos.shape[2]
    sum_re = sums[:, :, :n_slow]
    sum_im = sums[:, :, n_slow:]
    panel_re = (sum_re * src_cos + sum_im * src_sin) * factor
    panel_im = (sum_im * src_cos - sum_re * src_sin) * factor
    return jnp.transpose(jnp.stack([panel_re, panel_im]), (3, 0, 2, 1))


def receiver_right(src_cos_b, src_sin_b):
    upper_half = jnp.concatenate([src_cos_b, -src_sin_b], axis=2)
    bottom = jnp.concatenate([src_sin_b, src_cos_b], axis=2)
    return jnp.concatenate([upper_half, bottom], axis=1)


def receiver_sums(left_op, right_op):
    return jnp.einsum("fkr,fkq->fqr", left_op, right_op, preferred_element_type=jnp.float32)


def receiver_outer(sums, rcv_cos, rcv_sin, factor):
    n_slow = rcv_cos.shape[2]
    cos_t = jnp.transpose(rcv_cos, (0, 2, 1))
    sin_t = jnp.transpose(rcv_sin, (0, 2, 1))
    sum_re = sums[:, :n_slow, :]
    sum_im = sums[:, n_slow:, :]
    panel_re = (sum_re * cos_t - sum_im * sin_t) * factor
    panel_im = (sum_re * sin_t + sum_im * cos_t) * factor
    return jnp.transpose(jnp.stack([panel_re, panel_im]), (2, 0, 1, 3))


def per_device_general(src_spec, rcv_spec, lag_table, src_pos, rcv_pos):
    src_full = lax.all_gather(src_spec, "rcv", axis=2, tiled=True)
    n_freq = src_full.shape[2]
    src_dev = src_full.shape[3]
    rcv_dev = rcv_spec.shape[3]
    n_slow = lag_table.shape[0]
    n_src = lax.axis_size("src")
    n_rcv = lax.axis_size("rcv")
    src_factor = 1.0 / math.sqrt(rcv_dev * n_rcv)
    rcv_factor = 1.0 / math.sqrt(src_dev * n_src)
    lag_src = jnp.take(lag_table, src_pos, axis=1)
    lag_rcv = jnp.take(lag_table, rcv_pos, axis=1)
    src_init = jnp.zeros((n_slow, 2, src_dev, n_freq), jnp.float32)
    other_init = jnp.zeros((n_slow, 2, n_freq, rcv_dev), jnp.float32)
    shard_piece = lax.all_gather(rcv_spec, "src", axis=2, tiled=True)
    block_width = math.gcd(shard_piece.shape[2], 16)

    def inner(turn_index, totals):
        offset = turn_index * block_width
        freqs = offset + jnp.arange(block_width, dtype=jnp.int32)
        src_block = lax.dynamic_slice_in_dim(src_full, offset, block_width, 2)
        rcv_block = lax.dynamic_slice_in_dim(shard_piece, offset, block_width, 2)
        stacked_re, stacked_im = cross_block(src_block, rcv_block)
        rcv_cos, rcv_sin = phase_table(freqs, lag_rcv, n_freq)
        src_cos, src_sin = phase_table(freqs, lag_src, n_freq)
        src_part = source_slant(
            stacked_re, stacked_im, rcv_cos, rcv_sin, src_cos, src_sin, src_factor
        )
        src_total = lax.dynamic_update_slice_in_dim(totals[0], src_part, offset, 3)
        left_op = jnp.concatenate([stacked_re, stacked_im], axis=1)
        right_op = receiver_right(src_cos.astype(jnp.bfloat16), src_sin.astype(jnp.bfloat16))
        rcv_part = receiver_outer(receiver_sums(left_op, right_op), rcv_cos, rcv_sin, rcv_factor)
        other = lax.dynamic_update_slice_in_dim(totals[1], rcv_part, offset, 2)
        return (src_total, other)

    src_total, other = lax.fori_loop(
        0, shard_piece.shape[2] // block_width, inner, (src_init, other_init)
    )
    panel_src = lax.psum_scatter(src_total, "rcv", scatter_dimension=2, tiled=True)
    panel_rcv = lax.psum_scatter(other, "src", scatter_dimension=2, tiled=True)
    return (panel_src, panel_rcv)


LANES = 128
HALVES = 2
ROWS = 32
LAG_ROWS = 16
VMEM = 56 * 2**20
F32 = jnp.float32
BF16 = jnp.bfloat16
SIN = [(-1) ** n * (math.pi / 2) ** (2 * n + 1) / math.factorial(2 * n + 1) for n in range(5)]
COS = [(-1) ** n * (math.pi / 2) ** (2 * n) / math.factorial(2 * n) for n in range(6)]


def horner(coefs, v):
    total = coefs[-1]
    for coef in coefs[-2::-1]:
        total = coef + v * total
    return total


def phases(lag, freq, period):
    turns = lag * freq * (1.0 / period)
    quarters = 4.0 * (turns - jnp.floor(turns))
    near = jnp.floor(quarters + 0.5)
    u = quarters - near
    v = u * u
    s = u * horner(SIN, v)
    c = horner(COS, v)
    odd = (near == 1.0) | (near == 3.0)
    cos = jnp.where(odd, s, c)
    sin = jnp.where(odd, c, s)
    cos = jnp.where((near == 1.0) | (near == 2.0), -cos, cos)
    sin = jnp.where((near == 2.0) | (near == 3.0), -sin, sin)
    return cos, sin


def lanes_of(rows):
    return lax.broadcasted_iota(jnp.int32, (rows, LANES), 1)


class Sizes:
    def __init__(self, shapes, n_src, n_rcv):
        src_spec, rcv_spec, lag_table = shapes
        self.n_src, self.n_rcv, self.n_dev = n_src, n_rcv, n_src * n_rcv
        self.n_slow, self.n_pos = lag_table
        self.n_win = src_spec[1]
        self.src_freq, self.src_dev = src_spec[2:]
        self.rcv_freq, self.rcv_dev = rcv_spec[2:]
        self.n_freq = self.rcv_freq * n_src
        self.own = self.n_freq // self.n_dev
        self.s_all, self.r_all = self.src_dev * n_src, self.rcv_dev * n_rcv
        self.r_half = self.r_all // HALVES
        self.src_part, self.rcv_part = self.src_dev // n_rcv, self.rcv_dev // n_src

    def fits(self):
        return (
            2 * self.n_win == ROWS
            and 2 * self.n_slow == ROWS
            and self.n_win == WIN * SEGS
            and self.own == self.n_src
            and self.rcv_freq == self.n_dev
            and self.src_freq == 2 * self.n_dev
            and 2 * self.src_dev == LANES
            and self.rcv_dev == HALVES * LANES
            and self.src_part * self.own == LANES
            and self.rcv_part * self.n_src == HALVES * LANES
            and LANES % self.rcv_part == 0
            and self.n_pos % LANES == 0
            and self.own * self.n_dev == HALVES * LANES
        )


def pack_first(z):
    def kernel(me_ref, src_pos_ref, rcv_pos_ref, src_ref, rcv_ref, lag_ref, out_ref, flat_src, flat_rcv):
        lane = lanes_of(LAG_ROWS)
        acc = jnp.zeros((LAG_ROWS, LANES), jnp.int32)
        for n in range(z.src_part + z.rcv_part):
            if n < z.src_part:
                pos = src_pos_ref[me_ref[1] * z.src_part + n]
            else:
                pos = rcv_pos_ref[me_ref[0] * z.rcv_part + n - z.src_part]
            base = pl.multiple_of((pos // LANES) * LANES, LANES)
            tile = lag_ref[:, pl.ds(base, LANES)]
            acc = jnp.where(lane == n, pltpu.roll(tile, (n - pos) & (LANES - 1), 1), acc)
        lags = (acc - z.n_freq).astype(F32).astype(BF16)
        count = z.n_dev
        for row in range(ROWS):
            both = src_ref[row].astype(F32)
            flat_src[row * count:(row + 1) * count, :] = jnp.concatenate([both[:count], both[count:]], 1)
            flat_rcv[row * count:(row + 1) * count, :] = rcv_ref[row].astype(F32)
        for dev in range(count):
            out_ref[dev, :ROWS, :] = flat_src[pl.ds(dev, ROWS, stride=count), :].astype(BF16)
            out_ref[dev, ROWS:2 * ROWS, :] = flat_rcv[pl.ds(dev, ROWS, stride=count), :].astype(BF16)
            out_ref[dev, 2 * ROWS:, :] = lags

    rows = 2 * ROWS + LAG_ROWS
    flat = pltpu.VMEM((ROWS * z.n_dev, LANES), F32)
    return pl.pallas_call(
        kernel,
        grid=(1,),
        in_specs=[pl.BlockSpec(memory_space=pltpu.SMEM)] * 3
        + [
            pl.BlockSpec((ROWS, z.src_freq, z.src_dev), lambda n: (0, 0, 0)),
            pl.BlockSpec((ROWS, z.rcv_freq, LANES), lambda n: (0, 0, 0)),
            pl.BlockSpec((z.n_slow, z.n_pos), lambda n: (0, 0)),
        ],
        out_specs=pl.BlockSpec((z.n_dev, rows, LANES), lambda n: (0, 0, 0)),
        out_shape=jax.ShapeDtypeStruct((z.n_dev, rows, LANES), BF16),
        scratch_shapes=[flat, flat],
        compiler_params=pltpu.CompilerParams(vmem_limit_bytes=VMEM),
        cost_estimate=pl.CostEstimate(flops=10**6, bytes_accessed=2 * 10**6, transcendentals=0),
        name="pack_first",
    )


def pack_second(z):
    def kernel(rcv_ref, out_ref, flat):
        count = z.n_dev
        for row in range(ROWS):
            flat[row * count:(row + 1) * count, :] = rcv_ref[row].astype(F32)
        for dev in range(count):
            out_ref[dev] = flat[pl.ds(dev, ROWS, stride=count), :].astype(BF16)

    return pl.pallas_call(
        kernel,
        grid=(1,),
        in_specs=[pl.BlockSpec((ROWS, z.rcv_freq, LANES), lambda n: (0, 0, 1))],
        out_specs=pl.BlockSpec((z.n_dev, ROWS, LANES), lambda n: (0, 0, 0)),
        out_shape=jax.ShapeDtypeStruct((z.n_dev, ROWS, LANES), BF16),
        scratch_shapes=[pltpu.VMEM((ROWS * z.n_dev, LANES), F32)],
        compiler_params=pltpu.CompilerParams(vmem_limit_bytes=VMEM),
        cost_estimate=pl.CostEstimate(flops=10**6, bytes_accessed=10**6, transcendentals=0),
        name="pack_second",
    )


def gather_lags(z, first_ref, half, src_lag, rcv_lag):
    lane = lanes_of(LAG_ROWS)

    def spread(pieces):
        total = jnp.zeros((LAG_ROWS, LANES), F32)
        for sender, begin, place, width in pieces:
            tile = first_ref[sender, 2 * ROWS:, :].astype(F32) + float(z.n_freq)
            shift = (place - begin) % LANES
            moved = pltpu.roll(tile, shift, 1) if shift else tile
            total = jnp.where((lane >= place) & (lane < place + width), moved, total)
        return total

    for block in range(z.s_all // LANES):
        pieces = [
            ((2 * block + odd) * z.n_rcv + rcv, 0, odd * z.src_dev + rcv * z.src_part, z.src_part)
            for odd in range(2)
            for rcv in range(z.n_rcv)
        ]
        src_lag[:, block * LANES:(block + 1) * LANES] = spread(pieces)
    per_half = z.n_src // HALVES
    for rcv in range(z.n_rcv):
        pieces = [
            ((half * per_half + n) * z.n_rcv + rcv, z.src_part, n * z.rcv_part, z.rcv_part)
            for n in range(per_half)
        ]
        rcv_lag[:, rcv * LANES:(rcv + 1) * LANES] = spread(pieces)


def cross_spectra(z, first_ref, rcv_ref, rcv_row, turn, left, right, stack):
    pair, odd = turn // 2, turn % 2
    lane = lanes_of(ROWS)
    blocks = []
    for block in range(z.s_all // LANES):
        one = first_ref[(2 * block) * z.n_rcv + pair, :ROWS, :].astype(F32)
        two = first_ref[(2 * block + 1) * z.n_rcv + pair, :ROWS, :].astype(F32)
        one = jnp.where(odd == 0, one, pltpu.roll(one, z.src_dev, 1))
        two = jnp.where(odd == 0, pltpu.roll(two, z.src_dev, 1), two)
        blocks.append(jnp.where(lane < z.src_dev, one, two))
    left[...] = jnp.transpose(jnp.concatenate(blocks, 1)).astype(BF16)
    pieces = [rcv_ref[turn * z.n_rcv + rcv, rcv_row:rcv_row + ROWS, :] for rcv in range(z.n_rcv)]
    spec = jnp.concatenate(pieces, 1).astype(F32)
    turned = jnp.concatenate([-spec[z.n_win:], spec[:z.n_win]], 0)
    window = lax.broadcasted_iota(jnp.int32, (ROWS, 1), 0) % z.n_win
    for seg in range(SEGS):
        here = window // WIN == seg
        right[seg] = jnp.where(here, spec, 0.0).astype(BF16)
        right[SEGS + seg] = jnp.where(here, turned, 0.0).astype(BF16)
    width, height = 2 * LANES, TILE_ROWS
    for col in range(0, z.r_half, width):
        for row in range(0, z.s_all, height):
            part = left[row:row + height, :]
            total_re, total_im = 0.0, 0.0
            for seg in range(SEGS):
                real = jnp.dot(part, right[seg, :, col:col + width], preferred_element_type=F32)
                imag = jnp.dot(part, right[SEGS + seg, :, col:col + width], preferred_element_type=F32)
                scale = lax.rsqrt(jnp.maximum(real * real + imag * imag, 1.0))
                total_re, total_im = total_re + real * scale, total_im + imag * scale
            stack[row:row + height, col:col + width] = total_re.astype(BF16)
            stack[z.s_all + row:z.s_all + row + height, col:col + width] = total_im.astype(BF16)


TILE_ROWS = 32


def compute(z, half):
    last = half == HALVES - 1
    src_factor = 1.0 / (SEGS * math.sqrt(z.r_all))
    rcv_factor = 1.0 / (SEGS * math.sqrt(z.s_all))
    n = z.n_slow

    def kernel(me_ref, first_ref, *refs):
        if last:
            second_ref, before_ref, out_ref, src_lag, rcv_lag, left, right, stack, sums = refs
            rcv_ref, rcv_row = second_ref, 0
        else:
            out_ref, part_ref, src_lag, rcv_lag, left, right, stack = refs
            rcv_ref, rcv_row = first_ref, ROWS
        turn = pl.program_id(0)

        @pl.when(turn == 0)
        def _():
            gather_lags(z, first_ref, half, src_lag, rcv_lag)

        cross_spectra(z, first_ref, rcv_ref, rcv_row, turn, left, right, stack)
        freq = (turn * z.n_dev + me_ref[0] * z.n_rcv + me_ref[1]).astype(F32)
        src_cos, src_sin = phases(src_lag[...], freq, 2.0 * z.n_freq)
        rcv_cos, rcv_sin = phases(rcv_lag[...], freq, 2.0 * z.n_freq)
        upper = jnp.concatenate([src_cos, src_sin], 1)
        lower = jnp.concatenate([-src_sin, src_cos], 1)
        both = jnp.concatenate([upper, lower], 0).astype(BF16)
        over_src = jnp.dot(both, stack[...], preferred_element_type=F32) * rcv_factor
        over_re, over_im = over_src[:n], over_src[n:]
        panel = jnp.concatenate([over_re * rcv_cos - over_im * rcv_sin, over_re * rcv_sin + over_im * rcv_cos], 0)
        for rcv in range(z.n_rcv):
            out_ref[turn * z.n_rcv + rcv, :ROWS, :] = panel[:, rcv * LANES:(rcv + 1) * LANES].astype(BF16)
        dims = (((1,), (1,)), ((), ()))
        with_re = jnp.concatenate([rcv_cos, rcv_sin], 0).astype(BF16)
        with_im = jnp.concatenate([-rcv_sin, rcv_cos], 0).astype(BF16)
        over_rcv = lax.dot_general(with_re, stack[:z.s_all, :], dims, preferred_element_type=F32)
        over_rcv += lax.dot_general(with_im, stack[z.s_all:, :], dims, preferred_element_type=F32)
        if not last:
            part_ref[0] = over_rcv
            return
        over_rcv = (over_rcv + before_ref[0]) * src_factor
        over_re, over_im = over_rcv[:n], over_rcv[n:]
        panel = jnp.concatenate([over_re * src_cos + over_im * src_sin, over_im * src_cos - over_re * src_sin], 0)
        sums[turn] = panel

        @pl.when(turn == z.own - 1)
        def _():
            lane = lanes_of(ROWS)
            width = z.src_part
            for dev in range(z.n_dev):
                block, place = divmod(dev * width, LANES)
                total = jnp.zeros((ROWS, LANES), F32)
                for k in range(z.own):
                    tile = sums[k, :, block * LANES:(block + 1) * LANES]
                    shift = (k * width - place) % LANES
                    moved = pltpu.roll(tile, shift, 1) if shift else tile
                    total = jnp.where((lane >= k * width) & (lane < (k + 1) * width), moved, total)
                out_ref[dev, ROWS:, :] = total.astype(BF16)

    whole = lambda *shape: pl.BlockSpec(shape, lambda k: (0,) * len(shape))
    part_spec = pl.BlockSpec((1, ROWS, z.s_all), lambda k: (k, 0, 0))
    part_shape = jax.ShapeDtypeStruct((z.own, ROWS, z.s_all), F32)
    in_specs = [pl.BlockSpec(memory_space=pltpu.SMEM), whole(z.n_dev, 2 * ROWS + LAG_ROWS, LANES)]
    out_rows = ROWS * (2 if last else 1)
    out_specs = [whole(z.n_dev, out_rows, LANES)]
    out_shape = [jax.ShapeDtypeStruct((z.n_dev, out_rows, LANES), BF16)]
    scratch = [
        pltpu.VMEM((n, z.s_all), F32),
        pltpu.VMEM((n, z.r_half), F32),
        pltpu.VMEM((z.s_all, ROWS), BF16),
        pltpu.VMEM((2 * SEGS, ROWS, z.r_half), BF16),
        pltpu.VMEM((2 * z.s_all, z.r_half), BF16),
    ]
    if last:
        in_specs += [whole(z.n_dev, ROWS, LANES), part_spec]
        scratch.append(pltpu.VMEM((z.own, ROWS, z.s_all), F32))
    else:
        out_specs.append(part_spec)
        out_shape.append(part_shape)
    return pl.pallas_call(
        kernel,
        grid=(z.own,),
        in_specs=in_specs,
        out_specs=out_specs,
        out_shape=out_shape,
        scratch_shapes=scratch,
        compiler_params=pltpu.CompilerParams(vmem_limit_bytes=VMEM),
        cost_estimate=pl.CostEstimate(flops=8 * 10**9, bytes_accessed=2 * 10**6, transcendentals=4 * 10**6),
        name="compute_last" if last else "compute_first",
    )


def unpack_receivers(z, in_ref, flat, out_ref):
    n = z.n_slow
    for dev in range(z.n_dev):
        flat[dev * ROWS:(dev + 1) * ROWS, :] = in_ref[dev, :ROWS, :].astype(F32)
    for slow in range(n):
        for part in range(2):
            out_ref[2 * slow + part] = flat[pl.ds(part * n + slow, z.n_dev, stride=ROWS), :]


def unpack_first(z):
    def kernel(in_ref, out_ref, flat):
        unpack_receivers(z, in_ref, flat, out_ref)

    return pl.pallas_call(
        kernel,
        grid=(1,),
        in_specs=[pl.BlockSpec((z.n_dev, ROWS, LANES), lambda k: (0, 0, 0))],
        out_specs=pl.BlockSpec((ROWS, z.rcv_freq, LANES), lambda k: (0, 0, 0)),
        out_shape=jax.ShapeDtypeStruct((ROWS, z.rcv_freq, z.rcv_dev), F32),
        scratch_shapes=[pltpu.VMEM((z.n_dev * ROWS, LANES), F32)],
        compiler_params=pltpu.CompilerParams(vmem_limit_bytes=VMEM),
        cost_estimate=pl.CostEstimate(flops=10**6, bytes_accessed=10**6, transcendentals=0),
        name="unpack_first",
    )


def unpack_last(z):
    n = z.n_slow
    group = LANES // z.n_dev
    width = z.src_part

    def kernel(in_ref, held_ref, rcv_ref, src_ref, flat):
        del held_ref
        unpack_receivers(z, in_ref, flat, rcv_ref)
        for dev in range(z.n_dev):
            flat[dev * ROWS:(dev + 1) * ROWS, :] = in_ref[dev, ROWS:, :].astype(F32)
        lane = lanes_of(width)
        for first in range(0, ROWS, group):
            tiles = [flat[pl.ds(first + j, z.n_dev, stride=ROWS), :] for j in range(group)]
            turned = jnp.transpose(jnp.concatenate(tiles, 0))
            for j in range(group):
                part, slow = divmod(first + j, n)
                for block in range(z.own // group):
                    total = jnp.zeros((width, LANES), F32)
                    for k in range(group):
                        row = (block * group + k) * width
                        tile = turned[row:row + width, :]
                        shift = (k - j) * z.n_dev % LANES
                        moved = pltpu.roll(tile, shift, 1) if shift else tile
                        total = jnp.where((lane >= k * z.n_dev) & (lane < (k + 1) * z.n_dev), moved, total)
                    src_ref[2 * slow + part, :, block * LANES:(block + 1) * LANES] = total

    return pl.pallas_call(
        kernel,
        grid=(1,),
        in_specs=[pl.BlockSpec((z.n_dev, 2 * ROWS, LANES), lambda k: (0, 0, 0)), pl.BlockSpec(memory_space=pl.ANY)],
        out_specs=[
            pl.BlockSpec((ROWS, z.rcv_freq, LANES), lambda k: (0, 0, 1)),
            pl.BlockSpec((ROWS, width, z.n_freq), lambda k: (0, 0, 0)),
        ],
        out_shape=[
            jax.ShapeDtypeStruct((ROWS, z.rcv_freq, z.rcv_dev), F32),
            jax.ShapeDtypeStruct((ROWS, width, z.n_freq), F32),
        ],
        input_output_aliases={1: 0},
        scratch_shapes=[pltpu.VMEM((z.n_dev * ROWS, LANES), F32)],
        compiler_params=pltpu.CompilerParams(vmem_limit_bytes=VMEM),
        cost_estimate=pl.CostEstimate(flops=10**6, bytes_accessed=2 * 10**6, transcendentals=0),
        name="unpack_last",
    )


def exchange(payload):
    return lax.all_to_all(payload, ("src", "rcv"), 0, 0, tiled=True)


def per_device(src_spec, rcv_spec, lag_table, src_pos, rcv_pos):
    n_src, n_rcv = lax.axis_size("src"), lax.axis_size("rcv")
    z = Sizes((src_spec.shape, rcv_spec.shape, lag_table.shape), n_src, n_rcv)
    if not z.fits():
        return per_device_general(src_spec, rcv_spec, lag_table, src_pos, rcv_pos)
    me = jnp.stack([lax.axis_index("src"), lax.axis_index("rcv")]).astype(jnp.int32)
    src_rows = src_spec.reshape(ROWS, z.src_freq, z.src_dev)
    rcv_rows = rcv_spec.reshape(ROWS, z.rcv_freq, z.rcv_dev)
    first = exchange(pack_first(z)(me, src_pos, rcv_pos, src_rows, rcv_rows, lag_table))
    second = exchange(pack_second(z)(rcv_rows))
    out_first, before = compute(z, 0)(me, first)
    got_first = exchange(out_first)
    (out_last,) = compute(z, 1)(me, first, second, before)
    got_last = exchange(out_last)
    held = unpack_first(z)(got_first)
    panel_rcv, panel_src = unpack_last(z)(got_last, held)
    return (
        panel_src.reshape(z.n_slow, 2, z.src_part, z.n_freq),
        panel_rcv.reshape(z.n_slow, 2, z.rcv_freq, z.rcv_dev),
    )


def solution(mesh):
    placed = (P(None, None, "rcv", "src"), P(None, None, "src", "rcv"), P(), P("src"), P("rcv"))
    return jax.shard_map(
        per_device,
        mesh=mesh,
        in_specs=placed,
        out_specs=(P(None, None, ("src", "rcv"), None), P(None, None, "src", "rcv")),
        check_vma=False,
    )
```

```python
import math

import jax
import jax.numpy as jnp
from jax import lax
from jax.experimental import pallas as pl
from jax.experimental.pallas import tpu as pltpu
from jax.sharding import PartitionSpec as P

WIN = 8
SEGS = 2


def phase_table(freqs, lags, n_freq):
    index_mod = freqs[:, None, None] * jnp.transpose(lags)[None, :, :] % (2 * n_freq)
    angles = index_mod.astype(jnp.float32) * (math.pi / n_freq)
    return (jnp.cos(angles), jnp.sin(angles))


def cross_block(src_block, rcv_block):
    block_width = src_block.shape[2]
    src_five = src_block.reshape(2, SEGS, WIN, block_width, src_block.shape[3])
    rcv_five = rcv_block.reshape(2, SEGS, WIN, block_width, rcv_block.shape[3])
    swapped = jnp.stack([src_five[1], -src_five[0]])
    real_part = jnp.einsum(
        "cgwfs,cgwfr->gfsr", src_five, rcv_five, preferred_element_type=jnp.float32
    )
    imag_part = jnp.einsum(
        "cgwfs,cgwfr->gfsr", swapped, rcv_five, preferred_element_type=jnp.float32
    )
    floor_mod = jnp.maximum(jnp.sqrt(real_part * real_part + imag_part * imag_part), 1.0)
    stacked_re = (jnp.sum(real_part / floor_mod, axis=0) / SEGS).astype(jnp.bfloat16)
    stacked_im = (jnp.sum(imag_part / floor_mod, axis=0) / SEGS).astype(jnp.bfloat16)
    return (stacked_re, stacked_im)


def source_slant(stacked_re, stacked_im, rcv_cos, rcv_sin, src_cos, src_sin, factor):
    left_op = jnp.concatenate([stacked_re, stacked_im], axis=2)
    cos_b = rcv_cos.astype(jnp.bfloat16)
    sin_b = rcv_sin.astype(jnp.bfloat16)
    upper_half = jnp.concatenate([cos_b, sin_b], axis=2)
    bottom = jnp.concatenate([-sin_b, cos_b], axis=2)
    right_op = jnp.concatenate([upper_half, bottom], axis=1)
    sums = jnp.einsum("fsk,fkq->fsq", left_op, right_op, preferred_element_type=jnp.float32)
    n_slow = rcv_cos.shape[2]
    sum_re = sums[:, :, :n_slow]
    sum_im = sums[:, :, n_slow:]
    panel_re = (sum_re * src_cos + sum_im * src_sin) * factor
    panel_im = (sum_im * src_cos - sum_re * src_sin) * factor
    return jnp.transpose(jnp.stack([panel_re, panel_im]), (3, 0, 2, 1))


def receiver_right(src_cos_b, src_sin_b):
    upper_half = jnp.concatenate([src_cos_b, -src_sin_b], axis=2)
    bottom = jnp.concatenate([src_sin_b, src_cos_b], axis=2)
    return jnp.concatenate([upper_half, bottom], axis=1)


def receiver_sums(left_op, right_op):
    return jnp.einsum("fkr,fkq->fqr", left_op, right_op, preferred_element_type=jnp.float32)


def receiver_outer(sums, rcv_cos, rcv_sin, factor):
    n_slow = rcv_cos.shape[2]
    cos_t = jnp.transpose(rcv_cos, (0, 2, 1))
    sin_t = jnp.transpose(rcv_sin, (0, 2, 1))
    sum_re = sums[:, :n_slow, :]
    sum_im = sums[:, n_slow:, :]
    panel_re = (sum_re * cos_t - sum_im * sin_t) * factor
    panel_im = (sum_re * sin_t + sum_im * cos_t) * factor
    return jnp.transpose(jnp.stack([panel_re, panel_im]), (2, 0, 1, 3))


def per_device_general(src_spec, rcv_spec, lag_table, src_pos, rcv_pos):
    src_full = lax.all_gather(src_spec, "rcv", axis=2, tiled=True)
    n_freq = src_full.shape[2]
    src_dev = src_full.shape[3]
    rcv_dev = rcv_spec.shape[3]
    n_slow = lag_table.shape[0]
    n_src = lax.axis_size("src")
    n_rcv = lax.axis_size("rcv")
    src_factor = 1.0 / math.sqrt(rcv_dev * n_rcv)
    rcv_factor = 1.0 / math.sqrt(src_dev * n_src)
    lag_src = jnp.take(lag_table, src_pos, axis=1)
    lag_rcv = jnp.take(lag_table, rcv_pos, axis=1)
    src_init = jnp.zeros((n_slow, 2, src_dev, n_freq), jnp.float32)
    other_init = jnp.zeros((n_slow, 2, n_freq, rcv_dev), jnp.float32)
    shard_piece = lax.all_gather(rcv_spec, "src", axis=2, tiled=True)
    block_width = math.gcd(shard_piece.shape[2], 16)

    def inner(turn_index, totals):
        offset = turn_index * block_width
        freqs = offset + jnp.arange(block_width, dtype=jnp.int32)
        src_block = lax.dynamic_slice_in_dim(src_full, offset, block_width, 2)
        rcv_block = lax.dynamic_slice_in_dim(shard_piece, offset, block_width, 2)
        stacked_re, stacked_im = cross_block(src_block, rcv_block)
        rcv_cos, rcv_sin = phase_table(freqs, lag_rcv, n_freq)
        src_cos, src_sin = phase_table(freqs, lag_src, n_freq)
        src_part = source_slant(
            stacked_re, stacked_im, rcv_cos, rcv_sin, src_cos, src_sin, src_factor
        )
        src_total = lax.dynamic_update_slice_in_dim(totals[0], src_part, offset, 3)
        left_op = jnp.concatenate([stacked_re, stacked_im], axis=1)
        right_op = receiver_right(src_cos.astype(jnp.bfloat16), src_sin.astype(jnp.bfloat16))
        rcv_part = receiver_outer(receiver_sums(left_op, right_op), rcv_cos, rcv_sin, rcv_factor)
        other = lax.dynamic_update_slice_in_dim(totals[1], rcv_part, offset, 2)
        return (src_total, other)

    src_total, other = lax.fori_loop(
        0, shard_piece.shape[2] // block_width, inner, (src_init, other_init)
    )
    panel_src = lax.psum_scatter(src_total, "rcv", scatter_dimension=2, tiled=True)
    panel_rcv = lax.psum_scatter(other, "src", scatter_dimension=2, tiled=True)
    return (panel_src, panel_rcv)


LANES = 128
ROWS = 32
LAG_ROWS = 16
CALLS = ((0,), (3, 2), (1,))
VMEM = 20 * 2**20
FULL_VMEM = 56 * 2**20
TILE_ROWS = 64
COST = 10**6
F32 = jnp.float32
BF16 = jnp.bfloat16
SIN = [(-1) ** n * (math.pi / 2) ** (2 * n + 1) / math.factorial(2 * n + 1) for n in range(5)]
COS = [(-1) ** n * (math.pi / 2) ** (2 * n) / math.factorial(2 * n) for n in range(6)]


def horner(coefs, v):
    total = coefs[-1]
    for coef in coefs[-2::-1]:
        total = coef + v * total
    return total


def phases(lag, freq, period):
    turns = lag * freq * (1.0 / period)
    quarters = 4.0 * (turns - jnp.floor(turns))
    near = jnp.floor(quarters + 0.5)
    u = quarters - near
    v = u * u
    s = u * horner(SIN, v)
    c = horner(COS, v)
    odd = (near == 1.0) | (near == 3.0)
    cos = jnp.where(odd, s, c)
    sin = jnp.where(odd, c, s)
    cos = jnp.where((near == 1.0) | (near == 2.0), -cos, cos)
    sin = jnp.where((near == 2.0) | (near == 3.0), -sin, sin)
    return cos, sin


def lanes_of(rows):
    return lax.broadcasted_iota(jnp.int32, (rows, LANES), 1)


class Sizes:
    def __init__(self, shapes, n_src, n_rcv):
        src_spec, rcv_spec, lag_table = shapes
        self.n_src, self.n_rcv, self.n_dev = n_src, n_rcv, n_src * n_rcv
        self.n_slow, self.n_pos = lag_table
        self.n_win = src_spec[1]
        self.src_freq, self.src_dev = src_spec[2:]
        self.rcv_freq, self.rcv_dev = rcv_spec[2:]
        self.n_freq = self.rcv_freq * n_src
        self.own = self.n_freq // self.n_dev
        self.s_all, self.r_all = self.src_dev * n_src, self.rcv_dev * n_rcv
        self.src_part = self.src_dev // n_rcv
        self.low = n_src // n_rcv
        self.chunk = self.own // 2 * ROWS

    def fits(self):
        return (
            2 * self.n_win == ROWS
            and 2 * self.n_slow == ROWS
            and self.n_win == WIN * SEGS
            and self.n_rcv == 4
            and self.own == 8
            and self.src_freq == self.low * self.n_rcv * self.own
            and self.rcv_freq == self.n_rcv * self.own
            and self.n_dev * self.own == self.n_freq == 2 * LANES
            and 2 * self.src_dev == LANES
            and self.n_src % 2 == 0
            and self.rcv_dev == 2 * LANES
            and self.src_part * self.own == LANES
            and LANES % self.n_dev == 0
            and self.n_pos % LANES == 0
        )


def look_up(lag_ref, pos_ref, begin, count, offset):
    lane = lanes_of(LAG_ROWS)
    acc = jnp.zeros((LAG_ROWS, LANES), jnp.int32)
    for n in range(count):
        pos = pos_ref[begin + n]
        base = pl.multiple_of((pos // LANES) * LANES, LANES)
        tile = lag_ref[:, pl.ds(base, LANES)]
        acc = jnp.where(lane == n, pltpu.roll(tile, (n - pos) & (LANES - 1), 1), acc)
    return (acc - offset).astype(F32).astype(BF16)


def whole(*shape):
    return pl.BlockSpec(shape, lambda *_: (0,) * len(shape))


def pack_sources(z):
    def kernel(pos_ref, src_ref, lag_ref, out_ref, flat):
        lags = look_up(lag_ref, pos_ref, 0, z.src_dev, z.n_freq)
        for row in range(ROWS):
            flat[row * z.src_freq:(row + 1) * z.src_freq, :z.src_dev] = src_ref[row].astype(F32)
        half = z.own // 2
        for rcv in range(z.n_rcv):
            for low in range(z.low):
                for m in range(half):
                    freq = (low * z.n_rcv + rcv) * z.own + m
                    one = flat[pl.ds(freq, ROWS, stride=z.src_freq), :]
                    two = flat[pl.ds(freq + half, ROWS, stride=z.src_freq), :]
                    both = jnp.concatenate([one[:, :z.src_dev], two[:, :z.src_dev]], 1)
                    out_ref[rcv, low, m * ROWS:(m + 1) * ROWS, :] = both.astype(BF16)
                out_ref[rcv, low, z.chunk:, :] = lags

    shape = (z.n_rcv, z.low, z.chunk + LAG_ROWS, LANES)
    return pl.pallas_call(
        kernel,
        grid=(1,),
        in_specs=[
            pl.BlockSpec(memory_space=pltpu.SMEM),
            whole(ROWS, z.src_freq, z.src_dev),
            whole(z.n_slow, z.n_pos),
        ],
        out_specs=whole(*shape),
        out_shape=jax.ShapeDtypeStruct(shape, BF16),
        scratch_shapes=[pltpu.VMEM((ROWS * z.src_freq, LANES), F32)],
        compiler_params=pltpu.CompilerParams(vmem_limit_bytes=FULL_VMEM),
        cost_estimate=pl.CostEstimate(flops=10**6, bytes_accessed=2 * 10**6, transcendentals=0),
        name="pack_sources",
    )


def pack_receivers(z):
    def kernel(pos_ref, rcv_ref, lag_ref, *refs):
        outs, flat = refs[:z.n_rcv], refs[z.n_rcv:]
        spans = range(0, z.rcv_dev, LANES)
        lags = [look_up(lag_ref, pos_ref, span, LANES, z.n_freq) for span in spans]
        for row in range(ROWS):
            here = rcv_ref[row].astype(F32)
            for n, span in enumerate(spans):
                flat[n][row * z.rcv_freq:(row + 1) * z.rcv_freq, :] = here[:, span:span + LANES]
        for other in range(z.n_rcv):
            first = (lax.axis_index("rcv") ^ other) * z.own
            for n, span in enumerate(spans):
                for k in range(z.own):
                    tile = flat[n][pl.ds(first + k, ROWS, stride=z.rcv_freq), :]
                    outs[other][k * ROWS:(k + 1) * ROWS, span:span + LANES] = tile.astype(BF16)
                outs[other][z.own * ROWS:, span:span + LANES] = lags[n]

    shape = (z.own * ROWS + LAG_ROWS, z.rcv_dev)
    return pl.pallas_call(
        kernel,
        grid=(1,),
        in_specs=[
            pl.BlockSpec(memory_space=pltpu.SMEM),
            whole(ROWS, z.rcv_freq, z.rcv_dev),
            whole(z.n_slow, z.n_pos),
        ],
        out_specs=[whole(*shape)] * z.n_rcv,
        out_shape=[jax.ShapeDtypeStruct(shape, BF16)] * z.n_rcv,
        scratch_shapes=[pltpu.VMEM((ROWS * z.rcv_freq, LANES), F32)] * (z.rcv_dev // LANES),
        compiler_params=pltpu.CompilerParams(vmem_limit_bytes=VMEM),
        cost_estimate=pl.CostEstimate(flops=10**6, bytes_accessed=2 * 10**6, transcendentals=0),
        name="pack_receivers",
    )


def cross_spectra(z, src_ref, rcv_refs, turn, left, right, stack):
    half = z.own // 2
    begin = pl.multiple_of(turn % half * ROWS, ROWS)
    odd = turn // half
    lane = lanes_of(ROWS)
    blocks = []
    for block in range(z.s_all // LANES):
        one = src_ref[2 * block, pl.ds(begin, ROWS), :].astype(F32)
        two = src_ref[2 * block + 1, pl.ds(begin, ROWS), :].astype(F32)
        one = jnp.where(odd == 0, one, pltpu.roll(one, z.src_dev, 1))
        two = jnp.where(odd == 0, pltpu.roll(two, z.src_dev, 1), two)
        blocks.append(jnp.where(lane < z.src_dev, one, two))
    left[...] = jnp.transpose(jnp.concatenate(blocks, 1)).astype(BF16)
    rows = pl.ds(pl.multiple_of(turn * ROWS, ROWS), ROWS)
    spec = jnp.concatenate([ref[rows, :] for ref in rcv_refs], 1).astype(F32)
    turned = jnp.concatenate([-spec[z.n_win:], spec[:z.n_win]], 0)
    window = lax.broadcasted_iota(jnp.int32, (ROWS, 1), 0) % z.n_win
    for seg in range(SEGS):
        here = window // WIN == seg
        right[seg] = jnp.where(here, spec, 0.0).astype(BF16)
        right[SEGS + seg] = jnp.where(here, turned, 0.0).astype(BF16)
    width, height = 2 * LANES, TILE_ROWS
    r_now = spec.shape[1]
    for col in range(0, r_now, width):
        for row in range(0, z.s_all, height):
            part = left[row:row + height, :]
            total_re, total_im = 0.0, 0.0
            for seg in range(SEGS):
                real = jnp.dot(part, right[seg, :, col:col + width], preferred_element_type=F32)
                imag = jnp.dot(part, right[SEGS + seg, :, col:col + width], preferred_element_type=F32)
                scale = lax.rsqrt(jnp.maximum(real * real + imag * imag, 1.0))
                total_re, total_im = total_re + real * scale, total_im + imag * scale
            stack[row:row + height, col:col + width] = total_re.astype(BF16)
            stack[z.s_all + row:z.s_all + row + height, col:col + width] = total_im.astype(BF16)


def compute(z, count, first, last):
    src_factor = 1.0 / (SEGS * math.sqrt(z.r_all))
    rcv_factor = 1.0 / (SEGS * math.sqrt(z.s_all))
    n = z.n_slow
    r_now = count * z.rcv_dev
    place_lag = z.own * ROWS

    def kernel(src_ref, *refs):
        rcv_refs, refs = refs[:count], refs[count:]
        if not first:
            before_ref, refs = refs[0], refs[1:]
        out_refs, refs = refs[:count], refs[count:]
        sum_ref, src_lag, rcv_lag, left, right, stack = refs[:6]
        for src in range(z.n_src):
            lags = src_ref[src, z.chunk:, :z.src_dev].astype(F32) + float(z.n_freq)
            src_lag[:, src * z.src_dev:(src + 1) * z.src_dev] = lags
        for block, ref in enumerate(rcv_refs):
            rcv_lag[:, block * z.rcv_dev:(block + 1) * z.rcv_dev] = ref[place_lag:, :].astype(F32) + float(z.n_freq)
        begin = lax.axis_index("src") * z.rcv_freq + lax.axis_index("rcv") * z.own

        def cross(turn, slot):
            cross_spectra(z, src_ref, rcv_refs, turn, left.at[slot], right.at[slot], stack.at[slot])

        def slant(turn, slot):
            freq = (begin + turn).astype(F32)
            src_cos, src_sin = phases(src_lag[...], freq, 2.0 * z.n_freq)
            rcv_cos, rcv_sin = phases(rcv_lag[...], freq, 2.0 * z.n_freq)
            upper = jnp.concatenate([src_cos, src_sin], 1)
            lower = jnp.concatenate([-src_sin, src_cos], 1)
            both = jnp.concatenate([upper, lower], 0).astype(BF16)
            over_src = jnp.dot(both, stack[slot], preferred_element_type=F32) * rcv_factor
            over_re, over_im = over_src[:n], over_src[n:]
            panel_re = over_re * rcv_cos - over_im * rcv_sin
            panel_im = over_re * rcv_sin + over_im * rcv_cos
            panel = jnp.concatenate([panel_re, panel_im], 0).astype(BF16)
            for block, ref in enumerate(out_refs):
                ref[turn] = panel[:, block * z.rcv_dev:(block + 1) * z.rcv_dev]
            dims = (((1,), (1,)), ((), ()))
            with_re = jnp.concatenate([rcv_cos, rcv_sin], 0).astype(BF16)
            with_im = jnp.concatenate([-rcv_sin, rcv_cos], 0).astype(BF16)
            over_rcv = lax.dot_general(with_re, stack[slot, :z.s_all, :], dims, preferred_element_type=F32)
            over_rcv += lax.dot_general(with_im, stack[slot, z.s_all:, :], dims, preferred_element_type=F32)
            if not first:
                over_rcv += before_ref[turn]
            if not last:
                sum_ref[turn] = over_rcv
                return
            over_rcv *= src_factor
            over_re, over_im = over_rcv[:n], over_rcv[n:]
            panel_re = over_re * src_cos + over_im * src_sin
            panel_im = over_im * src_cos - over_re * src_sin
            refs[6][turn] = jnp.concatenate([panel_re, panel_im], 0)

        cross(0, 0)
        for turn in range(1, z.own):
            cross(turn, turn % 2)
            slant(turn - 1, (turn - 1) % 2)
        slant(z.own - 1, (z.own - 1) % 2)
        if last:
            send_sources(z, refs[6], sum_ref)

    in_specs = [whole(z.n_src, z.chunk + LAG_ROWS, LANES)]
    in_specs += [whole(z.own * ROWS + LAG_ROWS, z.rcv_dev)] * count
    out_specs = [whole(z.own, ROWS, z.rcv_dev)] * count
    out_shape = [jax.ShapeDtypeStruct((z.own, ROWS, z.rcv_dev), BF16)] * count
    part_spec = whole(z.own, ROWS, z.s_all)
    scratch = [
        pltpu.VMEM((n, z.s_all), F32),
        pltpu.VMEM((n, r_now), F32),
        pltpu.VMEM((2, z.s_all, ROWS), BF16),
        pltpu.VMEM((2, 2 * SEGS, ROWS, r_now), BF16),
        pltpu.VMEM((2, 2 * z.s_all, r_now), BF16),
    ]
    if not first:
        in_specs.append(part_spec)
    if last:
        out_specs.append(whole(z.n_dev, ROWS, LANES))
        out_shape.append(jax.ShapeDtypeStruct((z.n_dev, ROWS, LANES), BF16))
        scratch.append(pltpu.VMEM((z.own, ROWS, z.s_all), F32))
    else:
        out_specs.append(part_spec)
        out_shape.append(jax.ShapeDtypeStruct((z.own, ROWS, z.s_all), F32))
    return pl.pallas_call(
        kernel,
        grid=(1,),
        in_specs=in_specs,
        out_specs=out_specs,
        out_shape=out_shape,
        scratch_shapes=scratch,
        compiler_params=pltpu.CompilerParams(vmem_limit_bytes=VMEM),
        cost_estimate=pl.CostEstimate(flops=COST * count, bytes_accessed=10**6, transcendentals=0),
        name="compute_first" if first else "compute_last" if last else "compute_next",
    )


def send_sources(z, sums, out_ref):
    lane = lanes_of(ROWS)
    width = z.src_part
    for dev in range(z.n_dev):
        block, place = divmod(dev * width, LANES)
        total = jnp.zeros((ROWS, LANES), F32)
        for k in range(z.own):
            tile = sums[k, :, block * LANES:(block + 1) * LANES]
            shift = (k * width - place) % LANES
            moved = pltpu.roll(tile, shift, 1) if shift else tile
            total = jnp.where((lane >= k * width) & (lane < (k + 1) * width), moved, total)
        out_ref[dev] = total.astype(BF16)


def unpack_block(z, in_ref, flat, write):
    n = z.n_slow
    for span in range(0, z.rcv_dev, LANES):
        for k in range(z.own):
            flat[k * ROWS:(k + 1) * ROWS, :] = in_ref[k, :, span:span + LANES].astype(F32)
        for slow in range(n):
            for part in range(2):
                write(2 * slow + part, span, flat[pl.ds(part * n + slow, z.own, stride=ROWS), :])


def unpack_first(z, others):
    def kernel(*refs):
        in_refs, out_ref, flat = refs[:len(others)], refs[-2], refs[-1]
        for other, in_ref in zip(others, in_refs):
            rows = pl.ds(pl.multiple_of((lax.axis_index("rcv") ^ other) * z.own, z.own), z.own)

            def write(index, span, tile):
                out_ref[index, rows, span:span + LANES] = tile

            unpack_block(z, in_ref, flat, write)

    return pl.pallas_call(
        kernel,
        grid=(1,),
        in_specs=[whole(z.own, ROWS, z.rcv_dev)] * len(others),
        out_specs=whole(ROWS, z.rcv_freq, z.rcv_dev),
        out_shape=jax.ShapeDtypeStruct((ROWS, z.rcv_freq, z.rcv_dev), F32),
        scratch_shapes=[pltpu.VMEM((z.own * ROWS, LANES), F32)],
        compiler_params=pltpu.CompilerParams(vmem_limit_bytes=VMEM),
        cost_estimate=pl.CostEstimate(flops=10**6, bytes_accessed=10**6, transcendentals=0),
        name="unpack_first",
    )


def unpack_last(z, other):
    n = z.n_slow
    group = LANES // z.n_dev
    width = z.src_part

    def kernel(rcv_in, src_in, held_ref, rcv_ref, src_ref, flat, small, table):
        del held_ref

        def write(index, span, tile):
            rcv_ref[index, :, span:span + LANES] = tile

        unpack_block(z, rcv_in, small, write)
        for dev in range(z.n_dev):
            flat[dev * ROWS:(dev + 1) * ROWS, :] = src_in[dev].astype(F32)
        lane = lanes_of(width)
        for first in range(0, ROWS, group):
            tiles = [flat[pl.ds(first + j, z.n_dev, stride=ROWS), :] for j in range(group)]
            turned = jnp.transpose(jnp.concatenate(tiles, 0))
            for j in range(group):
                for block in range(z.own // group):
                    total = jnp.zeros((width, LANES), F32)
                    for k in range(group):
                        row = (block * group + k) * width
                        tile = turned[row:row + width, :]
                        shift = (k - j) * z.n_dev % LANES
                        moved = pltpu.roll(tile, shift, 1) if shift else tile
                        total = jnp.where((lane >= k * z.n_dev) & (lane < (k + 1) * z.n_dev), moved, total)
                    rows = slice((first + j) * width, (first + j + 1) * width)
                    table[rows, block * LANES:(block + 1) * LANES] = total.astype(BF16)
        here = lax.broadcasted_iota(jnp.int32, (z.n_freq, z.n_freq), 0)
        there = lax.broadcasted_iota(jnp.int32, (z.n_freq, z.n_freq), 1)
        order = (there == here % z.n_dev * z.own + here // z.n_dev).astype(F32).astype(BF16)
        for index in range(ROWS):
            part, slow = divmod(index, n)
            rows = table[index * width:(index + 1) * width, :]
            src_ref[2 * slow + part] = jnp.dot(rows, order, preferred_element_type=F32)

    return pl.pallas_call(
        kernel,
        grid=(1,),
        in_specs=[
            whole(z.own, ROWS, z.rcv_dev),
            whole(z.n_dev, ROWS, LANES),
            pl.BlockSpec(memory_space=pl.ANY),
        ],
        out_specs=[
            pl.BlockSpec((ROWS, z.own, z.rcv_dev), lambda k: (0, lax.axis_index("rcv") ^ other, 0)),
            whole(ROWS, width, z.n_freq),
        ],
        scratch_shapes=[
            pltpu.VMEM((z.n_dev * ROWS, LANES), F32),
            pltpu.VMEM((z.own * ROWS, LANES), F32),
            pltpu.VMEM((ROWS * width, z.n_freq), BF16),
        ],
        out_shape=[
            jax.ShapeDtypeStruct((ROWS, z.rcv_freq, z.rcv_dev), F32),
            jax.ShapeDtypeStruct((ROWS, width, z.n_freq), F32),
        ],
        input_output_aliases={2: 0},
        compiler_params=pltpu.CompilerParams(vmem_limit_bytes=VMEM),
        cost_estimate=pl.CostEstimate(flops=10**6, bytes_accessed=2 * 10**6, transcendentals=0),
        name="unpack_last",
    )


def swap(z, block, other):
    if other == 0:
        return block
    return lax.ppermute(block, "rcv", [(j, j ^ other) for j in range(z.n_rcv)])


def per_device(src_spec, rcv_spec, lag_table, src_pos, rcv_pos):
    n_src, n_rcv = lax.axis_size("src"), lax.axis_size("rcv")
    z = Sizes((src_spec.shape, rcv_spec.shape, lag_table.shape), n_src, n_rcv)
    if not z.fits():
        return per_device_general(src_spec, rcv_spec, lag_table, src_pos, rcv_pos)
    src_rows = src_spec.reshape(ROWS, z.src_freq, z.src_dev)
    rcv_rows = rcv_spec.reshape(ROWS, z.rcv_freq, z.rcv_dev)
    spread = lax.all_to_all(pack_sources(z)(src_pos, src_rows, lag_table), "rcv", 0, 0, tiled=True)
    packed = pack_receivers(z)(rcv_pos, rcv_rows, lag_table)
    spread, packed = lax.optimization_barrier((spread, packed))
    spread = spread.reshape(z.n_src, z.chunk + LAG_ROWS, LANES)
    sources = lax.all_to_all(spread, "src", 0, 0, tiled=True)
    blocks = {other: swap(z, packed[other], other) for others in CALLS for other in others}
    done, carry = {}, ()
    for n, others in enumerate(CALLS):
        call = compute(z, len(others), n == 0, n == len(CALLS) - 1)
        *panels, total = call(sources, *(blocks[other] for other in others), *carry)
        done.update({other: swap(z, panel, other) for other, panel in zip(others, panels)})
        carry = (total,)
    late = CALLS[-1][0]
    early = tuple(other for others in CALLS[:-1] for other in others)
    total, arrived = lax.optimization_barrier((total, [done[other] for other in early]))
    done.update(zip(early, arrived))
    got_src = lax.all_to_all(total, ("src", "rcv"), 0, 0, tiled=True)
    held = unpack_first(z, early)(*(done[other] for other in early))
    panel_rcv, panel_src = unpack_last(z, late)(done[late], got_src, held)
    return (
        panel_src.reshape(z.n_slow, 2, z.src_part, z.n_freq),
        panel_rcv.reshape(z.n_slow, 2, z.rcv_freq, z.rcv_dev),
    )


def solution(mesh):
    placed = (P(None, None, "rcv", "src"), P(None, None, "src", "rcv"), P(), P("src"), P("rcv"))
    return jax.shard_map(
        per_device,
        mesh=mesh,
        in_specs=placed,
        out_specs=(P(None, None, ("src", "rcv"), None), P(None, None, "src", "rcv")),
        check_vma=False,
    )
```

```python
import math

import jax
import jax.numpy as jnp
from jax import lax
from jax.experimental import pallas as pl
from jax.experimental.pallas import tpu as pltpu
from jax.sharding import PartitionSpec as P

WIN = 8
SEGS = 2


def phase_table(freqs, lags, n_freq):
    index_mod = freqs[:, None, None] * jnp.transpose(lags)[None, :, :] % (2 * n_freq)
    angles = index_mod.astype(jnp.float32) * (math.pi / n_freq)
    return (jnp.cos(angles), jnp.sin(angles))


def cross_block(src_block, rcv_block):
    block_width = src_block.shape[2]
    src_five = src_block.reshape(2, SEGS, WIN, block_width, src_block.shape[3])
    rcv_five = rcv_block.reshape(2, SEGS, WIN, block_width, rcv_block.shape[3])
    swapped = jnp.stack([src_five[1], -src_five[0]])
    real_part = jnp.einsum(
        "cgwfs,cgwfr->gfsr", src_five, rcv_five, preferred_element_type=jnp.float32
    )
    imag_part = jnp.einsum(
        "cgwfs,cgwfr->gfsr", swapped, rcv_five, preferred_element_type=jnp.float32
    )
    floor_mod = jnp.maximum(jnp.sqrt(real_part * real_part + imag_part * imag_part), 1.0)
    stacked_re = (jnp.sum(real_part / floor_mod, axis=0) / SEGS).astype(jnp.bfloat16)
    stacked_im = (jnp.sum(imag_part / floor_mod, axis=0) / SEGS).astype(jnp.bfloat16)
    return (stacked_re, stacked_im)


def source_slant(stacked_re, stacked_im, rcv_cos, rcv_sin, src_cos, src_sin, factor):
    left_op = jnp.concatenate([stacked_re, stacked_im], axis=2)
    cos_b = rcv_cos.astype(jnp.bfloat16)
    sin_b = rcv_sin.astype(jnp.bfloat16)
    upper_half = jnp.concatenate([cos_b, sin_b], axis=2)
    bottom = jnp.concatenate([-sin_b, cos_b], axis=2)
    right_op = jnp.concatenate([upper_half, bottom], axis=1)
    sums = jnp.einsum("fsk,fkq->fsq", left_op, right_op, preferred_element_type=jnp.float32)
    n_slow = rcv_cos.shape[2]
    sum_re = sums[:, :, :n_slow]
    sum_im = sums[:, :, n_slow:]
    panel_re = (sum_re * src_cos + sum_im * src_sin) * factor
    panel_im = (sum_im * src_cos - sum_re * src_sin) * factor
    return jnp.transpose(jnp.stack([panel_re, panel_im]), (3, 0, 2, 1))


def receiver_right(src_cos_b, src_sin_b):
    upper_half = jnp.concatenate([src_cos_b, -src_sin_b], axis=2)
    bottom = jnp.concatenate([src_sin_b, src_cos_b], axis=2)
    return jnp.concatenate([upper_half, bottom], axis=1)


def receiver_sums(left_op, right_op):
    return jnp.einsum("fkr,fkq->fqr", left_op, right_op, preferred_element_type=jnp.float32)


def receiver_outer(sums, rcv_cos, rcv_sin, factor):
    n_slow = rcv_cos.shape[2]
    cos_t = jnp.transpose(rcv_cos, (0, 2, 1))
    sin_t = jnp.transpose(rcv_sin, (0, 2, 1))
    sum_re = sums[:, :n_slow, :]
    sum_im = sums[:, n_slow:, :]
    panel_re = (sum_re * cos_t - sum_im * sin_t) * factor
    panel_im = (sum_re * sin_t + sum_im * cos_t) * factor
    return jnp.transpose(jnp.stack([panel_re, panel_im]), (2, 0, 1, 3))


def per_device_general(src_spec, rcv_spec, lag_table, src_pos, rcv_pos):
    src_full = lax.all_gather(src_spec, "rcv", axis=2, tiled=True)
    n_freq = src_full.shape[2]
    src_dev = src_full.shape[3]
    rcv_dev = rcv_spec.shape[3]
    n_slow = lag_table.shape[0]
    n_src = lax.axis_size("src")
    n_rcv = lax.axis_size("rcv")
    src_factor = 1.0 / math.sqrt(rcv_dev * n_rcv)
    rcv_factor = 1.0 / math.sqrt(src_dev * n_src)
    lag_src = jnp.take(lag_table, src_pos, axis=1)
    lag_rcv = jnp.take(lag_table, rcv_pos, axis=1)
    src_init = jnp.zeros((n_slow, 2, src_dev, n_freq), jnp.float32)
    other_init = jnp.zeros((n_slow, 2, n_freq, rcv_dev), jnp.float32)
    shard_piece = lax.all_gather(rcv_spec, "src", axis=2, tiled=True)
    block_width = math.gcd(shard_piece.shape[2], 16)

    def inner(turn_index, totals):
        offset = turn_index * block_width
        freqs = offset + jnp.arange(block_width, dtype=jnp.int32)
        src_block = lax.dynamic_slice_in_dim(src_full, offset, block_width, 2)
        rcv_block = lax.dynamic_slice_in_dim(shard_piece, offset, block_width, 2)
        stacked_re, stacked_im = cross_block(src_block, rcv_block)
        rcv_cos, rcv_sin = phase_table(freqs, lag_rcv, n_freq)
        src_cos, src_sin = phase_table(freqs, lag_src, n_freq)
        src_part = source_slant(
            stacked_re, stacked_im, rcv_cos, rcv_sin, src_cos, src_sin, src_factor
        )
        src_total = lax.dynamic_update_slice_in_dim(totals[0], src_part, offset, 3)
        left_op = jnp.concatenate([stacked_re, stacked_im], axis=1)
        right_op = receiver_right(src_cos.astype(jnp.bfloat16), src_sin.astype(jnp.bfloat16))
        rcv_part = receiver_outer(receiver_sums(left_op, right_op), rcv_cos, rcv_sin, rcv_factor)
        other = lax.dynamic_update_slice_in_dim(totals[1], rcv_part, offset, 2)
        return (src_total, other)

    src_total, other = lax.fori_loop(
        0, shard_piece.shape[2] // block_width, inner, (src_init, other_init)
    )
    panel_src = lax.psum_scatter(src_total, "rcv", scatter_dimension=2, tiled=True)
    panel_rcv = lax.psum_scatter(other, "src", scatter_dimension=2, tiled=True)
    return (panel_src, panel_rcv)


LANES = 128
ROWS = 32
LAG_ROWS = 16
CALLS = ((0,), (3,), (2,), (1,))
VMEM = 20 * 2**20
FULL_VMEM = 56 * 2**20
TILE_ROWS = 64
COST = 10**6
F32 = jnp.float32
BF16 = jnp.bfloat16
SIN = [(-1) ** n * (math.pi / 2) ** (2 * n + 1) / math.factorial(2 * n + 1) for n in range(5)]
COS = [(-1) ** n * (math.pi / 2) ** (2 * n) / math.factorial(2 * n) for n in range(6)]


def horner(coefs, v):
    total = coefs[-1]
    for coef in coefs[-2::-1]:
        total = coef + v * total
    return total


def phases(lag, freq, period):
    turns = lag * freq * (1.0 / period)
    quarters = 4.0 * (turns - jnp.floor(turns))
    near = jnp.floor(quarters + 0.5)
    u = quarters - near
    v = u * u
    s = u * horner(SIN, v)
    c = horner(COS, v)
    odd = (near == 1.0) | (near == 3.0)
    cos = jnp.where(odd, s, c)
    sin = jnp.where(odd, c, s)
    cos = jnp.where((near == 1.0) | (near == 2.0), -cos, cos)
    sin = jnp.where((near == 2.0) | (near == 3.0), -sin, sin)
    return cos, sin


def lanes_of(rows):
    return lax.broadcasted_iota(jnp.int32, (rows, LANES), 1)


class Sizes:
    def __init__(self, shapes, n_src, n_rcv):
        src_spec, rcv_spec, lag_table = shapes
        self.n_src, self.n_rcv, self.n_dev = n_src, n_rcv, n_src * n_rcv
        self.n_slow, self.n_pos = lag_table
        self.n_win = src_spec[1]
        self.src_freq, self.src_dev = src_spec[2:]
        self.rcv_freq, self.rcv_dev = rcv_spec[2:]
        self.n_freq = self.rcv_freq * n_src
        self.own = self.n_freq // self.n_dev
        self.s_all, self.r_all = self.src_dev * n_src, self.rcv_dev * n_rcv
        self.src_part = self.src_dev // n_rcv
        self.low = n_src // n_rcv
        self.chunk = self.own // 2 * ROWS

    def fits(self):
        return (
            2 * self.n_win == ROWS
            and 2 * self.n_slow == ROWS
            and self.n_win == WIN * SEGS
            and self.n_rcv == 4
            and self.own == 8
            and self.src_freq == self.low * self.n_rcv * self.own
            and self.rcv_freq == self.n_rcv * self.own
            and self.n_dev * self.own == self.n_freq == 2 * LANES
            and 2 * self.src_dev == LANES
            and self.n_src % 2 == 0
            and self.rcv_dev == 2 * LANES
            and self.src_part * self.own == LANES
            and LANES % self.n_dev == 0
            and self.n_pos % LANES == 0
        )


def look_up(lag_ref, pos_ref, begin, count, offset):
    lane = lanes_of(LAG_ROWS)
    acc = jnp.zeros((LAG_ROWS, LANES), jnp.int32)
    for n in range(count):
        pos = pos_ref[begin + n]
        base = pl.multiple_of((pos // LANES) * LANES, LANES)
        tile = lag_ref[:, pl.ds(base, LANES)]
        acc = jnp.where(lane == n, pltpu.roll(tile, (n - pos) & (LANES - 1), 1), acc)
    return (acc - offset).astype(F32)


def whole(*shape):
    return pl.BlockSpec(shape, lambda *_: (0,) * len(shape))


def pack_sources(z):
    def kernel(pos_ref, src_ref, lag_ref, out_ref, flat):
        lags = look_up(lag_ref, pos_ref, 0, z.src_dev, z.n_freq)[:, :z.src_dev]
        lags = jnp.concatenate([lags[:LAG_ROWS // 2], lags[LAG_ROWS // 2:]], 1).astype(BF16)
        for row in range(ROWS):
            flat[row * z.src_freq:(row + 1) * z.src_freq, :z.src_dev] = src_ref[row].astype(F32)
        half = z.own // 2
        for rcv in range(z.n_rcv):
            for low in range(z.low):
                for m in range(half):
                    freq = (low * z.n_rcv + rcv) * z.own + m
                    one = flat[pl.ds(freq, ROWS, stride=z.src_freq), :]
                    two = flat[pl.ds(freq + half, ROWS, stride=z.src_freq), :]
                    both = jnp.concatenate([one[:, :z.src_dev], two[:, :z.src_dev]], 1)
                    out_ref[rcv, low, m * ROWS:(m + 1) * ROWS, :] = both.astype(BF16)
                out_ref[rcv, low, z.chunk:, :] = lags

    shape = (z.n_rcv, z.low, z.chunk + LAG_ROWS // 2, LANES)
    return pl.pallas_call(
        kernel,
        grid=(1,),
        in_specs=[
            pl.BlockSpec(memory_space=pltpu.SMEM),
            whole(ROWS, z.src_freq, z.src_dev),
            whole(z.n_slow, z.n_pos),
        ],
        out_specs=whole(*shape),
        out_shape=jax.ShapeDtypeStruct(shape, BF16),
        scratch_shapes=[pltpu.VMEM((ROWS * z.src_freq, LANES), F32)],
        compiler_params=pltpu.CompilerParams(vmem_limit_bytes=FULL_VMEM),
        cost_estimate=pl.CostEstimate(flops=10**6, bytes_accessed=2 * 10**6, transcendentals=0),
        name="pack_sources",
    )


def pack_receivers(z):
    def kernel(pos_ref, rcv_ref, lag_ref, *refs):
        outs, flat = refs[:z.n_rcv], refs[z.n_rcv:]
        spans = range(0, z.rcv_dev, LANES)
        lags = [look_up(lag_ref, pos_ref, span, LANES, z.n_freq).astype(BF16) for span in spans]
        for row in range(ROWS):
            here = rcv_ref[row].astype(F32)
            for n, span in enumerate(spans):
                flat[n][row * z.rcv_freq:(row + 1) * z.rcv_freq, :] = here[:, span:span + LANES]
        for other in range(z.n_rcv):
            first = (lax.axis_index("rcv") ^ other) * z.own
            for n, span in enumerate(spans):
                for k in range(z.own):
                    tile = flat[n][pl.ds(first + k, ROWS, stride=z.rcv_freq), :]
                    outs[other][k * ROWS:(k + 1) * ROWS, span:span + LANES] = tile.astype(BF16)
                outs[other][z.own * ROWS:, span:span + LANES] = lags[n]

    shape = (z.own * ROWS + LAG_ROWS, z.rcv_dev)
    return pl.pallas_call(
        kernel,
        grid=(1,),
        in_specs=[
            pl.BlockSpec(memory_space=pltpu.SMEM),
            whole(ROWS, z.rcv_freq, z.rcv_dev),
            whole(z.n_slow, z.n_pos),
        ],
        out_specs=[whole(*shape)] * z.n_rcv,
        out_shape=[jax.ShapeDtypeStruct(shape, BF16)] * z.n_rcv,
        scratch_shapes=[pltpu.VMEM((ROWS * z.rcv_freq, LANES), F32)] * (z.rcv_dev // LANES),
        compiler_params=pltpu.CompilerParams(vmem_limit_bytes=VMEM),
        cost_estimate=pl.CostEstimate(flops=10**6, bytes_accessed=2 * 10**6, transcendentals=0),
        name="pack_receivers",
    )


def cross_spectra(z, src_ref, rcv_refs, turn, left, right, stack):
    half = z.own // 2
    begin = pl.multiple_of(turn % half * ROWS, ROWS)
    odd = turn // half
    lane = lanes_of(ROWS)
    blocks = []
    for block in range(z.s_all // LANES):
        one = src_ref[2 * block, pl.ds(begin, ROWS), :].astype(F32)
        two = src_ref[2 * block + 1, pl.ds(begin, ROWS), :].astype(F32)
        one = jnp.where(odd == 0, one, pltpu.roll(one, z.src_dev, 1))
        two = jnp.where(odd == 0, pltpu.roll(two, z.src_dev, 1), two)
        blocks.append(jnp.where(lane < z.src_dev, one, two))
    left[...] = jnp.transpose(jnp.concatenate(blocks, 1)).astype(BF16)
    rows = pl.ds(pl.multiple_of(turn * ROWS, ROWS), ROWS)
    spec = jnp.concatenate([ref[rows, :] for ref in rcv_refs], 1).astype(F32)
    turned = jnp.concatenate([-spec[z.n_win:], spec[:z.n_win]], 0)
    window = lax.broadcasted_iota(jnp.int32, (ROWS, 1), 0) % z.n_win
    for seg in range(SEGS):
        here = window // WIN == seg
        right[seg] = jnp.where(here, spec, 0.0).astype(BF16)
        right[SEGS + seg] = jnp.where(here, turned, 0.0).astype(BF16)
    width, height = 2 * LANES, TILE_ROWS
    r_now = spec.shape[1]
    for col in range(0, r_now, width):
        for row in range(0, z.s_all, height):
            part = left[row:row + height, :]
            total_re, total_im = 0.0, 0.0
            for seg in range(SEGS):
                real = jnp.dot(part, right[seg, :, col:col + width], preferred_element_type=F32)
                imag = jnp.dot(part, right[SEGS + seg, :, col:col + width], preferred_element_type=F32)
                scale = lax.rsqrt(jnp.maximum(real * real + imag * imag, 1.0))
                total_re, total_im = total_re + real * scale, total_im + imag * scale
            stack[row:row + height, col:col + width] = total_re.astype(BF16)
            stack[z.s_all + row:z.s_all + row + height, col:col + width] = total_im.astype(BF16)


def compute(z, count, first, last):
    src_factor = 1.0 / (SEGS * math.sqrt(z.r_all))
    rcv_factor = 1.0 / (SEGS * math.sqrt(z.s_all))
    n = z.n_slow
    r_now = count * z.rcv_dev
    place_lag = z.own * ROWS

    def kernel(src_ref, *refs):
        rcv_refs, refs = refs[:count], refs[count:]
        if not first:
            before_ref, refs = refs[0], refs[1:]
        out_refs, refs = refs[:count], refs[count:]
        sum_ref, src_lag, rcv_lag, left, right, stack = refs[:6]
        for src in range(z.n_src):
            lags = src_ref[src, z.chunk:, :].astype(F32) + float(z.n_freq)
            for part in range(2):
                rows = slice(part * LAG_ROWS // 2, (part + 1) * LAG_ROWS // 2)
                lanes = slice(part * z.src_dev, (part + 1) * z.src_dev)
                src_lag[rows, src * z.src_dev:(src + 1) * z.src_dev] = lags[:, lanes]
        for block, ref in enumerate(rcv_refs):
            rcv_lag[:, block * z.rcv_dev:(block + 1) * z.rcv_dev] = ref[place_lag:, :].astype(F32) + float(z.n_freq)
        begin = lax.axis_index("src") * z.rcv_freq + lax.axis_index("rcv") * z.own

        def cross(turn, slot):
            cross_spectra(z, src_ref, rcv_refs, turn, left.at[slot], right.at[slot], stack.at[slot])

        def slant(turn, slot):
            freq = (begin + turn).astype(F32)
            src_cos, src_sin = phases(src_lag[...], freq, 2.0 * z.n_freq)
            rcv_cos, rcv_sin = phases(rcv_lag[...], freq, 2.0 * z.n_freq)
            upper = jnp.concatenate([src_cos, src_sin], 1)
            lower = jnp.concatenate([-src_sin, src_cos], 1)
            both = jnp.concatenate([upper, lower], 0).astype(BF16)
            over_src = jnp.dot(both, stack[slot], preferred_element_type=F32) * rcv_factor
            over_re, over_im = over_src[:n], over_src[n:]
            panel_re = over_re * rcv_cos - over_im * rcv_sin
            panel_im = over_re * rcv_sin + over_im * rcv_cos
            panel = jnp.concatenate([panel_re, panel_im], 0).astype(BF16)
            for block, ref in enumerate(out_refs):
                ref[turn] = panel[:, block * z.rcv_dev:(block + 1) * z.rcv_dev]
            dims = (((1,), (1,)), ((), ()))
            with_re = jnp.concatenate([rcv_cos, rcv_sin], 0).astype(BF16)
            with_im = jnp.concatenate([-rcv_sin, rcv_cos], 0).astype(BF16)
            over_rcv = lax.dot_general(with_re, stack[slot, :z.s_all, :], dims, preferred_element_type=F32)
            over_rcv += lax.dot_general(with_im, stack[slot, z.s_all:, :], dims, preferred_element_type=F32)
            if not first:
                over_rcv += before_ref[turn]
            if not last:
                sum_ref[turn] = over_rcv
                return
            over_rcv *= src_factor
            over_re, over_im = over_rcv[:n], over_rcv[n:]
            panel_re = over_re * src_cos + over_im * src_sin
            panel_im = over_im * src_cos - over_re * src_sin
            panel = jnp.concatenate([panel_re, panel_im], 0)
            width, acc = z.src_part, refs[6]
            lanes = slice(turn * width, (turn + 1) * width)
            for dev in range(z.n_dev):
                block, place = divmod(dev * width, LANES)
                tile = panel[:, block * LANES:(block + 1) * LANES]
                shift = (turn * width - place) % LANES
                moved = pltpu.roll(tile, shift, 1) if shift else tile
                acc[dev, :, lanes] = moved[:, lanes]

        cross(0, 0)
        for turn in range(1, z.own):
            cross(turn, turn % 2)
            slant(turn - 1, (turn - 1) % 2)
        slant(z.own - 1, (z.own - 1) % 2)
        if last:
            sum_ref[...] = refs[6][...].astype(BF16)

    in_specs = [whole(z.n_src, z.chunk + LAG_ROWS // 2, LANES)]
    in_specs += [whole(z.own * ROWS + LAG_ROWS, z.rcv_dev)] * count
    out_specs = [whole(z.own, ROWS, z.rcv_dev)] * count
    out_shape = [jax.ShapeDtypeStruct((z.own, ROWS, z.rcv_dev), BF16)] * count
    part_spec = whole(z.own, ROWS, z.s_all)
    scratch = [
        pltpu.VMEM((n, z.s_all), F32),
        pltpu.VMEM((n, r_now), F32),
        pltpu.VMEM((2, z.s_all, ROWS), BF16),
        pltpu.VMEM((2, 2 * SEGS, ROWS, r_now), BF16),
        pltpu.VMEM((2, 2 * z.s_all, r_now), BF16),
    ]
    if not first:
        in_specs.append(part_spec)
    if last:
        out_specs.append(whole(z.n_dev, ROWS, LANES))
        out_shape.append(jax.ShapeDtypeStruct((z.n_dev, ROWS, LANES), BF16))
        scratch.append(pltpu.VMEM((z.n_dev, ROWS, LANES), F32))
    else:
        out_specs.append(part_spec)
        out_shape.append(jax.ShapeDtypeStruct((z.own, ROWS, z.s_all), F32))
    return pl.pallas_call(
        kernel,
        grid=(1,),
        in_specs=in_specs,
        out_specs=out_specs,
        out_shape=out_shape,
        scratch_shapes=scratch,
        compiler_params=pltpu.CompilerParams(vmem_limit_bytes=VMEM),
        cost_estimate=pl.CostEstimate(flops=COST * count, bytes_accessed=10**6, transcendentals=0),
        name="compute_first" if first else "compute_last" if last else "compute_next",
    )


def unpack_block(z, in_ref, flat, write):
    n = z.n_slow
    for span in range(0, z.rcv_dev, LANES):
        for k in range(z.own):
            flat[k * ROWS:(k + 1) * ROWS, :] = in_ref[k, :, span:span + LANES].astype(F32)
        for slow in range(n):
            for part in range(2):
                write(2 * slow + part, span, flat[pl.ds(part * n + slow, z.own, stride=ROWS), :])


def unpack_first(z, others):
    def kernel(*refs):
        in_refs, out_ref, flat = refs[:len(others)], refs[-2], refs[-1]
        for other, in_ref in zip(others, in_refs):
            rows = pl.ds(pl.multiple_of((lax.axis_index("rcv") ^ other) * z.own, z.own), z.own)

            def write(index, span, tile):
                out_ref[index, rows, span:span + LANES] = tile

            unpack_block(z, in_ref, flat, write)

    return pl.pallas_call(
        kernel,
        grid=(1,),
        in_specs=[whole(z.own, ROWS, z.rcv_dev)] * len(others),
        out_specs=whole(ROWS, z.rcv_freq, z.rcv_dev),
        out_shape=jax.ShapeDtypeStruct((ROWS, z.rcv_freq, z.rcv_dev), F32),
        scratch_shapes=[pltpu.VMEM((z.own * ROWS, LANES), F32)],
        compiler_params=pltpu.CompilerParams(vmem_limit_bytes=VMEM),
        cost_estimate=pl.CostEstimate(flops=10**6, bytes_accessed=10**6, transcendentals=0),
        name="unpack_first",
    )


def unpack_last(z, other):
    n = z.n_slow
    group = LANES // z.n_dev
    width = z.src_part

    def kernel(rcv_in, src_in, held_ref, rcv_ref, src_ref, flat, small, table):
        del held_ref

        def write(index, span, tile):
            rcv_ref[index, :, span:span + LANES] = tile

        unpack_block(z, rcv_in, small, write)
        for dev in range(z.n_dev):
            flat[dev * ROWS:(dev + 1) * ROWS, :] = src_in[dev].astype(F32)
        lane = lanes_of(width)
        for first in range(0, ROWS, group):
            tiles = [flat[pl.ds(first + j, z.n_dev, stride=ROWS), :] for j in range(group)]
            turned = jnp.transpose(jnp.concatenate(tiles, 0))
            for j in range(group):
                for block in range(z.own // group):
                    total = jnp.zeros((width, LANES), F32)
                    for k in range(group):
                        row = (block * group + k) * width
                        tile = turned[row:row + width, :]
                        shift = (k - j) * z.n_dev % LANES
                        moved = pltpu.roll(tile, shift, 1) if shift else tile
                        total = jnp.where((lane >= k * z.n_dev) & (lane < (k + 1) * z.n_dev), moved, total)
                    rows = slice((first + j) * width, (first + j + 1) * width)
                    table[rows, block * LANES:(block + 1) * LANES] = total.astype(BF16)
        here = lax.broadcasted_iota(jnp.int32, (z.n_freq, z.n_freq), 0)
        there = lax.broadcasted_iota(jnp.int32, (z.n_freq, z.n_freq), 1)
        order = (there == here % z.n_dev * z.own + here // z.n_dev).astype(F32).astype(BF16)
        for index in range(ROWS):
            part, slow = divmod(index, n)
            rows = table[index * width:(index + 1) * width, :]
            src_ref[2 * slow + part] = jnp.dot(rows, order, preferred_element_type=F32)

    return pl.pallas_call(
        kernel,
        grid=(1,),
        in_specs=[
            whole(z.own, ROWS, z.rcv_dev),
            whole(z.n_dev, ROWS, LANES),
            pl.BlockSpec(memory_space=pl.ANY),
        ],
        out_specs=[
            pl.BlockSpec((ROWS, z.own, z.rcv_dev), lambda k: (0, lax.axis_index("rcv") ^ other, 0)),
            whole(ROWS, width, z.n_freq),
        ],
        scratch_shapes=[
            pltpu.VMEM((z.n_dev * ROWS, LANES), F32),
            pltpu.VMEM((z.own * ROWS, LANES), F32),
            pltpu.VMEM((ROWS * width, z.n_freq), BF16),
        ],
        out_shape=[
            jax.ShapeDtypeStruct((ROWS, z.rcv_freq, z.rcv_dev), F32),
            jax.ShapeDtypeStruct((ROWS, width, z.n_freq), F32),
        ],
        input_output_aliases={2: 0},
        compiler_params=pltpu.CompilerParams(vmem_limit_bytes=VMEM),
        cost_estimate=pl.CostEstimate(flops=10**6, bytes_accessed=2 * 10**6, transcendentals=0),
        name="unpack_last",
    )


def swap(z, block, other):
    if other == 0:
        return block
    return lax.ppermute(block, "rcv", [(j, j ^ other) for j in range(z.n_rcv)])


def arrive(done, others, values):
    here, values = lax.optimization_barrier(([done[other] for other in others], values))
    done.update(zip(others, here))
    return values


def per_device(src_spec, rcv_spec, lag_table, src_pos, rcv_pos):
    n_src, n_rcv = lax.axis_size("src"), lax.axis_size("rcv")
    z = Sizes((src_spec.shape, rcv_spec.shape, lag_table.shape), n_src, n_rcv)
    if not z.fits():
        return per_device_general(src_spec, rcv_spec, lag_table, src_pos, rcv_pos)
    src_rows = src_spec.reshape(ROWS, z.src_freq, z.src_dev)
    rcv_rows = rcv_spec.reshape(ROWS, z.rcv_freq, z.rcv_dev)
    spread = lax.all_to_all(pack_sources(z)(src_pos, src_rows, lag_table), "rcv", 0, 0, tiled=True)
    packed = pack_receivers(z)(rcv_pos, rcv_rows, lag_table)
    spread, packed = lax.optimization_barrier((spread, packed))
    spread = spread.reshape(z.n_src, z.chunk + LAG_ROWS // 2, LANES)
    sources = lax.all_to_all(spread, "src", 0, 0, tiled=True)
    blocks = {other: swap(z, packed[other], other) for others in CALLS for other in others}
    done, carry = {}, ()
    for n, others in enumerate(CALLS):
        ready = [blocks[other] for other in others]
        if n >= 2:
            ready, carry = arrive(done, CALLS[n - 2], (ready, carry))
        call = compute(z, len(others), n == 0, n == len(CALLS) - 1)
        *panels, total = call(sources, *ready, *carry)
        done.update({other: swap(z, panel, other) for other, panel in zip(others, panels)})
        carry = (total,)
    total = arrive(done, CALLS[-2], total)
    got_src = lax.all_to_all(total, ("src", "rcv"), 0, 0, tiled=True)
    late = CALLS[-1][0]
    early = tuple(other for other in done if other != late)
    held = unpack_first(z, early)(*(done[other] for other in early))
    panel_rcv, panel_src = unpack_last(z, late)(done[late], got_src, held)
    return (
        panel_src.reshape(z.n_slow, 2, z.src_part, z.n_freq),
        panel_rcv.reshape(z.n_slow, 2, z.rcv_freq, z.rcv_dev),
    )


def solution(mesh):
    placed = (P(None, None, "rcv", "src"), P(None, None, "src", "rcv"), P(), P("src"), P("rcv"))
    return jax.shard_map(
        per_device,
        mesh=mesh,
        in_specs=placed,
        out_specs=(P(None, None, ("src", "rcv"), None), P(None, None, "src", "rcv")),
        check_vma=False,
    )
```

```python
import math

import jax
import jax.numpy as jnp
from jax import lax
from jax.experimental import pallas as pl
from jax.experimental.pallas import tpu as pltpu
from jax.sharding import PartitionSpec as P

WIN = 8
SEGS = 2


def phase_table(freqs, lags, n_freq):
    index_mod = freqs[:, None, None] * jnp.transpose(lags)[None, :, :] % (2 * n_freq)
    angles = index_mod.astype(jnp.float32) * (math.pi / n_freq)
    return (jnp.cos(angles), jnp.sin(angles))


def cross_block(src_block, rcv_block):
    block_width = src_block.shape[2]
    src_five = src_block.reshape(2, SEGS, WIN, block_width, src_block.shape[3])
    rcv_five = rcv_block.reshape(2, SEGS, WIN, block_width, rcv_block.shape[3])
    swapped = jnp.stack([src_five[1], -src_five[0]])
    real_part = jnp.einsum(
        "cgwfs,cgwfr->gfsr", src_five, rcv_five, preferred_element_type=jnp.float32
    )
    imag_part = jnp.einsum(
        "cgwfs,cgwfr->gfsr", swapped, rcv_five, preferred_element_type=jnp.float32
    )
    floor_mod = jnp.maximum(jnp.sqrt(real_part * real_part + imag_part * imag_part), 1.0)
    stacked_re = (jnp.sum(real_part / floor_mod, axis=0) / SEGS).astype(jnp.bfloat16)
    stacked_im = (jnp.sum(imag_part / floor_mod, axis=0) / SEGS).astype(jnp.bfloat16)
    return (stacked_re, stacked_im)


def source_slant(stacked_re, stacked_im, rcv_cos, rcv_sin, src_cos, src_sin, factor):
    left_op = jnp.concatenate([stacked_re, stacked_im], axis=2)
    cos_b = rcv_cos.astype(jnp.bfloat16)
    sin_b = rcv_sin.astype(jnp.bfloat16)
    upper_half = jnp.concatenate([cos_b, sin_b], axis=2)
    bottom = jnp.concatenate([-sin_b, cos_b], axis=2)
    right_op = jnp.concatenate([upper_half, bottom], axis=1)
    sums = jnp.einsum("fsk,fkq->fsq", left_op, right_op, preferred_element_type=jnp.float32)
    n_slow = rcv_cos.shape[2]
    sum_re = sums[:, :, :n_slow]
    sum_im = sums[:, :, n_slow:]
    panel_re = (sum_re * src_cos + sum_im * src_sin) * factor
    panel_im = (sum_im * src_cos - sum_re * src_sin) * factor
    return jnp.transpose(jnp.stack([panel_re, panel_im]), (3, 0, 2, 1))


def receiver_right(src_cos_b, src_sin_b):
    upper_half = jnp.concatenate([src_cos_b, -src_sin_b], axis=2)
    bottom = jnp.concatenate([src_sin_b, src_cos_b], axis=2)
    return jnp.concatenate([upper_half, bottom], axis=1)


def receiver_sums(left_op, right_op):
    return jnp.einsum("fkr,fkq->fqr", left_op, right_op, preferred_element_type=jnp.float32)


def receiver_outer(sums, rcv_cos, rcv_sin, factor):
    n_slow = rcv_cos.shape[2]
    cos_t = jnp.transpose(rcv_cos, (0, 2, 1))
    sin_t = jnp.transpose(rcv_sin, (0, 2, 1))
    sum_re = sums[:, :n_slow, :]
    sum_im = sums[:, n_slow:, :]
    panel_re = (sum_re * cos_t - sum_im * sin_t) * factor
    panel_im = (sum_re * sin_t + sum_im * cos_t) * factor
    return jnp.transpose(jnp.stack([panel_re, panel_im]), (2, 0, 1, 3))


def per_device_general(src_spec, rcv_spec, lag_table, src_pos, rcv_pos):
    src_full = lax.all_gather(src_spec, "rcv", axis=2, tiled=True)
    n_freq = src_full.shape[2]
    src_dev = src_full.shape[3]
    rcv_dev = rcv_spec.shape[3]
    n_slow = lag_table.shape[0]
    n_src = lax.axis_size("src")
    n_rcv = lax.axis_size("rcv")
    src_factor = 1.0 / math.sqrt(rcv_dev * n_rcv)
    rcv_factor = 1.0 / math.sqrt(src_dev * n_src)
    lag_src = jnp.take(lag_table, src_pos, axis=1)
    lag_rcv = jnp.take(lag_table, rcv_pos, axis=1)
    src_init = jnp.zeros((n_slow, 2, src_dev, n_freq), jnp.float32)
    other_init = jnp.zeros((n_slow, 2, n_freq, rcv_dev), jnp.float32)
    shard_piece = lax.all_gather(rcv_spec, "src", axis=2, tiled=True)
    block_width = math.gcd(shard_piece.shape[2], 16)

    def inner(turn_index, totals):
        offset = turn_index * block_width
        freqs = offset + jnp.arange(block_width, dtype=jnp.int32)
        src_block = lax.dynamic_slice_in_dim(src_full, offset, block_width, 2)
        rcv_block = lax.dynamic_slice_in_dim(shard_piece, offset, block_width, 2)
        stacked_re, stacked_im = cross_block(src_block, rcv_block)
        rcv_cos, rcv_sin = phase_table(freqs, lag_rcv, n_freq)
        src_cos, src_sin = phase_table(freqs, lag_src, n_freq)
        src_part = source_slant(
            stacked_re, stacked_im, rcv_cos, rcv_sin, src_cos, src_sin, src_factor
        )
        src_total = lax.dynamic_update_slice_in_dim(totals[0], src_part, offset, 3)
        left_op = jnp.concatenate([stacked_re, stacked_im], axis=1)
        right_op = receiver_right(src_cos.astype(jnp.bfloat16), src_sin.astype(jnp.bfloat16))
        rcv_part = receiver_outer(receiver_sums(left_op, right_op), rcv_cos, rcv_sin, rcv_factor)
        other = lax.dynamic_update_slice_in_dim(totals[1], rcv_part, offset, 2)
        return (src_total, other)

    src_total, other = lax.fori_loop(
        0, shard_piece.shape[2] // block_width, inner, (src_init, other_init)
    )
    panel_src = lax.psum_scatter(src_total, "rcv", scatter_dimension=2, tiled=True)
    panel_rcv = lax.psum_scatter(other, "src", scatter_dimension=2, tiled=True)
    return (panel_src, panel_rcv)


LANES = 128
ROWS = 32
LAG_ROWS = 16
CALLS = ((0,), (3,), (2,), (1,))
VMEM = 20 * 2**20
FULL_VMEM = 56 * 2**20
TILE_ROWS = 256
COST = 10**6
F32 = jnp.float32
BF16 = jnp.bfloat16
SIN = [(-1) ** n * (math.pi / 2) ** (2 * n + 1) / math.factorial(2 * n + 1) for n in range(5)]
COS = [(-1) ** n * (math.pi / 2) ** (2 * n) / math.factorial(2 * n) for n in range(6)]


def horner(coefs, v):
    total = coefs[-1]
    for coef in coefs[-2::-1]:
        total = coef + v * total
    return total


def phases(lag, freq, period):
    turns = lag * freq * (1.0 / period)
    quarters = 4.0 * (turns - jnp.floor(turns))
    near = jnp.floor(quarters + 0.5)
    u = quarters - near
    v = u * u
    s = u * horner(SIN, v)
    c = horner(COS, v)
    odd = (near == 1.0) | (near == 3.0)
    cos = jnp.where(odd, s, c)
    sin = jnp.where(odd, c, s)
    cos = jnp.where((near == 1.0) | (near == 2.0), -cos, cos)
    sin = jnp.where((near == 2.0) | (near == 3.0), -sin, sin)
    return cos, sin


def lanes_of(rows):
    return lax.broadcasted_iota(jnp.int32, (rows, LANES), 1)


class Sizes:
    def __init__(self, shapes, n_src, n_rcv):
        src_spec, rcv_spec, lag_table = shapes
        self.n_src, self.n_rcv, self.n_dev = n_src, n_rcv, n_src * n_rcv
        self.n_slow, self.n_pos = lag_table
        self.n_win = src_spec[1]
        self.src_freq, self.src_dev = src_spec[2:]
        self.rcv_freq, self.rcv_dev = rcv_spec[2:]
        self.n_freq = self.rcv_freq * n_src
        self.own = self.n_freq // self.n_dev
        self.s_all, self.r_all = self.src_dev * n_src, self.rcv_dev * n_rcv
        self.src_part = self.src_dev // n_rcv
        self.low = n_src // n_rcv
        self.chunk = self.own // 2 * ROWS

    def fits(self):
        return (
            2 * self.n_win == ROWS
            and 2 * self.n_slow == ROWS
            and self.n_win == WIN * SEGS
            and self.n_rcv == 4
            and self.own == 8
            and self.own // 2 * ROWS == LANES
            and self.src_freq == self.low * self.n_rcv * self.own
            and self.rcv_freq == self.n_rcv * self.own
            and self.n_dev * self.own == self.n_freq == 2 * LANES
            and 2 * self.src_dev == LANES
            and self.n_src % 2 == 0
            and self.rcv_dev == 2 * LANES
            and self.src_part * self.own == LANES
            and LANES % self.n_dev == 0
            and self.n_pos % LANES == 0
        )


def look_up(lag_ref, pos_ref, begin, count, offset):
    lane = lanes_of(LAG_ROWS)
    acc = jnp.zeros((LAG_ROWS, LANES), jnp.int32)
    for n in range(count):
        pos = pos_ref[begin + n]
        base = pl.multiple_of((pos // LANES) * LANES, LANES)
        tile = lag_ref[:, pl.ds(base, LANES)]
        acc = jnp.where(lane == n, pltpu.roll(tile, (n - pos) & (LANES - 1), 1), acc)
    return (acc - offset).astype(F32)


def whole(*shape):
    return pl.BlockSpec(shape, lambda *_: (0,) * len(shape))


def pack_sources(z):
    def kernel(pos_ref, src_ref, lag_ref, out_ref, flat):
        lags = look_up(lag_ref, pos_ref, 0, z.src_dev, z.n_freq)[:, :z.src_dev]
        lags = jnp.concatenate([lags[:LAG_ROWS // 2], lags[LAG_ROWS // 2:]], 1).astype(BF16)
        for row in range(ROWS):
            flat[row * z.src_freq:(row + 1) * z.src_freq, :z.src_dev] = src_ref[row].astype(F32)
        half = z.own // 2
        for rcv in range(z.n_rcv):
            for low in range(z.low):
                for group in range(2):
                    freq = (low * z.n_rcv + rcv) * z.own + group * half
                    tiles = [flat[pl.ds(freq + m, ROWS, stride=z.src_freq), :] for m in range(half)]
                    turned = jnp.transpose(jnp.concatenate(tiles, 0))[:z.src_dev]
                    out_ref[rcv, low, group * z.src_dev:(group + 1) * z.src_dev, :] = turned.astype(BF16)
                out_ref[rcv, low, z.chunk:, :] = lags

    shape = (z.n_rcv, z.low, z.chunk + LAG_ROWS // 2, LANES)
    return pl.pallas_call(
        kernel,
        grid=(1,),
        in_specs=[
            pl.BlockSpec(memory_space=pltpu.SMEM),
            whole(ROWS, z.src_freq, z.src_dev),
            whole(z.n_slow, z.n_pos),
        ],
        out_specs=whole(*shape),
        out_shape=jax.ShapeDtypeStruct(shape, BF16),
        scratch_shapes=[pltpu.VMEM((ROWS * z.src_freq, LANES), F32)],
        compiler_params=pltpu.CompilerParams(vmem_limit_bytes=FULL_VMEM),
        cost_estimate=pl.CostEstimate(flops=10**6, bytes_accessed=2 * 10**6, transcendentals=0),
        name="pack_sources",
    )


def pack_receivers(z):
    def kernel(pos_ref, rcv_ref, lag_ref, *refs):
        outs, flat = refs[:z.n_rcv], refs[z.n_rcv:]
        spans = range(0, z.rcv_dev, LANES)
        lags = [look_up(lag_ref, pos_ref, span, LANES, z.n_freq).astype(BF16) for span in spans]
        for row in range(ROWS):
            here = rcv_ref[row].astype(F32)
            for n, span in enumerate(spans):
                flat[n][row * z.rcv_freq:(row + 1) * z.rcv_freq, :] = here[:, span:span + LANES]
        for other in range(z.n_rcv):
            first = (lax.axis_index("rcv") ^ other) * z.own
            for n, span in enumerate(spans):
                for k in range(z.own):
                    tile = flat[n][pl.ds(first + k, ROWS, stride=z.rcv_freq), :]
                    outs[other][k * ROWS:(k + 1) * ROWS, span:span + LANES] = tile.astype(BF16)
                outs[other][z.own * ROWS:, span:span + LANES] = lags[n]

    shape = (z.own * ROWS + LAG_ROWS, z.rcv_dev)
    return pl.pallas_call(
        kernel,
        grid=(1,),
        in_specs=[
            pl.BlockSpec(memory_space=pltpu.SMEM),
            whole(ROWS, z.rcv_freq, z.rcv_dev),
            whole(z.n_slow, z.n_pos),
        ],
        out_specs=[whole(*shape)] * z.n_rcv,
        out_shape=[jax.ShapeDtypeStruct(shape, BF16)] * z.n_rcv,
        scratch_shapes=[pltpu.VMEM((ROWS * z.rcv_freq, LANES), F32)] * (z.rcv_dev // LANES),
        compiler_params=pltpu.CompilerParams(vmem_limit_bytes=VMEM),
        cost_estimate=pl.CostEstimate(flops=10**6, bytes_accessed=2 * 10**6, transcendentals=0),
        name="pack_receivers",
    )


def cross_spectra(z, src_ref, rcv_refs, turn, right, stack):
    half = z.own // 2
    group, place = divmod(turn, half)
    begin = place * ROWS
    rows = slice(turn * ROWS, (turn + 1) * ROWS)
    spec = jnp.concatenate([ref[rows, :] for ref in rcv_refs], 1).astype(F32)
    turned = jnp.concatenate([-spec[z.n_win:], spec[:z.n_win]], 0)
    window = lax.broadcasted_iota(jnp.int32, (ROWS, 1), 0) % z.n_win
    for seg in range(SEGS):
        here = window // WIN == seg
        right[seg, begin:begin + ROWS, :] = jnp.where(here, spec, 0.0).astype(BF16)
        right[SEGS + seg, begin:begin + ROWS, :] = jnp.where(here, turned, 0.0).astype(BF16)
    width, height = 2 * LANES, TILE_ROWS
    r_now = spec.shape[1]
    for col in range(0, r_now, width):
        for row in range(0, z.s_all, height):
            senders = range(row // z.src_dev, (row + height) // z.src_dev)
            lines = slice(group * z.src_dev, (group + 1) * z.src_dev)
            part = jnp.concatenate([src_ref[sender, lines, :] for sender in senders], 0)
            total_re, total_im = 0.0, 0.0
            for seg in range(SEGS):
                real = jnp.dot(part, right[seg, :, col:col + width], preferred_element_type=F32)
                imag = jnp.dot(part, right[SEGS + seg, :, col:col + width], preferred_element_type=F32)
                scale = lax.rsqrt(jnp.maximum(real * real + imag * imag, 1.0))
                total_re, total_im = total_re + real * scale, total_im + imag * scale
            stack[row:row + height, col:col + width] = total_re.astype(BF16)
            stack[z.s_all + row:z.s_all + row + height, col:col + width] = total_im.astype(BF16)


def compute(z, count, first, last):
    src_factor = 1.0 / (SEGS * math.sqrt(z.r_all))
    rcv_factor = 1.0 / (SEGS * math.sqrt(z.s_all))
    n = z.n_slow
    r_now = count * z.rcv_dev
    place_lag = z.own * ROWS

    def kernel(src_ref, *refs):
        rcv_refs, refs = refs[:count], refs[count:]
        if not first:
            before_ref, refs = refs[0], refs[1:]
        out_refs, refs = refs[:count], refs[count:]
        sum_ref, lag, waves, right, stack = refs[:5]
        right[...] = jnp.zeros_like(right)
        for src in range(z.n_src):
            lags = src_ref[src, z.chunk:, :].astype(F32) + float(z.n_freq)
            for part in range(2):
                rows = slice(part * LAG_ROWS // 2, (part + 1) * LAG_ROWS // 2)
                lanes = slice(part * z.src_dev, (part + 1) * z.src_dev)
                lag[rows, src * z.src_dev:(src + 1) * z.src_dev] = lags[:, lanes]
        for block, ref in enumerate(rcv_refs):
            place = z.s_all + block * z.rcv_dev
            lag[:, place:place + z.rcv_dev] = ref[place_lag:, :].astype(F32) + float(z.n_freq)
        begin = lax.axis_index("src") * z.rcv_freq + lax.axis_index("rcv") * z.own
        waves[0], waves[1] = phases(lag[...], begin.astype(F32), 2.0 * z.n_freq)
        waves[2], waves[3] = phases(lag[...], 1.0, 2.0 * z.n_freq)

        def next_waves():
            cos, sin = waves[0], waves[1]
            step_cos, step_sin = waves[2], waves[3]
            waves[0], waves[1] = cos * step_cos - sin * step_sin, sin * step_cos + cos * step_sin
            return cos[:, :z.s_all], sin[:, :z.s_all], cos[:, z.s_all:], sin[:, z.s_all:]

        def cross(turn, slot):
            cross_spectra(z, src_ref, rcv_refs, turn, right.at[turn % (z.own // 2)], stack.at[slot])

        def slant(turn, slot):
            src_cos, src_sin, rcv_cos, rcv_sin = next_waves()
            upper = jnp.concatenate([src_cos, src_sin], 1)
            lower = jnp.concatenate([-src_sin, src_cos], 1)
            both = jnp.concatenate([upper, lower], 0).astype(BF16)
            over_src = jnp.dot(both, stack[slot], preferred_element_type=F32) * rcv_factor
            over_re, over_im = over_src[:n], over_src[n:]
            panel_re = over_re * rcv_cos - over_im * rcv_sin
            panel_im = over_re * rcv_sin + over_im * rcv_cos
            panel = jnp.concatenate([panel_re, panel_im], 0).astype(BF16)
            for block, ref in enumerate(out_refs):
                ref[turn] = panel[:, block * z.rcv_dev:(block + 1) * z.rcv_dev]
            dims = (((1,), (1,)), ((), ()))
            with_re = jnp.concatenate([rcv_cos, rcv_sin], 0).astype(BF16)
            with_im = jnp.concatenate([-rcv_sin, rcv_cos], 0).astype(BF16)
            over_rcv = lax.dot_general(with_re, stack[slot, :z.s_all, :], dims, preferred_element_type=F32)
            over_rcv += lax.dot_general(with_im, stack[slot, z.s_all:, :], dims, preferred_element_type=F32)
            if not first:
                over_rcv += before_ref[turn]
            if not last:
                sum_ref[turn] = over_rcv
                return
            over_rcv *= src_factor
            over_re, over_im = over_rcv[:n], over_rcv[n:]
            panel_re = over_re * src_cos + over_im * src_sin
            panel_im = over_im * src_cos - over_re * src_sin
            refs[5][turn] = jnp.concatenate([panel_re, panel_im], 0)

        cross(0, 0)
        for turn in range(1, z.own):
            cross(turn, turn % 2)
            slant(turn - 1, (turn - 1) % 2)
        slant(z.own - 1, (z.own - 1) % 2)
        if last:
            send_sources(z, refs[5], sum_ref)

    in_specs = [whole(z.n_src, z.chunk + LAG_ROWS // 2, LANES)]
    in_specs += [whole(z.own * ROWS + LAG_ROWS, z.rcv_dev)] * count
    out_specs = [whole(z.own, ROWS, z.rcv_dev)] * count
    out_shape = [jax.ShapeDtypeStruct((z.own, ROWS, z.rcv_dev), BF16)] * count
    part_spec = whole(z.own, ROWS, z.s_all)
    scratch = [
        pltpu.VMEM((n, z.s_all + r_now), F32),
        pltpu.VMEM((4, n, z.s_all + r_now), F32),
        pltpu.VMEM((z.own // 2, 2 * SEGS, LANES, r_now), BF16),
        pltpu.VMEM((2, 2 * z.s_all, r_now), BF16),
    ]
    if not first:
        in_specs.append(part_spec)
    if last:
        out_specs.append(whole(z.n_dev, ROWS, LANES))
        out_shape.append(jax.ShapeDtypeStruct((z.n_dev, ROWS, LANES), BF16))
        scratch.append(pltpu.VMEM((z.own, ROWS, z.s_all), F32))
    else:
        out_specs.append(part_spec)
        out_shape.append(jax.ShapeDtypeStruct((z.own, ROWS, z.s_all), F32))
    return pl.pallas_call(
        kernel,
        grid=(1,),
        in_specs=in_specs,
        out_specs=out_specs,
        out_shape=out_shape,
        scratch_shapes=scratch,
        compiler_params=pltpu.CompilerParams(vmem_limit_bytes=VMEM),
        cost_estimate=pl.CostEstimate(flops=COST * count, bytes_accessed=10**6, transcendentals=0),
        name="compute_first" if first else "compute_last" if last else "compute_next",
    )


def send_sources(z, sums, out_ref):
    lane = lanes_of(ROWS)
    for block in range(z.s_all // LANES):
        tiles = [sums[k, :, block * LANES:(block + 1) * LANES] for k in range(z.own)]
        bit = 1
        while bit < z.own:
            shift = bit * z.src_part
            upper = lane & shift != 0
            for k in range(z.own):
                if not k & bit:
                    one, two = tiles[k], tiles[k | bit]
                    tiles[k] = jnp.where(upper, pltpu.roll(two, shift, 1), one)
                    tiles[k | bit] = jnp.where(upper, two, pltpu.roll(one, LANES - shift, 1))
            bit *= 2
        for group in range(z.own):
            out_ref[block * z.own + group] = tiles[group].astype(BF16)


def unpack_block(z, in_ref, flat, write):
    n = z.n_slow
    for span in range(0, z.rcv_dev, LANES):
        for k in range(z.own):
            flat[k * ROWS:(k + 1) * ROWS, :] = in_ref[k, :, span:span + LANES].astype(F32)
        for slow in range(n):
            for part in range(2):
                write(2 * slow + part, span, flat[pl.ds(part * n + slow, z.own, stride=ROWS), :])


def unpack_first(z, others):
    def kernel(*refs):
        in_refs, out_ref, flat = refs[:len(others)], refs[-2], refs[-1]
        for other, in_ref in zip(others, in_refs):
            rows = pl.ds(pl.multiple_of((lax.axis_index("rcv") ^ other) * z.own, z.own), z.own)

            def write(index, span, tile):
                out_ref[index, rows, span:span + LANES] = tile

            unpack_block(z, in_ref, flat, write)

    return pl.pallas_call(
        kernel,
        grid=(1,),
        in_specs=[whole(z.own, ROWS, z.rcv_dev)] * len(others),
        out_specs=whole(ROWS, z.rcv_freq, z.rcv_dev),
        out_shape=jax.ShapeDtypeStruct((ROWS, z.rcv_freq, z.rcv_dev), F32),
        scratch_shapes=[pltpu.VMEM((z.own * ROWS, LANES), F32)],
        compiler_params=pltpu.CompilerParams(vmem_limit_bytes=VMEM),
        cost_estimate=pl.CostEstimate(flops=10**6, bytes_accessed=10**6, transcendentals=0),
        name="unpack_first",
    )


def unpack_last(z, other):
    n = z.n_slow
    group = LANES // z.n_dev
    width = z.src_part

    def kernel(rcv_in, src_in, held_ref, rcv_ref, src_ref, flat, small, table):
        del held_ref

        def write(index, span, tile):
            rcv_ref[index, :, span:span + LANES] = tile

        unpack_block(z, rcv_in, small, write)
        for dev in range(z.n_dev):
            flat[dev * ROWS:(dev + 1) * ROWS, :] = src_in[dev].astype(F32)
        lane = lanes_of(width)
        for first in range(0, ROWS, group):
            tiles = [flat[pl.ds(first + j, z.n_dev, stride=ROWS), :] for j in range(group)]
            turned = jnp.transpose(jnp.concatenate(tiles, 0))
            for j in range(group):
                for block in range(z.own // group):
                    total = jnp.zeros((width, LANES), F32)
                    for k in range(group):
                        row = (block * group + k) * width
                        tile = turned[row:row + width, :]
                        shift = (k - j) * z.n_dev % LANES
                        moved = pltpu.roll(tile, shift, 1) if shift else tile
                        total = jnp.where((lane >= k * z.n_dev) & (lane < (k + 1) * z.n_dev), moved, total)
                    rows = slice((first + j) * width, (first + j + 1) * width)
                    table[rows, block * LANES:(block + 1) * LANES] = total.astype(BF16)
        here = lax.broadcasted_iota(jnp.int32, (z.n_freq, z.n_freq), 0)
        there = lax.broadcasted_iota(jnp.int32, (z.n_freq, z.n_freq), 1)
        order = (there == here % z.n_dev * z.own + here // z.n_dev).astype(F32).astype(BF16)
        for index in range(ROWS):
            part, slow = divmod(index, n)
            rows = table[index * width:(index + 1) * width, :]
            src_ref[2 * slow + part] = jnp.dot(rows, order, preferred_element_type=F32)

    return pl.pallas_call(
        kernel,
        grid=(1,),
        in_specs=[
            whole(z.own, ROWS, z.rcv_dev),
            whole(z.n_dev, ROWS, LANES),
            pl.BlockSpec(memory_space=pl.ANY),
        ],
        out_specs=[
            pl.BlockSpec((ROWS, z.own, z.rcv_dev), lambda k: (0, lax.axis_index("rcv") ^ other, 0)),
            whole(ROWS, width, z.n_freq),
        ],
        scratch_shapes=[
            pltpu.VMEM((z.n_dev * ROWS, LANES), F32),
            pltpu.VMEM((z.own * ROWS, LANES), F32),
            pltpu.VMEM((ROWS * width, z.n_freq), BF16),
        ],
        out_shape=[
            jax.ShapeDtypeStruct((ROWS, z.rcv_freq, z.rcv_dev), F32),
            jax.ShapeDtypeStruct((ROWS, width, z.n_freq), F32),
        ],
        input_output_aliases={2: 0},
        compiler_params=pltpu.CompilerParams(vmem_limit_bytes=VMEM),
        cost_estimate=pl.CostEstimate(flops=10**6, bytes_accessed=2 * 10**6, transcendentals=0),
        name="unpack_last",
    )


def swap(z, block, other):
    if other == 0:
        return block
    return lax.ppermute(block, "rcv", [(j, j ^ other) for j in range(z.n_rcv)])


def arrive(done, others, values):
    here, values = lax.optimization_barrier(([done[other] for other in others], values))
    done.update(zip(others, here))
    return values


def per_device(src_spec, rcv_spec, lag_table, src_pos, rcv_pos):
    n_src, n_rcv = lax.axis_size("src"), lax.axis_size("rcv")
    z = Sizes((src_spec.shape, rcv_spec.shape, lag_table.shape), n_src, n_rcv)
    if not z.fits():
        return per_device_general(src_spec, rcv_spec, lag_table, src_pos, rcv_pos)
    src_rows = src_spec.reshape(ROWS, z.src_freq, z.src_dev)
    rcv_rows = rcv_spec.reshape(ROWS, z.rcv_freq, z.rcv_dev)
    spread = lax.all_to_all(pack_sources(z)(src_pos, src_rows, lag_table), "rcv", 0, 0, tiled=True)
    packed = pack_receivers(z)(rcv_pos, rcv_rows, lag_table)
    spread, packed = lax.optimization_barrier((spread, packed))
    spread = spread.reshape(z.n_src, z.chunk + LAG_ROWS // 2, LANES)
    sources = lax.all_to_all(spread, "src", 0, 0, tiled=True)
    blocks = {other: swap(z, packed[other], other) for others in CALLS for other in others}
    done, carry = {}, ()
    for n, others in enumerate(CALLS):
        ready = [blocks[other] for other in others]
        if n >= 2:
            ready, carry = arrive(done, CALLS[n - 2], (ready, carry))
        call = compute(z, len(others), n == 0, n == len(CALLS) - 1)
        *panels, total = call(sources, *ready, *carry)
        done.update({other: swap(z, panel, other) for other, panel in zip(others, panels)})
        carry = (total,)
    total = arrive(done, CALLS[-2], total)
    got_src = lax.all_to_all(total, ("src", "rcv"), 0, 0, tiled=True)
    late = CALLS[-1][0]
    early = tuple(other for other in done if other != late)
    held = unpack_first(z, early)(*(done[other] for other in early))
    panel_rcv, panel_src = unpack_last(z, late)(done[late], got_src, held)
    return (
        panel_src.reshape(z.n_slow, 2, z.src_part, z.n_freq),
        panel_rcv.reshape(z.n_slow, 2, z.rcv_freq, z.rcv_dev),
    )


def solution(mesh):
    placed = (P(None, None, "rcv", "src"), P(None, None, "src", "rcv"), P(), P("src"), P("rcv"))
    return jax.shard_map(
        per_device,
        mesh=mesh,
        in_specs=placed,
        out_specs=(P(None, None, ("src", "rcv"), None), P(None, None, "src", "rcv")),
        check_vma=False,
    )
```

```python
import math

import jax
import jax.numpy as jnp
from jax import lax
from jax.experimental import pallas as pl
from jax.experimental.pallas import tpu as pltpu
from jax.sharding import PartitionSpec as P

WIN = 8
SEGS = 2


def phase_table(freqs, lags, n_freq):
    index_mod = freqs[:, None, None] * jnp.transpose(lags)[None, :, :] % (2 * n_freq)
    angles = index_mod.astype(jnp.float32) * (math.pi / n_freq)
    return (jnp.cos(angles), jnp.sin(angles))


def cross_block(src_block, rcv_block):
    block_width = src_block.shape[2]
    src_five = src_block.reshape(2, SEGS, WIN, block_width, src_block.shape[3])
    rcv_five = rcv_block.reshape(2, SEGS, WIN, block_width, rcv_block.shape[3])
    swapped = jnp.stack([src_five[1], -src_five[0]])
    real_part = jnp.einsum(
        "cgwfs,cgwfr->gfsr", src_five, rcv_five, preferred_element_type=jnp.float32
    )
    imag_part = jnp.einsum(
        "cgwfs,cgwfr->gfsr", swapped, rcv_five, preferred_element_type=jnp.float32
    )
    floor_mod = jnp.maximum(jnp.sqrt(real_part * real_part + imag_part * imag_part), 1.0)
    stacked_re = (jnp.sum(real_part / floor_mod, axis=0) / SEGS).astype(jnp.bfloat16)
    stacked_im = (jnp.sum(imag_part / floor_mod, axis=0) / SEGS).astype(jnp.bfloat16)
    return (stacked_re, stacked_im)


def source_slant(stacked_re, stacked_im, rcv_cos, rcv_sin, src_cos, src_sin, factor):
    left_op = jnp.concatenate([stacked_re, stacked_im], axis=2)
    cos_b = rcv_cos.astype(jnp.bfloat16)
    sin_b = rcv_sin.astype(jnp.bfloat16)
    upper_half = jnp.concatenate([cos_b, sin_b], axis=2)
    bottom = jnp.concatenate([-sin_b, cos_b], axis=2)
    right_op = jnp.concatenate([upper_half, bottom], axis=1)
    sums = jnp.einsum("fsk,fkq->fsq", left_op, right_op, preferred_element_type=jnp.float32)
    n_slow = rcv_cos.shape[2]
    sum_re = sums[:, :, :n_slow]
    sum_im = sums[:, :, n_slow:]
    panel_re = (sum_re * src_cos + sum_im * src_sin) * factor
    panel_im = (sum_im * src_cos - sum_re * src_sin) * factor
    return jnp.transpose(jnp.stack([panel_re, panel_im]), (3, 0, 2, 1))


def receiver_right(src_cos_b, src_sin_b):
    upper_half = jnp.concatenate([src_cos_b, -src_sin_b], axis=2)
    bottom = jnp.concatenate([src_sin_b, src_cos_b], axis=2)
    return jnp.concatenate([upper_half, bottom], axis=1)


def receiver_sums(left_op, right_op):
    return jnp.einsum("fkr,fkq->fqr", left_op, right_op, preferred_element_type=jnp.float32)


def receiver_outer(sums, rcv_cos, rcv_sin, factor):
    n_slow = rcv_cos.shape[2]
    cos_t = jnp.transpose(rcv_cos, (0, 2, 1))
    sin_t = jnp.transpose(rcv_sin, (0, 2, 1))
    sum_re = sums[:, :n_slow, :]
    sum_im = sums[:, n_slow:, :]
    panel_re = (sum_re * cos_t - sum_im * sin_t) * factor
    panel_im = (sum_re * sin_t + sum_im * cos_t) * factor
    return jnp.transpose(jnp.stack([panel_re, panel_im]), (2, 0, 1, 3))


def per_device_general(src_spec, rcv_spec, lag_table, src_pos, rcv_pos):
    src_full = lax.all_gather(src_spec, "rcv", axis=2, tiled=True)
    n_freq = src_full.shape[2]
    src_dev = src_full.shape[3]
    rcv_dev = rcv_spec.shape[3]
    n_slow = lag_table.shape[0]
    n_src = lax.axis_size("src")
    n_rcv = lax.axis_size("rcv")
    src_factor = 1.0 / math.sqrt(rcv_dev * n_rcv)
    rcv_factor = 1.0 / math.sqrt(src_dev * n_src)
    lag_src = jnp.take(lag_table, src_pos, axis=1)
    lag_rcv = jnp.take(lag_table, rcv_pos, axis=1)
    src_init = jnp.zeros((n_slow, 2, src_dev, n_freq), jnp.float32)
    other_init = jnp.zeros((n_slow, 2, n_freq, rcv_dev), jnp.float32)
    shard_piece = lax.all_gather(rcv_spec, "src", axis=2, tiled=True)
    block_width = math.gcd(shard_piece.shape[2], 16)

    def inner(turn_index, totals):
        offset = turn_index * block_width
        freqs = offset + jnp.arange(block_width, dtype=jnp.int32)
        src_block = lax.dynamic_slice_in_dim(src_full, offset, block_width, 2)
        rcv_block = lax.dynamic_slice_in_dim(shard_piece, offset, block_width, 2)
        stacked_re, stacked_im = cross_block(src_block, rcv_block)
        rcv_cos, rcv_sin = phase_table(freqs, lag_rcv, n_freq)
        src_cos, src_sin = phase_table(freqs, lag_src, n_freq)
        src_part = source_slant(
            stacked_re, stacked_im, rcv_cos, rcv_sin, src_cos, src_sin, src_factor
        )
        src_total = lax.dynamic_update_slice_in_dim(totals[0], src_part, offset, 3)
        left_op = jnp.concatenate([stacked_re, stacked_im], axis=1)
        right_op = receiver_right(src_cos.astype(jnp.bfloat16), src_sin.astype(jnp.bfloat16))
        rcv_part = receiver_outer(receiver_sums(left_op, right_op), rcv_cos, rcv_sin, rcv_factor)
        other = lax.dynamic_update_slice_in_dim(totals[1], rcv_part, offset, 2)
        return (src_total, other)

    src_total, other = lax.fori_loop(
        0, shard_piece.shape[2] // block_width, inner, (src_init, other_init)
    )
    panel_src = lax.psum_scatter(src_total, "rcv", scatter_dimension=2, tiled=True)
    panel_rcv = lax.psum_scatter(other, "src", scatter_dimension=2, tiled=True)
    return (panel_src, panel_rcv)


LANES = 128
ROWS = 32
LAG_ROWS = 16
CALLS = ((0,), (3,), (2,), (1,))
VMEM = 20 * 2**20
FULL_VMEM = 56 * 2**20
TILE_ROWS = 256
COST = 10**6
F32 = jnp.float32
BF16 = jnp.bfloat16
SIN = [(-1) ** n * (math.pi / 2) ** (2 * n + 1) / math.factorial(2 * n + 1) for n in range(5)]
COS = [(-1) ** n * (math.pi / 2) ** (2 * n) / math.factorial(2 * n) for n in range(6)]


def horner(coefs, v):
    total = coefs[-1]
    for coef in coefs[-2::-1]:
        total = coef + v * total
    return total


def phases(lag, freq, period):
    turns = lag * freq * (1.0 / period)
    quarters = 4.0 * (turns - jnp.floor(turns))
    near = jnp.floor(quarters + 0.5)
    u = quarters - near
    v = u * u
    s = u * horner(SIN, v)
    c = horner(COS, v)
    odd = (near == 1.0) | (near == 3.0)
    cos = jnp.where(odd, s, c)
    sin = jnp.where(odd, c, s)
    cos = jnp.where((near == 1.0) | (near == 2.0), -cos, cos)
    sin = jnp.where((near == 2.0) | (near == 3.0), -sin, sin)
    return cos, sin


def lanes_of(rows):
    return lax.broadcasted_iota(jnp.int32, (rows, LANES), 1)


class Sizes:
    def __init__(self, shapes, n_src, n_rcv):
        src_spec, rcv_spec, lag_table = shapes
        self.n_src, self.n_rcv, self.n_dev = n_src, n_rcv, n_src * n_rcv
        self.n_slow, self.n_pos = lag_table
        self.n_win = src_spec[1]
        self.src_freq, self.src_dev = src_spec[2:]
        self.rcv_freq, self.rcv_dev = rcv_spec[2:]
        self.n_freq = self.rcv_freq * n_src
        self.own = self.n_freq // self.n_dev
        self.s_all, self.r_all = self.src_dev * n_src, self.rcv_dev * n_rcv
        self.src_part = self.src_dev // n_rcv
        self.low = n_src // n_rcv
        self.chunk = self.own // 2 * ROWS

    def fits(self):
        return (
            2 * self.n_win == ROWS
            and 2 * self.n_slow == ROWS
            and self.n_win == WIN * SEGS
            and self.n_rcv == 4
            and self.own == 8
            and self.own // 2 * ROWS == LANES
            and self.src_freq == self.low * self.n_rcv * self.own
            and self.rcv_freq == self.n_rcv * self.own
            and self.n_dev * self.own == self.n_freq == 2 * LANES
            and 2 * self.src_dev == LANES
            and self.n_src % 2 == 0
            and self.rcv_dev == 2 * LANES
            and self.src_part * self.own == LANES
            and LANES % self.n_dev == 0
            and self.n_pos % LANES == 0
        )


def look_up(z, table, pos_ref):
    pos = pos_ref[...]
    lane = lax.broadcasted_iota(jnp.int32, (LANES, pos.shape[1]), 0)
    spot = (lane == pos % LANES).astype(F32).astype(BF16)
    found = jnp.dot(table, spot, preferred_element_type=F32)
    total = 0.0
    for block in range(z.n_pos // LANES):
        total += jnp.where(pos // LANES == block, found[block * z.n_slow:(block + 1) * z.n_slow], 0.0)
    return total


def whole(*shape):
    return pl.BlockSpec(shape, lambda *_: (0,) * len(shape))


def pack_sources(z):
    def kernel(src_ref, *refs):
        outs, flat = refs[:z.n_rcv], refs[z.n_rcv]
        for row in range(ROWS):
            flat[row * z.src_freq:(row + 1) * z.src_freq, :z.src_dev] = src_ref[row].astype(F32)
        half = z.own // 2
        for other in range(z.n_rcv):
            rcv = lax.axis_index("rcv") ^ other
            for low in range(z.low):
                for group in range(2):
                    freq = (low * z.n_rcv + rcv) * z.own + group * half
                    tiles = [flat[pl.ds(freq + m, ROWS, stride=z.src_freq), :] for m in range(half)]
                    turned = jnp.transpose(jnp.concatenate(tiles, 0))[:z.src_dev]
                    outs[other][low, group * z.src_dev:(group + 1) * z.src_dev, :] = turned.astype(BF16)

    shape = (z.low, z.chunk, LANES)
    return pl.pallas_call(
        kernel,
        grid=(1,),
        in_specs=[whole(ROWS, z.src_freq, z.src_dev)],
        out_specs=[whole(*shape)] * z.n_rcv,
        out_shape=[jax.ShapeDtypeStruct(shape, BF16)] * z.n_rcv,
        scratch_shapes=[pltpu.VMEM((ROWS * z.src_freq, LANES), F32)],
        compiler_params=pltpu.CompilerParams(vmem_limit_bytes=FULL_VMEM),
        cost_estimate=pl.CostEstimate(flops=10**6, bytes_accessed=2 * 10**6, transcendentals=0),
        name="pack_sources",
    )


def order_sources(z):
    def kernel(lag_ref, *refs):
        out_ref = refs[-1]
        for other in range(z.n_rcv):
            place = lax.axis_index("rcv") ^ other
            out_ref[pl.ds(place * z.low, z.low), :z.chunk, :] = refs[other][...]
        for place in range(z.n_src):
            out_ref[place, z.chunk:, :] = lag_ref[...]

    shape = (z.chunk + LAG_ROWS // 2, LANES)
    return pl.pallas_call(
        kernel,
        grid=(1,),
        in_specs=[whole(LAG_ROWS // 2, LANES)] + [whole(z.low, z.chunk, LANES)] * z.n_rcv,
        out_specs=whole(z.n_src, *shape),
        out_shape=jax.ShapeDtypeStruct((z.n_src, *shape), BF16),
        compiler_params=pltpu.CompilerParams(vmem_limit_bytes=VMEM),
        cost_estimate=pl.CostEstimate(flops=10**6, bytes_accessed=10**6, transcendentals=0),
        name="order_sources",
    )


def pack_receivers(z):
    def kernel(pos_ref, src_pos_ref, rcv_ref, lag_ref, *refs):
        outs, src_out, flat = refs[:z.n_rcv], refs[z.n_rcv], refs[z.n_rcv + 1:]
        blocks = [lag_ref[:, place:place + LANES] for place in range(0, z.n_pos, LANES)]
        table = (jnp.concatenate(blocks, 0) - z.n_freq).astype(F32).astype(BF16)
        src_lags = look_up(z, table, src_pos_ref)
        src_out[...] = jnp.concatenate([src_lags[:LAG_ROWS // 2], src_lags[LAG_ROWS // 2:]], 1).astype(BF16)
        spans = range(0, z.rcv_dev, LANES)
        lags = look_up(z, table, pos_ref).astype(BF16)
        for row in range(ROWS):
            here = rcv_ref[row].astype(F32)
            for n, span in enumerate(spans):
                flat[n][row * z.rcv_freq:(row + 1) * z.rcv_freq, :] = here[:, span:span + LANES]
        for other in range(z.n_rcv):
            first = (lax.axis_index("rcv") ^ other) * z.own
            for n, span in enumerate(spans):
                for k in range(z.own):
                    tile = flat[n][pl.ds(first + k, ROWS, stride=z.rcv_freq), :]
                    outs[other][k * ROWS:(k + 1) * ROWS, span:span + LANES] = tile.astype(BF16)
                outs[other][z.own * ROWS:, span:span + LANES] = lags[:, span:span + LANES]

    shape = (z.own * ROWS + LAG_ROWS, z.rcv_dev)
    return pl.pallas_call(
        kernel,
        grid=(1,),
        in_specs=[
            whole(1, z.rcv_dev),
            whole(1, z.src_dev),
            whole(ROWS, z.rcv_freq, z.rcv_dev),
            whole(z.n_slow, z.n_pos),
        ],
        out_specs=[whole(*shape)] * z.n_rcv + [whole(LAG_ROWS // 2, LANES)],
        out_shape=[jax.ShapeDtypeStruct(shape, BF16)] * z.n_rcv
        + [jax.ShapeDtypeStruct((LAG_ROWS // 2, LANES), BF16)],
        scratch_shapes=[pltpu.VMEM((ROWS * z.rcv_freq, LANES), F32)] * (z.rcv_dev // LANES),
        compiler_params=pltpu.CompilerParams(vmem_limit_bytes=VMEM),
        cost_estimate=pl.CostEstimate(flops=10**6, bytes_accessed=2 * 10**6, transcendentals=0),
        name="pack_receivers",
    )


def cross_spectra(z, src_ref, rcv_refs, turn, right, stack):
    half = z.own // 2
    group, place = divmod(turn, half)
    begin = place * ROWS
    rows = slice(turn * ROWS, (turn + 1) * ROWS)
    spec = jnp.concatenate([ref[rows, :] for ref in rcv_refs], 1).astype(F32)
    turned = jnp.concatenate([-spec[z.n_win:], spec[:z.n_win]], 0)
    window = lax.broadcasted_iota(jnp.int32, (ROWS, 1), 0) % z.n_win
    for seg in range(SEGS):
        here = window // WIN == seg
        right[seg, begin:begin + ROWS, :] = jnp.where(here, spec, 0.0).astype(BF16)
        right[SEGS + seg, begin:begin + ROWS, :] = jnp.where(here, turned, 0.0).astype(BF16)
    width, height = 2 * LANES, TILE_ROWS
    r_now = spec.shape[1]
    for col in range(0, r_now, width):
        for row in range(0, z.s_all, height):
            senders = range(row // z.src_dev, (row + height) // z.src_dev)
            lines = slice(group * z.src_dev, (group + 1) * z.src_dev)
            part = jnp.concatenate([src_ref[sender, lines, :] for sender in senders], 0)
            total_re, total_im = 0.0, 0.0
            for seg in range(SEGS):
                real = jnp.dot(part, right[seg, :, col:col + width], preferred_element_type=F32)
                imag = jnp.dot(part, right[SEGS + seg, :, col:col + width], preferred_element_type=F32)
                scale = lax.rsqrt(jnp.maximum(real * real + imag * imag, 1.0))
                total_re, total_im = total_re + real * scale, total_im + imag * scale
            stack[row:row + height, col:col + width] = total_re.astype(BF16)
            stack[z.s_all + row:z.s_all + row + height, col:col + width] = total_im.astype(BF16)


def compute(z, count, first, last):
    src_factor = 1.0 / (SEGS * math.sqrt(z.r_all))
    rcv_factor = 1.0 / (SEGS * math.sqrt(z.s_all))
    n = z.n_slow
    r_now = count * z.rcv_dev
    place_lag = z.own * ROWS

    def kernel(src_ref, *refs):
        rcv_refs, refs = refs[:count], refs[count:]
        if not first:
            before_ref, refs = refs[0], refs[1:]
        out_refs, refs = refs[:count], refs[count:]
        sum_ref, lag, waves, right, stack = refs[:5]
        right[...] = jnp.zeros_like(right)
        for src in range(z.n_src):
            lags = src_ref[src, z.chunk:, :].astype(F32) + float(z.n_freq)
            for part in range(2):
                rows = slice(part * LAG_ROWS // 2, (part + 1) * LAG_ROWS // 2)
                lanes = slice(part * z.src_dev, (part + 1) * z.src_dev)
                lag[rows, src * z.src_dev:(src + 1) * z.src_dev] = lags[:, lanes]
        for block, ref in enumerate(rcv_refs):
            place = z.s_all + block * z.rcv_dev
            lag[:, place:place + z.rcv_dev] = ref[place_lag:, :].astype(F32) + float(z.n_freq)
        begin = lax.axis_index("src") * z.rcv_freq + lax.axis_index("rcv") * z.own
        waves[0], waves[1] = phases(lag[...], begin.astype(F32), 2.0 * z.n_freq)
        waves[2], waves[3] = phases(lag[...], 1.0, 2.0 * z.n_freq)

        def next_waves():
            cos, sin = waves[0], waves[1]
            step_cos, step_sin = waves[2], waves[3]
            waves[0], waves[1] = cos * step_cos - sin * step_sin, sin * step_cos + cos * step_sin
            return cos[:, :z.s_all], sin[:, :z.s_all], cos[:, z.s_all:], sin[:, z.s_all:]

        def cross(turn, slot):
            cross_spectra(z, src_ref, rcv_refs, turn, right.at[turn % (z.own // 2)], stack.at[slot])

        def slant(turn, slot):
            src_cos, src_sin, rcv_cos, rcv_sin = next_waves()
            upper = jnp.concatenate([src_cos, src_sin], 1)
            lower = jnp.concatenate([-src_sin, src_cos], 1)
            both = jnp.concatenate([upper, lower], 0).astype(BF16)
            over_src = jnp.dot(both, stack[slot], preferred_element_type=F32) * rcv_factor
            over_re, over_im = over_src[:n], over_src[n:]
            panel_re = over_re * rcv_cos - over_im * rcv_sin
            panel_im = over_re * rcv_sin + over_im * rcv_cos
            panel = jnp.concatenate([panel_re, panel_im], 0).astype(BF16)
            for block, ref in enumerate(out_refs):
                ref[turn] = panel[:, block * z.rcv_dev:(block + 1) * z.rcv_dev]
            dims = (((1,), (1,)), ((), ()))
            with_re = jnp.concatenate([rcv_cos, rcv_sin], 0).astype(BF16)
            with_im = jnp.concatenate([-rcv_sin, rcv_cos], 0).astype(BF16)
            over_rcv = lax.dot_general(with_re, stack[slot, :z.s_all, :], dims, preferred_element_type=F32)
            over_rcv += lax.dot_general(with_im, stack[slot, z.s_all:, :], dims, preferred_element_type=F32)
            if not first:
                over_rcv += before_ref[turn]
            if not last:
                sum_ref[turn] = over_rcv
                return
            over_rcv *= src_factor
            over_re, over_im = over_rcv[:n], over_rcv[n:]
            panel_re = over_re * src_cos + over_im * src_sin
            panel_im = over_im * src_cos - over_re * src_sin
            refs[5][turn] = jnp.concatenate([panel_re, panel_im], 0)
            regroup_after(z, refs[5], turn)

        cross(0, 0)
        for turn in range(1, z.own):
            cross(turn, turn % 2)
            slant(turn - 1, (turn - 1) % 2)
        slant(z.own - 1, (z.own - 1) % 2)
        if last:
            send_sources(z, refs[5], sum_ref)

    in_specs = [whole(z.n_src, z.chunk + LAG_ROWS // 2, LANES)]
    in_specs += [whole(z.own * ROWS + LAG_ROWS, z.rcv_dev)] * count
    out_specs = [whole(z.own, ROWS, z.rcv_dev)] * count
    out_shape = [jax.ShapeDtypeStruct((z.own, ROWS, z.rcv_dev), BF16)] * count
    part_spec = whole(z.own, ROWS, z.s_all)
    scratch = [
        pltpu.VMEM((n, z.s_all + r_now), F32),
        pltpu.VMEM((4, n, z.s_all + r_now), F32),
        pltpu.VMEM((z.own // 2, 2 * SEGS, LANES, r_now), BF16),
        pltpu.VMEM((2, 2 * z.s_all, r_now), BF16),
    ]
    if not first:
        in_specs.append(part_spec)
    if last:
        out_specs.append(whole(z.n_dev, ROWS, LANES))
        out_shape.append(jax.ShapeDtypeStruct((z.n_dev, ROWS, LANES), BF16))
        scratch.append(pltpu.VMEM((z.own, ROWS, z.s_all), F32))
    else:
        out_specs.append(part_spec)
        out_shape.append(jax.ShapeDtypeStruct((z.own, ROWS, z.s_all), F32))
    return pl.pallas_call(
        kernel,
        grid=(1,),
        in_specs=in_specs,
        out_specs=out_specs,
        out_shape=out_shape,
        scratch_shapes=scratch,
        compiler_params=pltpu.CompilerParams(vmem_limit_bytes=VMEM),
        cost_estimate=pl.CostEstimate(flops=COST * count, bytes_accessed=10**6, transcendentals=0),
        name="compute_first" if first else "compute_last" if last else "compute_next",
    )


def regroup(z, sums, bit, first):
    lane = lanes_of(ROWS)
    shift = bit * z.src_part
    upper = lane & shift != 0
    for block in range(z.s_all // LANES):
        lanes = slice(block * LANES, (block + 1) * LANES)
        one, two = sums[first, :, lanes], sums[first + bit, :, lanes]
        sums[first, :, lanes] = jnp.where(upper, pltpu.roll(two, shift, 1), one)
        sums[first + bit, :, lanes] = jnp.where(upper, two, pltpu.roll(one, LANES - shift, 1))


def regroup_after(z, sums, turn):
    bit = 1
    while bit < z.own and turn & bit:
        base = turn & ~(2 * bit - 1)
        for low in range(bit):
            regroup(z, sums, bit, base + low)
        bit *= 2


def send_sources(z, sums, out_ref):
    for block in range(z.s_all // LANES):
        for group in range(z.own):
            out_ref[block * z.own + group] = sums[group, :, block * LANES:(block + 1) * LANES].astype(BF16)


def unpack_block(z, in_ref, flat, write):
    n = z.n_slow
    for span in range(0, z.rcv_dev, LANES):
        for k in range(z.own):
            flat[k * ROWS:(k + 1) * ROWS, :] = in_ref[k, :, span:span + LANES].astype(F32)
        for slow in range(n):
            for part in range(2):
                write(2 * slow + part, span, flat[pl.ds(part * n + slow, z.own, stride=ROWS), :])


def unpack_first(z, others):
    def kernel(*refs):
        in_refs, out_ref, flat = refs[:len(others)], refs[-2], refs[-1]
        for other, in_ref in zip(others, in_refs):
            rows = pl.ds(pl.multiple_of((lax.axis_index("rcv") ^ other) * z.own, z.own), z.own)

            def write(index, span, tile):
                out_ref[index, rows, span:span + LANES] = tile

            unpack_block(z, in_ref, flat, write)

    return pl.pallas_call(
        kernel,
        grid=(1,),
        in_specs=[whole(z.own, ROWS, z.rcv_dev)] * len(others),
        out_specs=whole(ROWS, z.rcv_freq, z.rcv_dev),
        out_shape=jax.ShapeDtypeStruct((ROWS, z.rcv_freq, z.rcv_dev), F32),
        scratch_shapes=[pltpu.VMEM((z.own * ROWS, LANES), F32)],
        compiler_params=pltpu.CompilerParams(vmem_limit_bytes=VMEM),
        cost_estimate=pl.CostEstimate(flops=10**6, bytes_accessed=10**6, transcendentals=0),
        name="unpack_first",
    )


def unpack_last(z, other):
    n = z.n_slow
    group = LANES // z.n_dev
    width = z.src_part

    def kernel(rcv_in, src_in, held_ref, rcv_ref, src_ref, flat, small, table):
        del held_ref

        def write(index, span, tile):
            rcv_ref[index, :, span:span + LANES] = tile

        unpack_block(z, rcv_in, small, write)
        for dev in range(z.n_dev):
            flat[dev * ROWS:(dev + 1) * ROWS, :] = src_in[dev].astype(F32)
        lane = lanes_of(width)
        for first in range(0, ROWS, group):
            tiles = [flat[pl.ds(first + j, z.n_dev, stride=ROWS), :] for j in range(group)]
            turned = jnp.transpose(jnp.concatenate(tiles, 0))
            for j in range(group):
                for block in range(z.own // group):
                    total = jnp.zeros((width, LANES), F32)
                    for k in range(group):
                        row = (block * group + k) * width
                        tile = turned[row:row + width, :]
                        shift = (k - j) * z.n_dev % LANES
                        moved = pltpu.roll(tile, shift, 1) if shift else tile
                        total = jnp.where((lane >= k * z.n_dev) & (lane < (k + 1) * z.n_dev), moved, total)
                    rows = slice((first + j) * width, (first + j + 1) * width)
                    table[rows, block * LANES:(block + 1) * LANES] = total.astype(BF16)
        here = lax.broadcasted_iota(jnp.int32, (z.n_freq, z.n_freq), 0)
        there = lax.broadcasted_iota(jnp.int32, (z.n_freq, z.n_freq), 1)
        order = (there == here % z.n_dev * z.own + here // z.n_dev).astype(F32).astype(BF16)
        ordered = jnp.dot(table[...], order, preferred_element_type=F32)
        for index in range(ROWS):
            part, slow = divmod(index, n)
            src_ref[2 * slow + part] = ordered[index * width:(index + 1) * width, :]

    return pl.pallas_call(
        kernel,
        grid=(1,),
        in_specs=[
            whole(z.own, ROWS, z.rcv_dev),
            whole(z.n_dev, ROWS, LANES),
            pl.BlockSpec(memory_space=pl.ANY),
        ],
        out_specs=[
            pl.BlockSpec((ROWS, z.own, z.rcv_dev), lambda k: (0, lax.axis_index("rcv") ^ other, 0)),
            whole(ROWS, width, z.n_freq),
        ],
        scratch_shapes=[
            pltpu.VMEM((z.n_dev * ROWS, LANES), F32),
            pltpu.VMEM((z.own * ROWS, LANES), F32),
            pltpu.VMEM((ROWS * width, z.n_freq), BF16),
        ],
        out_shape=[
            jax.ShapeDtypeStruct((ROWS, z.rcv_freq, z.rcv_dev), F32),
            jax.ShapeDtypeStruct((ROWS, width, z.n_freq), F32),
        ],
        input_output_aliases={2: 0},
        compiler_params=pltpu.CompilerParams(vmem_limit_bytes=VMEM),
        cost_estimate=pl.CostEstimate(flops=10**6, bytes_accessed=2 * 10**6, transcendentals=0),
        name="unpack_last",
    )


def swap(z, block, other):
    if other == 0:
        return block
    return lax.ppermute(block, "rcv", [(j, j ^ other) for j in range(z.n_rcv)])


def arrive(done, others, values):
    here, values = lax.optimization_barrier(([done[other] for other in others], values))
    done.update(zip(others, here))
    return values


def per_device(src_spec, rcv_spec, lag_table, src_pos, rcv_pos):
    n_src, n_rcv = lax.axis_size("src"), lax.axis_size("rcv")
    z = Sizes((src_spec.shape, rcv_spec.shape, lag_table.shape), n_src, n_rcv)
    if not z.fits():
        return per_device_general(src_spec, rcv_spec, lag_table, src_pos, rcv_pos)
    src_rows = src_spec.reshape(ROWS, z.src_freq, z.src_dev)
    rcv_rows = rcv_spec.reshape(ROWS, z.rcv_freq, z.rcv_dev)
    parts = pack_sources(z)(src_rows)
    moved = {other: swap(z, parts[other], other) for other in (3, 2, 1, 0)}
    *packed, src_lags = pack_receivers(z)(rcv_pos[None], src_pos[None], rcv_rows, lag_table)
    moved, packed, src_lags = lax.optimization_barrier((moved, packed, src_lags))
    spread = order_sources(z)(src_lags, *(moved[other] for other in range(z.n_rcv)))
    sources = lax.all_to_all(spread, "src", 0, 0, tiled=True)
    blocks = {other: swap(z, packed[other], other) for others in CALLS for other in others}
    done, carry = {}, ()
    for n, others in enumerate(CALLS):
        ready = [blocks[other] for other in others]
        if n >= 2:
            ready, carry = arrive(done, CALLS[n - 2], (ready, carry))
        call = compute(z, len(others), n == 0, n == len(CALLS) - 1)
        *panels, total = call(sources, *ready, *carry)
        done.update({other: swap(z, panel, other) for other, panel in zip(others, panels)})
        carry = (total,)
    total = arrive(done, CALLS[-2], total)
    got_src = lax.all_to_all(total, ("src", "rcv"), 0, 0, tiled=True)
    late = CALLS[-1][0]
    early = tuple(other for other in done if other != late)
    held = unpack_first(z, early)(*(done[other] for other in early))
    panel_rcv, panel_src = unpack_last(z, late)(done[late], got_src, held)
    return (
        panel_src.reshape(z.n_slow, 2, z.src_part, z.n_freq),
        panel_rcv.reshape(z.n_slow, 2, z.rcv_freq, z.rcv_dev),
    )


def solution(mesh):
    placed = (P(None, None, "rcv", "src"), P(None, None, "src", "rcv"), P(), P("src"), P("rcv"))
    return jax.shard_map(
        per_device,
        mesh=mesh,
        in_specs=placed,
        out_specs=(P(None, None, ("src", "rcv"), None), P(None, None, "src", "rcv")),
        check_vma=False,
    )
```

```python
import math

import jax
import jax.numpy as jnp
from jax import lax
from jax.experimental import pallas as pl
from jax.experimental.pallas import tpu as pltpu
from jax.sharding import PartitionSpec as P

WIN = 8
SEGS = 2


def phase_table(freqs, lags, n_freq):
    index_mod = freqs[:, None, None] * jnp.transpose(lags)[None, :, :] % (2 * n_freq)
    angles = index_mod.astype(jnp.float32) * (math.pi / n_freq)
    return (jnp.cos(angles), jnp.sin(angles))


def cross_block(src_block, rcv_block):
    block_width = src_block.shape[2]
    src_five = src_block.reshape(2, SEGS, WIN, block_width, src_block.shape[3])
    rcv_five = rcv_block.reshape(2, SEGS, WIN, block_width, rcv_block.shape[3])
    swapped = jnp.stack([src_five[1], -src_five[0]])
    real_part = jnp.einsum(
        "cgwfs,cgwfr->gfsr", src_five, rcv_five, preferred_element_type=jnp.float32
    )
    imag_part = jnp.einsum(
        "cgwfs,cgwfr->gfsr", swapped, rcv_five, preferred_element_type=jnp.float32
    )
    floor_mod = jnp.maximum(jnp.sqrt(real_part * real_part + imag_part * imag_part), 1.0)
    stacked_re = (jnp.sum(real_part / floor_mod, axis=0) / SEGS).astype(jnp.bfloat16)
    stacked_im = (jnp.sum(imag_part / floor_mod, axis=0) / SEGS).astype(jnp.bfloat16)
    return (stacked_re, stacked_im)


def source_slant(stacked_re, stacked_im, rcv_cos, rcv_sin, src_cos, src_sin, factor):
    left_op = jnp.concatenate([stacked_re, stacked_im], axis=2)
    cos_b = rcv_cos.astype(jnp.bfloat16)
    sin_b = rcv_sin.astype(jnp.bfloat16)
    upper_half = jnp.concatenate([cos_b, sin_b], axis=2)
    bottom = jnp.concatenate([-sin_b, cos_b], axis=2)
    right_op = jnp.concatenate([upper_half, bottom], axis=1)
    sums = jnp.einsum("fsk,fkq->fsq", left_op, right_op, preferred_element_type=jnp.float32)
    n_slow = rcv_cos.shape[2]
    sum_re = sums[:, :, :n_slow]
    sum_im = sums[:, :, n_slow:]
    panel_re = (sum_re * src_cos + sum_im * src_sin) * factor
    panel_im = (sum_im * src_cos - sum_re * src_sin) * factor
    return jnp.transpose(jnp.stack([panel_re, panel_im]), (3, 0, 2, 1))


def receiver_right(src_cos_b, src_sin_b):
    upper_half = jnp.concatenate([src_cos_b, -src_sin_b], axis=2)
    bottom = jnp.concatenate([src_sin_b, src_cos_b], axis=2)
    return jnp.concatenate([upper_half, bottom], axis=1)


def receiver_sums(left_op, right_op):
    return jnp.einsum("fkr,fkq->fqr", left_op, right_op, preferred_element_type=jnp.float32)


def receiver_outer(sums, rcv_cos, rcv_sin, factor):
    n_slow = rcv_cos.shape[2]
    cos_t = jnp.transpose(rcv_cos, (0, 2, 1))
    sin_t = jnp.transpose(rcv_sin, (0, 2, 1))
    sum_re = sums[:, :n_slow, :]
    sum_im = sums[:, n_slow:, :]
    panel_re = (sum_re * cos_t - sum_im * sin_t) * factor
    panel_im = (sum_re * sin_t + sum_im * cos_t) * factor
    return jnp.transpose(jnp.stack([panel_re, panel_im]), (2, 0, 1, 3))


def per_device_general(src_spec, rcv_spec, lag_table, src_pos, rcv_pos):
    src_full = lax.all_gather(src_spec, "rcv", axis=2, tiled=True)
    n_freq = src_full.shape[2]
    src_dev = src_full.shape[3]
    rcv_dev = rcv_spec.shape[3]
    n_slow = lag_table.shape[0]
    n_src = lax.axis_size("src")
    n_rcv = lax.axis_size("rcv")
    src_factor = 1.0 / math.sqrt(rcv_dev * n_rcv)
    rcv_factor = 1.0 / math.sqrt(src_dev * n_src)
    lag_src = jnp.take(lag_table, src_pos, axis=1)
    lag_rcv = jnp.take(lag_table, rcv_pos, axis=1)
    src_init = jnp.zeros((n_slow, 2, src_dev, n_freq), jnp.float32)
    other_init = jnp.zeros((n_slow, 2, n_freq, rcv_dev), jnp.float32)
    shard_piece = lax.all_gather(rcv_spec, "src", axis=2, tiled=True)
    block_width = math.gcd(shard_piece.shape[2], 16)

    def inner(turn_index, totals):
        offset = turn_index * block_width
        freqs = offset + jnp.arange(block_width, dtype=jnp.int32)
        src_block = lax.dynamic_slice_in_dim(src_full, offset, block_width, 2)
        rcv_block = lax.dynamic_slice_in_dim(shard_piece, offset, block_width, 2)
        stacked_re, stacked_im = cross_block(src_block, rcv_block)
        rcv_cos, rcv_sin = phase_table(freqs, lag_rcv, n_freq)
        src_cos, src_sin = phase_table(freqs, lag_src, n_freq)
        src_part = source_slant(
            stacked_re, stacked_im, rcv_cos, rcv_sin, src_cos, src_sin, src_factor
        )
        src_total = lax.dynamic_update_slice_in_dim(totals[0], src_part, offset, 3)
        left_op = jnp.concatenate([stacked_re, stacked_im], axis=1)
        right_op = receiver_right(src_cos.astype(jnp.bfloat16), src_sin.astype(jnp.bfloat16))
        rcv_part = receiver_outer(receiver_sums(left_op, right_op), rcv_cos, rcv_sin, rcv_factor)
        other = lax.dynamic_update_slice_in_dim(totals[1], rcv_part, offset, 2)
        return (src_total, other)

    src_total, other = lax.fori_loop(
        0, shard_piece.shape[2] // block_width, inner, (src_init, other_init)
    )
    panel_src = lax.psum_scatter(src_total, "rcv", scatter_dimension=2, tiled=True)
    panel_rcv = lax.psum_scatter(other, "src", scatter_dimension=2, tiled=True)
    return (panel_src, panel_rcv)


LANES = 128
ROWS = 32
LAG_ROWS = 16
CALLS = ((0,), (3,), (2,), (1,))
VMEM = 20 * 2**20
FULL_VMEM = 56 * 2**20
TILE_ROWS = 256
COST = 10**6
F32 = jnp.float32
BF16 = jnp.bfloat16
SIN = [(-1) ** n * (math.pi / 2) ** (2 * n + 1) / math.factorial(2 * n + 1) for n in range(5)]
COS = [(-1) ** n * (math.pi / 2) ** (2 * n) / math.factorial(2 * n) for n in range(6)]


def horner(coefs, v):
    total = coefs[-1]
    for coef in coefs[-2::-1]:
        total = coef + v * total
    return total


def phases(lag, freq, period):
    turns = lag * freq * (1.0 / period)
    quarters = 4.0 * (turns - jnp.floor(turns))
    near = jnp.floor(quarters + 0.5)
    u = quarters - near
    v = u * u
    s = u * horner(SIN, v)
    c = horner(COS, v)
    odd = (near == 1.0) | (near == 3.0)
    cos = jnp.where(odd, s, c)
    sin = jnp.where(odd, c, s)
    cos = jnp.where((near == 1.0) | (near == 2.0), -cos, cos)
    sin = jnp.where((near == 2.0) | (near == 3.0), -sin, sin)
    return cos, sin


def lanes_of(rows):
    return lax.broadcasted_iota(jnp.int32, (rows, LANES), 1)


class Sizes:
    def __init__(self, shapes, n_src, n_rcv):
        src_spec, rcv_spec, lag_table = shapes
        self.n_src, self.n_rcv, self.n_dev = n_src, n_rcv, n_src * n_rcv
        self.n_slow, self.n_pos = lag_table
        self.n_win = src_spec[1]
        self.src_freq, self.src_dev = src_spec[2:]
        self.rcv_freq, self.rcv_dev = rcv_spec[2:]
        self.n_freq = self.rcv_freq * n_src
        self.own = self.n_freq // self.n_dev
        self.s_all, self.r_all = self.src_dev * n_src, self.rcv_dev * n_rcv
        self.src_part = self.src_dev // n_rcv
        self.low = n_src // n_rcv
        self.chunk = self.own // 2 * ROWS

    def fits(self):
        return (
            2 * self.n_win == ROWS
            and 2 * self.n_slow == ROWS
            and self.n_win == WIN * SEGS
            and self.n_rcv == 4
            and self.own == 8
            and self.own // 2 * ROWS == LANES
            and self.src_freq == self.low * self.n_rcv * self.own
            and self.rcv_freq == self.n_rcv * self.own
            and self.n_dev * self.own == self.n_freq == 2 * LANES
            and 2 * self.src_dev == LANES
            and self.n_src % 2 == 0
            and self.rcv_dev == 2 * LANES
            and self.src_part * self.own == LANES
            and LANES % self.n_dev == 0
            and self.n_pos % LANES == 0
        )


def look_up(z, table, pos_ref):
    pos = pos_ref[...]
    lane = lax.broadcasted_iota(jnp.int32, (LANES, pos.shape[1]), 0)
    spot = (lane == pos % LANES).astype(F32).astype(BF16)
    found = jnp.dot(table, spot, preferred_element_type=F32)
    total = 0.0
    for block in range(z.n_pos // LANES):
        total += jnp.where(pos // LANES == block, found[block * z.n_slow:(block + 1) * z.n_slow], 0.0)
    return total


def whole(*shape):
    return pl.BlockSpec(shape, lambda *_: (0,) * len(shape))


def pack_sources(z):
    def kernel(src_ref, *refs):
        outs, flat = refs[:z.n_rcv], refs[z.n_rcv]
        for row in range(ROWS):
            flat[row * z.src_freq:(row + 1) * z.src_freq, :z.src_dev] = src_ref[row].astype(F32)
        half = z.own // 2
        for other in range(z.n_rcv):
            rcv = lax.axis_index("rcv") ^ other
            for low in range(z.low):
                for group in range(2):
                    freq = (low * z.n_rcv + rcv) * z.own + group * half
                    tiles = [flat[pl.ds(freq + m, ROWS, stride=z.src_freq), :] for m in range(half)]
                    turned = jnp.transpose(jnp.concatenate(tiles, 0))[:z.src_dev]
                    outs[other][low, group * z.src_dev:(group + 1) * z.src_dev, :] = turned.astype(BF16)

    shape = (z.low, z.chunk, LANES)
    return pl.pallas_call(
        kernel,
        grid=(1,),
        in_specs=[whole(ROWS, z.src_freq, z.src_dev)],
        out_specs=[whole(*shape)] * z.n_rcv,
        out_shape=[jax.ShapeDtypeStruct(shape, BF16)] * z.n_rcv,
        scratch_shapes=[pltpu.VMEM(((ROWS + 1) * z.src_freq, LANES), F32)],
        compiler_params=pltpu.CompilerParams(vmem_limit_bytes=FULL_VMEM),
        cost_estimate=pl.CostEstimate(flops=10**6, bytes_accessed=2 * 10**6, transcendentals=0),
        name="pack_sources",
    )


def order_sources(z):
    def kernel(lag_ref, *refs):
        out_ref = refs[-1]
        for other in range(z.n_rcv):
            place = lax.axis_index("rcv") ^ other
            out_ref[pl.ds(place * z.low, z.low), :z.chunk, :] = refs[other][...]
        for place in range(z.n_src):
            out_ref[place, z.chunk:, :] = lag_ref[...]

    shape = (z.chunk + LAG_ROWS // 2, LANES)
    return pl.pallas_call(
        kernel,
        grid=(1,),
        in_specs=[whole(LAG_ROWS // 2, LANES)] + [whole(z.low, z.chunk, LANES)] * z.n_rcv,
        out_specs=whole(z.n_src, *shape),
        out_shape=jax.ShapeDtypeStruct((z.n_src, *shape), BF16),
        compiler_params=pltpu.CompilerParams(vmem_limit_bytes=VMEM),
        cost_estimate=pl.CostEstimate(flops=10**6, bytes_accessed=10**6, transcendentals=0),
        name="order_sources",
    )


def pack_receivers(z):
    def kernel(pos_ref, src_pos_ref, rcv_ref, lag_ref, *refs):
        outs, src_out, flat = refs[:z.n_rcv], refs[z.n_rcv], refs[z.n_rcv + 1:]
        blocks = [lag_ref[:, place:place + LANES] for place in range(0, z.n_pos, LANES)]
        table = (jnp.concatenate(blocks, 0) - z.n_freq).astype(F32).astype(BF16)
        src_lags = look_up(z, table, src_pos_ref)
        src_out[...] = jnp.concatenate([src_lags[:LAG_ROWS // 2], src_lags[LAG_ROWS // 2:]], 1).astype(BF16)
        spans = range(0, z.rcv_dev, LANES)
        lags = look_up(z, table, pos_ref).astype(BF16)
        for row in range(ROWS):
            here = rcv_ref[row].astype(F32)
            for n, span in enumerate(spans):
                flat[n][row * z.rcv_freq:(row + 1) * z.rcv_freq, :] = here[:, span:span + LANES]
        for other in range(z.n_rcv):
            first = (lax.axis_index("rcv") ^ other) * z.own
            for n, span in enumerate(spans):
                for k in range(z.own):
                    tile = flat[n][pl.ds(first + k, ROWS, stride=z.rcv_freq), :]
                    outs[other][k * ROWS:(k + 1) * ROWS, span:span + LANES] = tile.astype(BF16)
                outs[other][z.own * ROWS:, span:span + LANES] = lags[:, span:span + LANES]

    shape = (z.own * ROWS + LAG_ROWS, z.rcv_dev)
    return pl.pallas_call(
        kernel,
        grid=(1,),
        in_specs=[
            whole(1, z.rcv_dev),
            whole(1, z.src_dev),
            whole(ROWS, z.rcv_freq, z.rcv_dev),
            whole(z.n_slow, z.n_pos),
        ],
        out_specs=[whole(*shape)] * z.n_rcv + [whole(LAG_ROWS // 2, LANES)],
        out_shape=[jax.ShapeDtypeStruct(shape, BF16)] * z.n_rcv
        + [jax.ShapeDtypeStruct((LAG_ROWS // 2, LANES), BF16)],
        scratch_shapes=[pltpu.VMEM(((ROWS + 1) * z.rcv_freq, LANES), F32)] * (z.rcv_dev // LANES),
        compiler_params=pltpu.CompilerParams(vmem_limit_bytes=VMEM),
        cost_estimate=pl.CostEstimate(flops=10**6, bytes_accessed=2 * 10**6, transcendentals=0),
        name="pack_receivers",
    )


def cross_spectra(z, src_ref, rcv_refs, turn, right, stack):
    half = z.own // 2
    group, place = divmod(turn, half)
    begin = place * ROWS
    rows = slice(turn * ROWS, (turn + 1) * ROWS)
    spec = jnp.concatenate([ref[rows, :] for ref in rcv_refs], 1).astype(F32)
    turned = jnp.concatenate([-spec[z.n_win:], spec[:z.n_win]], 0)
    window = lax.broadcasted_iota(jnp.int32, (ROWS, 1), 0) % z.n_win
    for seg in range(SEGS):
        here = window // WIN == seg
        right[seg, begin:begin + ROWS, :] = jnp.where(here, spec, 0.0).astype(BF16)
        right[SEGS + seg, begin:begin + ROWS, :] = jnp.where(here, turned, 0.0).astype(BF16)
    width, height = 2 * LANES, TILE_ROWS
    r_now = spec.shape[1]
    for col in range(0, r_now, width):
        for row in range(0, z.s_all, height):
            senders = range(row // z.src_dev, (row + height) // z.src_dev)
            lines = slice(group * z.src_dev, (group + 1) * z.src_dev)
            part = jnp.concatenate([src_ref[sender, lines, :] for sender in senders], 0)
            total_re, total_im = 0.0, 0.0
            for seg in range(SEGS):
                real = jnp.dot(part, right[seg, :, col:col + width], preferred_element_type=F32)
                imag = jnp.dot(part, right[SEGS + seg, :, col:col + width], preferred_element_type=F32)
                scale = lax.rsqrt(jnp.maximum(real * real + imag * imag, 1.0))
                total_re, total_im = total_re + real * scale, total_im + imag * scale
            stack[row:row + height, col:col + width] = total_re.astype(BF16)
            stack[z.s_all + row:z.s_all + row + height, col:col + width] = total_im.astype(BF16)


def compute(z, count, first, last):
    src_factor = 1.0 / (SEGS * math.sqrt(z.r_all))
    rcv_factor = 1.0 / (SEGS * math.sqrt(z.s_all))
    n = z.n_slow
    r_now = count * z.rcv_dev
    place_lag = z.own * ROWS

    def kernel(src_ref, *refs):
        rcv_refs, refs = refs[:count], refs[count:]
        if not first:
            before_ref, refs = refs[0], refs[1:]
        out_refs, refs = refs[:count], refs[count:]
        sum_ref, lag, waves, right, stack = refs[:5]
        right[...] = jnp.zeros_like(right)
        for src in range(z.n_src):
            lags = src_ref[src, z.chunk:, :].astype(F32) + float(z.n_freq)
            for part in range(2):
                rows = slice(part * LAG_ROWS // 2, (part + 1) * LAG_ROWS // 2)
                lanes = slice(part * z.src_dev, (part + 1) * z.src_dev)
                lag[rows, src * z.src_dev:(src + 1) * z.src_dev] = lags[:, lanes]
        for block, ref in enumerate(rcv_refs):
            place = z.s_all + block * z.rcv_dev
            lag[:, place:place + z.rcv_dev] = ref[place_lag:, :].astype(F32) + float(z.n_freq)
        begin = lax.axis_index("src") * z.rcv_freq + lax.axis_index("rcv") * z.own
        waves[0], waves[1] = phases(lag[...], begin.astype(F32), 2.0 * z.n_freq)
        waves[2], waves[3] = phases(lag[...], 1.0, 2.0 * z.n_freq)

        def next_waves():
            cos, sin = waves[0], waves[1]
            step_cos, step_sin = waves[2], waves[3]
            waves[0], waves[1] = cos * step_cos - sin * step_sin, sin * step_cos + cos * step_sin
            return cos[:, :z.s_all], sin[:, :z.s_all], cos[:, z.s_all:], sin[:, z.s_all:]

        def cross(turn, slot):
            cross_spectra(z, src_ref, rcv_refs, turn, right.at[turn % (z.own // 2)], stack.at[slot])

        def slant(turn, slot):
            src_cos, src_sin, rcv_cos, rcv_sin = next_waves()
            upper = jnp.concatenate([src_cos, src_sin], 1)
            lower = jnp.concatenate([-src_sin, src_cos], 1)
            both = jnp.concatenate([upper, lower], 0).astype(BF16)
            over_src = jnp.dot(both, stack[slot], preferred_element_type=F32) * rcv_factor
            over_re, over_im = over_src[:n], over_src[n:]
            panel_re = over_re * rcv_cos - over_im * rcv_sin
            panel_im = over_re * rcv_sin + over_im * rcv_cos
            panel = jnp.concatenate([panel_re, panel_im], 0).astype(BF16)
            for block, ref in enumerate(out_refs):
                ref[turn] = panel[:, block * z.rcv_dev:(block + 1) * z.rcv_dev]
            dims = (((1,), (1,)), ((), ()))
            with_re = jnp.concatenate([rcv_cos, rcv_sin], 0).astype(BF16)
            with_im = jnp.concatenate([-rcv_sin, rcv_cos], 0).astype(BF16)
            over_rcv = lax.dot_general(with_re, stack[slot, :z.s_all, :], dims, preferred_element_type=F32)
            over_rcv += lax.dot_general(with_im, stack[slot, z.s_all:, :], dims, preferred_element_type=F32)
            if not first:
                over_rcv += before_ref[turn]
            if not last:
                sum_ref[turn] = over_rcv
                return
            over_rcv *= src_factor
            over_re, over_im = over_rcv[:n], over_rcv[n:]
            panel_re = over_re * src_cos + over_im * src_sin
            panel_im = over_im * src_cos - over_re * src_sin
            refs[5][turn] = jnp.concatenate([panel_re, panel_im], 0)
            regroup_after(z, refs[5], turn)

        cross(0, 0)
        for turn in range(1, z.own):
            cross(turn, turn % 2)
            slant(turn - 1, (turn - 1) % 2)
        slant(z.own - 1, (z.own - 1) % 2)
        if last:
            send_sources(z, refs[5], sum_ref)

    in_specs = [whole(z.n_src, z.chunk + LAG_ROWS // 2, LANES)]
    in_specs += [whole(z.own * ROWS + LAG_ROWS, z.rcv_dev)] * count
    out_specs = [whole(z.own, ROWS, z.rcv_dev)] * count
    out_shape = [jax.ShapeDtypeStruct((z.own, ROWS, z.rcv_dev), BF16)] * count
    part_spec = whole(z.own, ROWS, z.s_all)
    scratch = [
        pltpu.VMEM((n, z.s_all + r_now), F32),
        pltpu.VMEM((4, n, z.s_all + r_now), F32),
        pltpu.VMEM((z.own // 2, 2 * SEGS, LANES, r_now), BF16),
        pltpu.VMEM((2, 2 * z.s_all, r_now), BF16),
    ]
    if not first:
        in_specs.append(part_spec)
    if last:
        out_specs.append(whole(z.n_dev, ROWS, LANES))
        out_shape.append(jax.ShapeDtypeStruct((z.n_dev, ROWS, LANES), BF16))
        scratch.append(pltpu.VMEM((z.own, ROWS, z.s_all), F32))
    else:
        out_specs.append(part_spec)
        out_shape.append(jax.ShapeDtypeStruct((z.own, ROWS, z.s_all), F32))
    return pl.pallas_call(
        kernel,
        grid=(1,),
        in_specs=in_specs,
        out_specs=out_specs,
        out_shape=out_shape,
        scratch_shapes=scratch,
        compiler_params=pltpu.CompilerParams(vmem_limit_bytes=VMEM),
        cost_estimate=pl.CostEstimate(flops=COST * count, bytes_accessed=10**6, transcendentals=0),
        name="compute_first" if first else "compute_last" if last else "compute_next",
    )


def regroup(z, sums, bit, first):
    lane = lanes_of(ROWS)
    shift = bit * z.src_part
    upper = lane & shift != 0
    for block in range(z.s_all // LANES):
        lanes = slice(block * LANES, (block + 1) * LANES)
        one, two = sums[first, :, lanes], sums[first + bit, :, lanes]
        sums[first, :, lanes] = jnp.where(upper, pltpu.roll(two, shift, 1), one)
        sums[first + bit, :, lanes] = jnp.where(upper, two, pltpu.roll(one, LANES - shift, 1))


def regroup_after(z, sums, turn):
    bit = 1
    while bit < z.own and turn & bit:
        base = turn & ~(2 * bit - 1)
        for low in range(bit):
            regroup(z, sums, bit, base + low)
        bit *= 2


def send_sources(z, sums, out_ref):
    for block in range(z.s_all // LANES):
        for group in range(z.own):
            out_ref[block * z.own + group] = sums[group, :, block * LANES:(block + 1) * LANES].astype(BF16)


def unpack_block(z, in_ref, flat, write):
    n = z.n_slow
    for span in range(0, z.rcv_dev, LANES):
        for k in range(z.own):
            flat[k * ROWS:(k + 1) * ROWS, :] = in_ref[k, :, span:span + LANES].astype(F32)
        for slow in range(n):
            for part in range(2):
                write(2 * slow + part, span, flat[pl.ds(part * n + slow, z.own, stride=ROWS), :])


def unpack_first(z, others):
    def kernel(*refs):
        in_refs, out_ref, flat = refs[:len(others)], refs[-2], refs[-1]
        for other, in_ref in zip(others, in_refs):
            rows = pl.ds(pl.multiple_of((lax.axis_index("rcv") ^ other) * z.own, z.own), z.own)

            def write(index, span, tile):
                out_ref[index, rows, span:span + LANES] = tile

            unpack_block(z, in_ref, flat, write)

    return pl.pallas_call(
        kernel,
        grid=(1,),
        in_specs=[whole(z.own, ROWS, z.rcv_dev)] * len(others),
        out_specs=whole(ROWS, z.rcv_freq, z.rcv_dev),
        out_shape=jax.ShapeDtypeStruct((ROWS, z.rcv_freq, z.rcv_dev), F32),
        scratch_shapes=[pltpu.VMEM(((z.own + 1) * ROWS, LANES), F32)],
        compiler_params=pltpu.CompilerParams(vmem_limit_bytes=VMEM),
        cost_estimate=pl.CostEstimate(flops=10**6, bytes_accessed=10**6, transcendentals=0),
        name="unpack_first",
    )


def unpack_last(z, other):
    n = z.n_slow
    group = LANES // z.n_dev
    width = z.src_part

    def kernel(rcv_in, src_in, held_ref, rcv_ref, src_ref, flat, small, table):
        del held_ref

        def write(index, span, tile):
            rcv_ref[index, :, span:span + LANES] = tile

        unpack_block(z, rcv_in, small, write)
        for dev in range(z.n_dev):
            flat[dev * ROWS:(dev + 1) * ROWS, :] = src_in[dev].astype(F32)
        lane = lanes_of(width)
        for first in range(0, ROWS, group):
            tiles = [flat[pl.ds(first + j, z.n_dev, stride=ROWS), :] for j in range(group)]
            turned = jnp.transpose(jnp.concatenate(tiles, 0))
            for j in range(group):
                for block in range(z.own // group):
                    total = jnp.zeros((width, LANES), F32)
                    for k in range(group):
                        row = (block * group + k) * width
                        tile = turned[row:row + width, :]
                        shift = (k - j) * z.n_dev % LANES
                        moved = pltpu.roll(tile, shift, 1) if shift else tile
                        total = jnp.where((lane >= k * z.n_dev) & (lane < (k + 1) * z.n_dev), moved, total)
                    rows = slice((first + j) * width, (first + j + 1) * width)
                    table[rows, block * LANES:(block + 1) * LANES] = total.astype(BF16)
        here = lax.broadcasted_iota(jnp.int32, (z.n_freq, z.n_freq), 0)
        there = lax.broadcasted_iota(jnp.int32, (z.n_freq, z.n_freq), 1)
        order = (there == here % z.n_dev * z.own + here // z.n_dev).astype(F32).astype(BF16)
        ordered = jnp.dot(table[...], order, preferred_element_type=F32)
        for index in range(ROWS):
            part, slow = divmod(index, n)
            src_ref[2 * slow + part] = ordered[index * width:(index + 1) * width, :]

    return pl.pallas_call(
        kernel,
        grid=(1,),
        in_specs=[
            whole(z.own, ROWS, z.rcv_dev),
            whole(z.n_dev, ROWS, LANES),
            pl.BlockSpec(memory_space=pl.ANY),
        ],
        out_specs=[
            pl.BlockSpec((ROWS, z.own, z.rcv_dev), lambda k: (0, lax.axis_index("rcv") ^ other, 0)),
            whole(ROWS, width, z.n_freq),
        ],
        scratch_shapes=[
            pltpu.VMEM(((z.n_dev + 1) * ROWS, LANES), F32),
            pltpu.VMEM(((z.own + 1) * ROWS, LANES), F32),
            pltpu.VMEM((ROWS * width, z.n_freq), BF16),
        ],
        out_shape=[
            jax.ShapeDtypeStruct((ROWS, z.rcv_freq, z.rcv_dev), F32),
            jax.ShapeDtypeStruct((ROWS, width, z.n_freq), F32),
        ],
        input_output_aliases={2: 0},
        compiler_params=pltpu.CompilerParams(vmem_limit_bytes=VMEM),
        cost_estimate=pl.CostEstimate(flops=10**6, bytes_accessed=2 * 10**6, transcendentals=0),
        name="unpack_last",
    )


def swap(z, block, other):
    if other == 0:
        return block
    return lax.ppermute(block, "rcv", [(j, j ^ other) for j in range(z.n_rcv)])


def arrive(done, others, values):
    here, values = lax.optimization_barrier(([done[other] for other in others], values))
    done.update(zip(others, here))
    return values


def per_device(src_spec, rcv_spec, lag_table, src_pos, rcv_pos):
    n_src, n_rcv = lax.axis_size("src"), lax.axis_size("rcv")
    z = Sizes((src_spec.shape, rcv_spec.shape, lag_table.shape), n_src, n_rcv)
    if not z.fits():
        return per_device_general(src_spec, rcv_spec, lag_table, src_pos, rcv_pos)
    src_rows = src_spec.reshape(ROWS, z.src_freq, z.src_dev)
    rcv_rows = rcv_spec.reshape(ROWS, z.rcv_freq, z.rcv_dev)
    parts = pack_sources(z)(src_rows)
    moved = {other: swap(z, parts[other], other) for other in (3, 2, 1, 0)}
    *packed, src_lags = pack_receivers(z)(rcv_pos[None], src_pos[None], rcv_rows, lag_table)
    spread = order_sources(z)(src_lags, *(moved[other] for other in range(z.n_rcv)))
    sources = lax.all_to_all(spread, "src", 0, 0, tiled=True)
    blocks = {other: swap(z, packed[other], other) for others in CALLS for other in others}
    done, carry = {}, ()
    for n, others in enumerate(CALLS):
        ready = [blocks[other] for other in others]
        if n >= 2:
            ready, carry = arrive(done, CALLS[n - 2], (ready, carry))
        call = compute(z, len(others), n == 0, n == len(CALLS) - 1)
        *panels, total = call(sources, *ready, *carry)
        done.update({other: swap(z, panel, other) for other, panel in zip(others, panels)})
        carry = (total,)
    total = arrive(done, CALLS[-2], total)
    got_src = lax.all_to_all(total, ("src", "rcv"), 0, 0, tiled=True)
    late = CALLS[-1][0]
    early = tuple(other for other in done if other != late)
    held = unpack_first(z, early)(*(done[other] for other in early))
    panel_rcv, panel_src = unpack_last(z, late)(done[late], got_src, held)
    return (
        panel_src.reshape(z.n_slow, 2, z.src_part, z.n_freq),
        panel_rcv.reshape(z.n_slow, 2, z.rcv_freq, z.rcv_dev),
    )


def solution(mesh):
    placed = (P(None, None, "rcv", "src"), P(None, None, "src", "rcv"), P(), P("src"), P("rcv"))
    return jax.shard_map(
        per_device,
        mesh=mesh,
        in_specs=placed,
        out_specs=(P(None, None, ("src", "rcv"), None), P(None, None, "src", "rcv")),
        check_vma=False,
    )
```

```python
import math

import jax
import jax.numpy as jnp
from jax import lax
from jax.experimental import pallas as pl
from jax.experimental.pallas import tpu as pltpu
from jax.sharding import PartitionSpec as P

WIN = 8
SEGS = 2


def phase_table(freqs, lags, n_freq):
    index_mod = freqs[:, None, None] * jnp.transpose(lags)[None, :, :] % (2 * n_freq)
    angles = index_mod.astype(jnp.float32) * (math.pi / n_freq)
    return (jnp.cos(angles), jnp.sin(angles))


def cross_block(src_block, rcv_block):
    block_width = src_block.shape[2]
    src_five = src_block.reshape(2, SEGS, WIN, block_width, src_block.shape[3])
    rcv_five = rcv_block.reshape(2, SEGS, WIN, block_width, rcv_block.shape[3])
    swapped = jnp.stack([src_five[1], -src_five[0]])
    real_part = jnp.einsum(
        "cgwfs,cgwfr->gfsr", src_five, rcv_five, preferred_element_type=jnp.float32
    )
    imag_part = jnp.einsum(
        "cgwfs,cgwfr->gfsr", swapped, rcv_five, preferred_element_type=jnp.float32
    )
    floor_mod = jnp.maximum(jnp.sqrt(real_part * real_part + imag_part * imag_part), 1.0)
    stacked_re = (jnp.sum(real_part / floor_mod, axis=0) / SEGS).astype(jnp.bfloat16)
    stacked_im = (jnp.sum(imag_part / floor_mod, axis=0) / SEGS).astype(jnp.bfloat16)
    return (stacked_re, stacked_im)


def source_slant(stacked_re, stacked_im, rcv_cos, rcv_sin, src_cos, src_sin, factor):
    left_op = jnp.concatenate([stacked_re, stacked_im], axis=2)
    cos_b = rcv_cos.astype(jnp.bfloat16)
    sin_b = rcv_sin.astype(jnp.bfloat16)
    upper_half = jnp.concatenate([cos_b, sin_b], axis=2)
    bottom = jnp.concatenate([-sin_b, cos_b], axis=2)
    right_op = jnp.concatenate([upper_half, bottom], axis=1)
    sums = jnp.einsum("fsk,fkq->fsq", left_op, right_op, preferred_element_type=jnp.float32)
    n_slow = rcv_cos.shape[2]
    sum_re = sums[:, :, :n_slow]
    sum_im = sums[:, :, n_slow:]
    panel_re = (sum_re * src_cos + sum_im * src_sin) * factor
    panel_im = (sum_im * src_cos - sum_re * src_sin) * factor
    return jnp.transpose(jnp.stack([panel_re, panel_im]), (3, 0, 2, 1))


def receiver_right(src_cos_b, src_sin_b):
    upper_half = jnp.concatenate([src_cos_b, -src_sin_b], axis=2)
    bottom = jnp.concatenate([src_sin_b, src_cos_b], axis=2)
    return jnp.concatenate([upper_half, bottom], axis=1)


def receiver_sums(left_op, right_op):
    return jnp.einsum("fkr,fkq->fqr", left_op, right_op, preferred_element_type=jnp.float32)


def receiver_outer(sums, rcv_cos, rcv_sin, factor):
    n_slow = rcv_cos.shape[2]
    cos_t = jnp.transpose(rcv_cos, (0, 2, 1))
    sin_t = jnp.transpose(rcv_sin, (0, 2, 1))
    sum_re = sums[:, :n_slow, :]
    sum_im = sums[:, n_slow:, :]
    panel_re = (sum_re * cos_t - sum_im * sin_t) * factor
    panel_im = (sum_re * sin_t + sum_im * cos_t) * factor
    return jnp.transpose(jnp.stack([panel_re, panel_im]), (2, 0, 1, 3))


def per_device_general(src_spec, rcv_spec, lag_table, src_pos, rcv_pos):
    src_full = lax.all_gather(src_spec, "rcv", axis=2, tiled=True)
    n_freq = src_full.shape[2]
    src_dev = src_full.shape[3]
    rcv_dev = rcv_spec.shape[3]
    n_slow = lag_table.shape[0]
    n_src = lax.axis_size("src")
    n_rcv = lax.axis_size("rcv")
    src_factor = 1.0 / math.sqrt(rcv_dev * n_rcv)
    rcv_factor = 1.0 / math.sqrt(src_dev * n_src)
    lag_src = jnp.take(lag_table, src_pos, axis=1)
    lag_rcv = jnp.take(lag_table, rcv_pos, axis=1)
    src_init = jnp.zeros((n_slow, 2, src_dev, n_freq), jnp.float32)
    other_init = jnp.zeros((n_slow, 2, n_freq, rcv_dev), jnp.float32)
    shard_piece = lax.all_gather(rcv_spec, "src", axis=2, tiled=True)
    block_width = math.gcd(shard_piece.shape[2], 16)

    def inner(turn_index, totals):
        offset = turn_index * block_width
        freqs = offset + jnp.arange(block_width, dtype=jnp.int32)
        src_block = lax.dynamic_slice_in_dim(src_full, offset, block_width, 2)
        rcv_block = lax.dynamic_slice_in_dim(shard_piece, offset, block_width, 2)
        stacked_re, stacked_im = cross_block(src_block, rcv_block)
        rcv_cos, rcv_sin = phase_table(freqs, lag_rcv, n_freq)
        src_cos, src_sin = phase_table(freqs, lag_src, n_freq)
        src_part = source_slant(
            stacked_re, stacked_im, rcv_cos, rcv_sin, src_cos, src_sin, src_factor
        )
        src_total = lax.dynamic_update_slice_in_dim(totals[0], src_part, offset, 3)
        left_op = jnp.concatenate([stacked_re, stacked_im], axis=1)
        right_op = receiver_right(src_cos.astype(jnp.bfloat16), src_sin.astype(jnp.bfloat16))
        rcv_part = receiver_outer(receiver_sums(left_op, right_op), rcv_cos, rcv_sin, rcv_factor)
        other = lax.dynamic_update_slice_in_dim(totals[1], rcv_part, offset, 2)
        return (src_total, other)

    src_total, other = lax.fori_loop(
        0, shard_piece.shape[2] // block_width, inner, (src_init, other_init)
    )
    panel_src = lax.psum_scatter(src_total, "rcv", scatter_dimension=2, tiled=True)
    panel_rcv = lax.psum_scatter(other, "src", scatter_dimension=2, tiled=True)
    return (panel_src, panel_rcv)


LANES = 128
ROWS = 32
LAG_ROWS = 16
FAR_FIRST = (3, 2, 1, 0)
CALLS = ((0,), (3,), (2,), (1,))
VMEM = 20 * 2**20
FULL_VMEM = 56 * 2**20
TILE_ROWS = 256
COST = 10**6
F32 = jnp.float32
BF16 = jnp.bfloat16
SIN = [(-1) ** n * (math.pi / 2) ** (2 * n + 1) / math.factorial(2 * n + 1) for n in range(5)]
COS = [(-1) ** n * (math.pi / 2) ** (2 * n) / math.factorial(2 * n) for n in range(6)]


def horner(coefs, v):
    total = coefs[-1]
    for coef in coefs[-2::-1]:
        total = coef + v * total
    return total


def phases(lag, freq, period):
    turns = lag * freq * (1.0 / period)
    quarters = 4.0 * (turns - jnp.floor(turns))
    near = jnp.floor(quarters + 0.5)
    u = quarters - near
    v = u * u
    s = u * horner(SIN, v)
    c = horner(COS, v)
    odd = (near == 1.0) | (near == 3.0)
    cos = jnp.where(odd, s, c)
    sin = jnp.where(odd, c, s)
    cos = jnp.where((near == 1.0) | (near == 2.0), -cos, cos)
    sin = jnp.where((near == 2.0) | (near == 3.0), -sin, sin)
    return cos, sin


def lanes_of(rows):
    return lax.broadcasted_iota(jnp.int32, (rows, LANES), 1)


class Sizes:
    def __init__(self, shapes, n_src, n_rcv):
        src_spec, rcv_spec, lag_table = shapes
        self.n_src, self.n_rcv, self.n_dev = n_src, n_rcv, n_src * n_rcv
        self.n_slow, self.n_pos = lag_table
        self.n_win = src_spec[1]
        self.src_freq, self.src_dev = src_spec[2:]
        self.rcv_freq, self.rcv_dev = rcv_spec[2:]
        self.n_freq = self.rcv_freq * n_src
        self.own = self.n_freq // self.n_dev
        self.s_all, self.r_all = self.src_dev * n_src, self.rcv_dev * n_rcv
        self.src_part = self.src_dev // n_rcv
        self.low = n_src // n_rcv
        self.chunk = self.own // 2 * ROWS

    def fits(self):
        return (
            2 * self.n_win == ROWS
            and 2 * self.n_slow == ROWS
            and self.n_win == WIN * SEGS
            and self.n_rcv == 4
            and self.own == 8
            and self.own // 2 * ROWS == LANES
            and self.src_freq == self.low * self.n_rcv * self.own
            and self.rcv_freq == self.n_rcv * self.own
            and self.n_dev * self.own == self.n_freq == 2 * LANES
            and 2 * self.src_dev == LANES
            and self.n_src % 2 == 0
            and self.rcv_dev == 2 * LANES
            and self.src_part * self.own == LANES
            and LANES % self.n_dev == 0
            and self.n_pos % LANES == 0
        )


def look_up(z, table, pos_ref):
    pos = pos_ref[...]
    lane = lax.broadcasted_iota(jnp.int32, (LANES, pos.shape[1]), 0)
    spot = (lane == pos % LANES).astype(F32).astype(BF16)
    found = jnp.dot(table, spot, preferred_element_type=F32)
    total = 0.0
    for block in range(z.n_pos // LANES):
        total += jnp.where(pos // LANES == block, found[block * z.n_slow:(block + 1) * z.n_slow], 0.0)
    return total


def whole(*shape):
    return pl.BlockSpec(shape, lambda *_: (0,) * len(shape))


def pack_sources(z):
    def kernel(src_ref, *refs):
        outs, flat = refs[:z.n_rcv], refs[z.n_rcv]
        for row in range(ROWS):
            flat[row * z.src_freq:(row + 1) * z.src_freq, :z.src_dev] = src_ref[row].astype(F32)
        half = z.own // 2
        for other in range(z.n_rcv):
            rcv = lax.axis_index("rcv") ^ other
            for low in range(z.low):
                for group in range(2):
                    freq = (low * z.n_rcv + rcv) * z.own + group * half
                    tiles = [flat[pl.ds(freq + m, ROWS, stride=z.src_freq), :] for m in range(half)]
                    turned = jnp.transpose(jnp.concatenate(tiles, 0))[:z.src_dev]
                    outs[other][low, group * z.src_dev:(group + 1) * z.src_dev, :] = turned.astype(BF16)

    shape = (z.low, z.chunk, LANES)
    return pl.pallas_call(
        kernel,
        grid=(1,),
        in_specs=[whole(ROWS, z.src_freq, z.src_dev)],
        out_specs=[whole(*shape)] * z.n_rcv,
        out_shape=[jax.ShapeDtypeStruct(shape, BF16)] * z.n_rcv,
        scratch_shapes=[pltpu.VMEM(((ROWS + 1) * z.src_freq, LANES), F32)],
        compiler_params=pltpu.CompilerParams(vmem_limit_bytes=FULL_VMEM),
        cost_estimate=pl.CostEstimate(flops=10**6, bytes_accessed=2 * 10**6, transcendentals=0),
        name="pack_sources",
    )


def order_sources(z):
    def kernel(lag_ref, *refs):
        out_ref = refs[-1]
        for other, ref in zip(FAR_FIRST, refs):
            place = lax.axis_index("rcv") ^ other
            out_ref[pl.ds(place * z.low, z.low), :z.chunk, :] = ref[...]
        for place in range(z.n_src):
            out_ref[place, z.chunk:, :] = lag_ref[...]

    shape = (z.chunk + LAG_ROWS // 2, LANES)
    return pl.pallas_call(
        kernel,
        grid=(1,),
        in_specs=[whole(LAG_ROWS // 2, LANES)] + [whole(z.low, z.chunk, LANES)] * z.n_rcv,
        out_specs=whole(z.n_src, *shape),
        out_shape=jax.ShapeDtypeStruct((z.n_src, *shape), BF16),
        compiler_params=pltpu.CompilerParams(vmem_limit_bytes=VMEM),
        cost_estimate=pl.CostEstimate(flops=10**6, bytes_accessed=10**6, transcendentals=0),
        name="order_sources",
    )


def pack_receivers(z):
    def kernel(pos_ref, src_pos_ref, rcv_ref, lag_ref, *refs):
        outs, src_out, flat = refs[:z.n_rcv], refs[z.n_rcv], refs[z.n_rcv + 1:]
        blocks = [lag_ref[:, place:place + LANES] for place in range(0, z.n_pos, LANES)]
        table = (jnp.concatenate(blocks, 0) - z.n_freq).astype(F32).astype(BF16)
        src_lags = look_up(z, table, src_pos_ref)
        src_out[...] = jnp.concatenate([src_lags[:LAG_ROWS // 2], src_lags[LAG_ROWS // 2:]], 1).astype(BF16)
        spans = range(0, z.rcv_dev, LANES)
        lags = look_up(z, table, pos_ref).astype(BF16)
        for row in range(ROWS):
            here = rcv_ref[row].astype(F32)
            for n, span in enumerate(spans):
                flat[n][row * z.rcv_freq:(row + 1) * z.rcv_freq, :] = here[:, span:span + LANES]
        for other in range(z.n_rcv):
            first = (lax.axis_index("rcv") ^ other) * z.own
            for n, span in enumerate(spans):
                for k in range(z.own):
                    tile = flat[n][pl.ds(first + k, ROWS, stride=z.rcv_freq), :]
                    outs[other][k * ROWS:(k + 1) * ROWS, span:span + LANES] = tile.astype(BF16)
                outs[other][z.own * ROWS:, span:span + LANES] = lags[:, span:span + LANES]

    shape = (z.own * ROWS + LAG_ROWS, z.rcv_dev)
    return pl.pallas_call(
        kernel,
        grid=(1,),
        in_specs=[
            whole(1, z.rcv_dev),
            whole(1, z.src_dev),
            whole(ROWS, z.rcv_freq, z.rcv_dev),
            whole(z.n_slow, z.n_pos),
        ],
        out_specs=[whole(*shape)] * z.n_rcv + [whole(LAG_ROWS // 2, LANES)],
        out_shape=[jax.ShapeDtypeStruct(shape, BF16)] * z.n_rcv
        + [jax.ShapeDtypeStruct((LAG_ROWS // 2, LANES), BF16)],
        scratch_shapes=[pltpu.VMEM(((ROWS + 1) * z.rcv_freq, LANES), F32)] * (z.rcv_dev // LANES),
        compiler_params=pltpu.CompilerParams(vmem_limit_bytes=VMEM),
        cost_estimate=pl.CostEstimate(flops=10**6, bytes_accessed=2 * 10**6, transcendentals=0),
        name="pack_receivers",
    )


def cross_spectra(z, src_ref, rcv_refs, turn, right, stack):
    half = z.own // 2
    group, place = divmod(turn, half)
    begin = place * ROWS
    rows = slice(turn * ROWS, (turn + 1) * ROWS)
    spec = jnp.concatenate([ref[rows, :] for ref in rcv_refs], 1).astype(F32)
    turned = jnp.concatenate([-spec[z.n_win:], spec[:z.n_win]], 0)
    window = lax.broadcasted_iota(jnp.int32, (ROWS, 1), 0) % z.n_win
    for seg in range(SEGS):
        here = window // WIN == seg
        right[seg, begin:begin + ROWS, :] = jnp.where(here, spec, 0.0).astype(BF16)
        right[SEGS + seg, begin:begin + ROWS, :] = jnp.where(here, turned, 0.0).astype(BF16)
    width, height = 2 * LANES, TILE_ROWS
    r_now = spec.shape[1]
    for col in range(0, r_now, width):
        for row in range(0, z.s_all, height):
            senders = range(row // z.src_dev, (row + height) // z.src_dev)
            lines = slice(group * z.src_dev, (group + 1) * z.src_dev)
            part = jnp.concatenate([src_ref[sender, lines, :] for sender in senders], 0)
            total_re, total_im = 0.0, 0.0
            for seg in range(SEGS):
                real = jnp.dot(part, right[seg, :, col:col + width], preferred_element_type=F32)
                imag = jnp.dot(part, right[SEGS + seg, :, col:col + width], preferred_element_type=F32)
                scale = lax.rsqrt(jnp.maximum(real * real + imag * imag, 1.0))
                total_re, total_im = total_re + real * scale, total_im + imag * scale
            stack[row:row + height, col:col + width] = total_re.astype(BF16)
            stack[z.s_all + row:z.s_all + row + height, col:col + width] = total_im.astype(BF16)


def compute(z, count, first, last):
    src_factor = 1.0 / (SEGS * math.sqrt(z.r_all))
    rcv_factor = 1.0 / (SEGS * math.sqrt(z.s_all))
    n = z.n_slow
    r_now = count * z.rcv_dev
    place_lag = z.own * ROWS

    def kernel(src_ref, *refs):
        rcv_refs, refs = refs[:count], refs[count:]
        if not first:
            before_ref, refs = refs[0], refs[1:]
        out_refs, refs = refs[:count], refs[count:]
        sum_ref, lag, waves, right, stack = refs[:5]
        right[...] = jnp.zeros_like(right)
        for src in range(z.n_src):
            lags = src_ref[src, z.chunk:, :].astype(F32) + float(z.n_freq)
            for part in range(2):
                rows = slice(part * LAG_ROWS // 2, (part + 1) * LAG_ROWS // 2)
                lanes = slice(part * z.src_dev, (part + 1) * z.src_dev)
                lag[rows, src * z.src_dev:(src + 1) * z.src_dev] = lags[:, lanes]
        for block, ref in enumerate(rcv_refs):
            place = z.s_all + block * z.rcv_dev
            lag[:, place:place + z.rcv_dev] = ref[place_lag:, :].astype(F32) + float(z.n_freq)
        begin = lax.axis_index("src") * z.rcv_freq + lax.axis_index("rcv") * z.own
        waves[0], waves[1] = phases(lag[...], begin.astype(F32), 2.0 * z.n_freq)
        waves[2], waves[3] = phases(lag[...], 1.0, 2.0 * z.n_freq)

        def next_waves():
            cos, sin = waves[0], waves[1]
            step_cos, step_sin = waves[2], waves[3]
            waves[0], waves[1] = cos * step_cos - sin * step_sin, sin * step_cos + cos * step_sin
            return cos[:, :z.s_all], sin[:, :z.s_all], cos[:, z.s_all:], sin[:, z.s_all:]

        def cross(turn, slot):
            cross_spectra(z, src_ref, rcv_refs, turn, right.at[turn % (z.own // 2)], stack.at[slot])

        def slant(turn, slot):
            src_cos, src_sin, rcv_cos, rcv_sin = next_waves()
            upper = jnp.concatenate([src_cos, src_sin], 1)
            lower = jnp.concatenate([-src_sin, src_cos], 1)
            both = jnp.concatenate([upper, lower], 0).astype(BF16)
            over_src = jnp.dot(both, stack[slot], preferred_element_type=F32) * rcv_factor
            over_re, over_im = over_src[:n], over_src[n:]
            panel_re = over_re * rcv_cos - over_im * rcv_sin
            panel_im = over_re * rcv_sin + over_im * rcv_cos
            panel = jnp.concatenate([panel_re, panel_im], 0).astype(BF16)
            for block, ref in enumerate(out_refs):
                ref[turn] = panel[:, block * z.rcv_dev:(block + 1) * z.rcv_dev]
            dims = (((1,), (1,)), ((), ()))
            with_re = jnp.concatenate([rcv_cos, rcv_sin], 0).astype(BF16)
            with_im = jnp.concatenate([-rcv_sin, rcv_cos], 0).astype(BF16)
            over_rcv = lax.dot_general(with_re, stack[slot, :z.s_all, :], dims, preferred_element_type=F32)
            over_rcv += lax.dot_general(with_im, stack[slot, z.s_all:, :], dims, preferred_element_type=F32)
            if not first:
                over_rcv += before_ref[turn]
            if not last:
                sum_ref[turn] = over_rcv
                return
            over_rcv *= src_factor
            over_re, over_im = over_rcv[:n], over_rcv[n:]
            panel_re = over_re * src_cos + over_im * src_sin
            panel_im = over_im * src_cos - over_re * src_sin
            refs[5][turn] = jnp.concatenate([panel_re, panel_im], 0)
            regroup_after(z, refs[5], turn)

        cross(0, 0)
        for turn in range(1, z.own):
            cross(turn, turn % 2)
            slant(turn - 1, (turn - 1) % 2)
        slant(z.own - 1, (z.own - 1) % 2)
        if last:
            send_sources(z, refs[5], sum_ref)

    in_specs = [whole(z.n_src, z.chunk + LAG_ROWS // 2, LANES)]
    in_specs += [whole(z.own * ROWS + LAG_ROWS, z.rcv_dev)] * count
    out_specs = [whole(z.own, ROWS, z.rcv_dev)] * count
    out_shape = [jax.ShapeDtypeStruct((z.own, ROWS, z.rcv_dev), BF16)] * count
    part_spec = whole(z.own, ROWS, z.s_all)
    scratch = [
        pltpu.VMEM((n, z.s_all + r_now), F32),
        pltpu.VMEM((4, n, z.s_all + r_now), F32),
        pltpu.VMEM((z.own // 2, 2 * SEGS, LANES, r_now), BF16),
        pltpu.VMEM((2, 2 * z.s_all, r_now), BF16),
    ]
    if not first:
        in_specs.append(part_spec)
    if last:
        out_specs.append(whole(z.n_dev, ROWS, LANES))
        out_shape.append(jax.ShapeDtypeStruct((z.n_dev, ROWS, LANES), BF16))
        scratch.append(pltpu.VMEM((z.own, ROWS, z.s_all), F32))
    else:
        out_specs.append(part_spec)
        out_shape.append(jax.ShapeDtypeStruct((z.own, ROWS, z.s_all), F32))
    return pl.pallas_call(
        kernel,
        grid=(1,),
        in_specs=in_specs,
        out_specs=out_specs,
        out_shape=out_shape,
        scratch_shapes=scratch,
        compiler_params=pltpu.CompilerParams(vmem_limit_bytes=VMEM),
        cost_estimate=pl.CostEstimate(flops=COST * count, bytes_accessed=10**6, transcendentals=0),
        name="compute_first" if first else "compute_last" if last else "compute_next",
    )


def regroup(z, sums, bit, first):
    lane = lanes_of(ROWS)
    shift = bit * z.src_part
    upper = lane & shift != 0
    for block in range(z.s_all // LANES):
        lanes = slice(block * LANES, (block + 1) * LANES)
        one, two = sums[first, :, lanes], sums[first + bit, :, lanes]
        sums[first, :, lanes] = jnp.where(upper, pltpu.roll(two, shift, 1), one)
        sums[first + bit, :, lanes] = jnp.where(upper, two, pltpu.roll(one, LANES - shift, 1))


def regroup_after(z, sums, turn):
    bit = 1
    while bit < z.own and turn & bit:
        base = turn & ~(2 * bit - 1)
        for low in range(bit):
            regroup(z, sums, bit, base + low)
        bit *= 2


def send_sources(z, sums, out_ref):
    for block in range(z.s_all // LANES):
        for group in range(z.own):
            out_ref[block * z.own + group] = sums[group, :, block * LANES:(block + 1) * LANES].astype(BF16)


def unpack_block(z, in_ref, flat, write):
    n = z.n_slow
    for span in range(0, z.rcv_dev, LANES):
        for k in range(z.own):
            flat[k * ROWS:(k + 1) * ROWS, :] = in_ref[k, :, span:span + LANES].astype(F32)
        for slow in range(n):
            for part in range(2):
                write(2 * slow + part, span, flat[pl.ds(part * n + slow, z.own, stride=ROWS), :])


def unpack_first(z, others):
    def kernel(*refs):
        in_refs, out_ref, flat = refs[:len(others)], refs[-2], refs[-1]
        for other, in_ref in zip(others, in_refs):
            rows = pl.ds(pl.multiple_of((lax.axis_index("rcv") ^ other) * z.own, z.own), z.own)

            def write(index, span, tile):
                out_ref[index, rows, span:span + LANES] = tile

            unpack_block(z, in_ref, flat, write)

    return pl.pallas_call(
        kernel,
        grid=(1,),
        in_specs=[whole(z.own, ROWS, z.rcv_dev)] * len(others),
        out_specs=whole(ROWS, z.rcv_freq, z.rcv_dev),
        out_shape=jax.ShapeDtypeStruct((ROWS, z.rcv_freq, z.rcv_dev), F32),
        scratch_shapes=[pltpu.VMEM(((z.own + 1) * ROWS, LANES), F32)],
        compiler_params=pltpu.CompilerParams(vmem_limit_bytes=VMEM),
        cost_estimate=pl.CostEstimate(flops=10**6, bytes_accessed=10**6, transcendentals=0),
        name="unpack_first",
    )


def unpack_last(z, other):
    n = z.n_slow
    group = LANES // z.n_dev
    width = z.src_part

    def kernel(rcv_in, src_in, held_ref, rcv_ref, src_ref, flat, small, table):
        del held_ref

        def write(index, span, tile):
            rcv_ref[index, :, span:span + LANES] = tile

        unpack_block(z, rcv_in, small, write)
        for dev in range(z.n_dev):
            flat[dev * ROWS:(dev + 1) * ROWS, :] = src_in[dev].astype(F32)
        lane = lanes_of(width)
        for first in range(0, ROWS, group):
            tiles = [flat[pl.ds(first + j, z.n_dev, stride=ROWS), :] for j in range(group)]
            turned = jnp.transpose(jnp.concatenate(tiles, 0))
            for j in range(group):
                for block in range(z.own // group):
                    total = jnp.zeros((width, LANES), F32)
                    for k in range(group):
                        row = (block * group + k) * width
                        tile = turned[row:row + width, :]
                        shift = (k - j) * z.n_dev % LANES
                        moved = pltpu.roll(tile, shift, 1) if shift else tile
                        total = jnp.where((lane >= k * z.n_dev) & (lane < (k + 1) * z.n_dev), moved, total)
                    rows = slice((first + j) * width, (first + j + 1) * width)
                    table[rows, block * LANES:(block + 1) * LANES] = total.astype(BF16)
        here = lax.broadcasted_iota(jnp.int32, (z.n_freq, z.n_freq), 0)
        there = lax.broadcasted_iota(jnp.int32, (z.n_freq, z.n_freq), 1)
        order = (there == here % z.n_dev * z.own + here // z.n_dev).astype(F32).astype(BF16)
        ordered = jnp.dot(table[...], order, preferred_element_type=F32)
        for index in range(ROWS):
            part, slow = divmod(index, n)
            src_ref[2 * slow + part] = ordered[index * width:(index + 1) * width, :]

    return pl.pallas_call(
        kernel,
        grid=(1,),
        in_specs=[
            whole(z.own, ROWS, z.rcv_dev),
            whole(z.n_dev, ROWS, LANES),
            pl.BlockSpec(memory_space=pl.ANY),
        ],
        out_specs=[
            pl.BlockSpec((ROWS, z.own, z.rcv_dev), lambda k: (0, lax.axis_index("rcv") ^ other, 0)),
            whole(ROWS, width, z.n_freq),
        ],
        scratch_shapes=[
            pltpu.VMEM(((z.n_dev + 1) * ROWS, LANES), F32),
            pltpu.VMEM(((z.own + 1) * ROWS, LANES), F32),
            pltpu.VMEM((ROWS * width, z.n_freq), BF16),
        ],
        out_shape=[
            jax.ShapeDtypeStruct((ROWS, z.rcv_freq, z.rcv_dev), F32),
            jax.ShapeDtypeStruct((ROWS, width, z.n_freq), F32),
        ],
        input_output_aliases={2: 0},
        compiler_params=pltpu.CompilerParams(vmem_limit_bytes=VMEM),
        cost_estimate=pl.CostEstimate(flops=10**6, bytes_accessed=2 * 10**6, transcendentals=0),
        name="unpack_last",
    )


def swap(z, block, other):
    if other == 0:
        return block
    return lax.ppermute(block, "rcv", [(j, j ^ other) for j in range(z.n_rcv)])


def arrive(done, others, values):
    here, values = lax.optimization_barrier(([done[other] for other in others], values))
    done.update(zip(others, here))
    return values


def per_device(src_spec, rcv_spec, lag_table, src_pos, rcv_pos):
    n_src, n_rcv = lax.axis_size("src"), lax.axis_size("rcv")
    z = Sizes((src_spec.shape, rcv_spec.shape, lag_table.shape), n_src, n_rcv)
    if not z.fits():
        return per_device_general(src_spec, rcv_spec, lag_table, src_pos, rcv_pos)
    src_rows = src_spec.reshape(ROWS, z.src_freq, z.src_dev)
    rcv_rows = rcv_spec.reshape(ROWS, z.rcv_freq, z.rcv_dev)
    parts = pack_sources(z)(src_rows)
    moved = {other: swap(z, parts[other], other) for other in FAR_FIRST}
    *packed, src_lags = pack_receivers(z)(rcv_pos[None], src_pos[None], rcv_rows, lag_table)
    spread = order_sources(z)(src_lags, *(moved[other] for other in FAR_FIRST))
    sources = lax.all_to_all(spread, "src", 0, 0, tiled=True)
    blocks = {other: swap(z, packed[other], other) for others in CALLS for other in others}
    done, carry = {}, ()
    for n, others in enumerate(CALLS):
        ready = [blocks[other] for other in others]
        if n >= 2:
            ready, carry = arrive(done, CALLS[n - 2], (ready, carry))
        call = compute(z, len(others), n == 0, n == len(CALLS) - 1)
        *panels, total = call(sources, *ready, *carry)
        done.update({other: swap(z, panel, other) for other, panel in zip(others, panels)})
        carry = (total,)
    total = arrive(done, CALLS[-2], total)
    got_src = lax.all_to_all(total, ("src", "rcv"), 0, 0, tiled=True)
    late = CALLS[-1][0]
    early = tuple(other for other in done if other != late)
    held = unpack_first(z, early)(*(done[other] for other in early))
    panel_rcv, panel_src = unpack_last(z, late)(done[late], got_src, held)
    return (
        panel_src.reshape(z.n_slow, 2, z.src_part, z.n_freq),
        panel_rcv.reshape(z.n_slow, 2, z.rcv_freq, z.rcv_dev),
    )


def solution(mesh):
    placed = (P(None, None, "rcv", "src"), P(None, None, "src", "rcv"), P(), P("src"), P("rcv"))
    return jax.shard_map(
        per_device,
        mesh=mesh,
        in_specs=placed,
        out_specs=(P(None, None, ("src", "rcv"), None), P(None, None, "src", "rcv")),
        check_vma=False,
    )
```
